32 devices in a mesh: dp: 16 (over z, y, core), mp: 2 (over x).
Axes of the slice: x: 2, y: 2, z: 4, core: 2. Of those that a mesh axis runs over, the one named last changes fastest.
Arguments:
- inputs: bfloat16 [64, 512, 768], P('dp', 'mp'), may hold values from -6 to 6
- segment_ids: int32 [64, 512], P('dp'), may hold values from 0 to 15, as said below
- ln1_gain: bfloat16 [768], replicated, may hold values from 0.099609375 to 1.8984375
- ln1_bias: bfloat16 [768], replicated, may hold values from -0.3984375 to 0.3984375
- value_weight: bfloat16 [768, 768], replicated, may hold values from -0.21875 to 0.21875
- value_bias: bfloat16 [768], replicated, may hold values from -0.5 to 0.5
- random_logits: bfloat16 [12, 512, 512], P(None, 'mp'), may hold values from -8 to 8
- out_weight: bfloat16 [768, 768], replicated, may hold values from -0.875 to 0.875
- out_bias: bfloat16 [768], replicated, may hold values from -0.5 to 0.5
- ln2_gain: bfloat16 [768], replicated, may hold values from 0.099609375 to 1.8984375
- ln2_bias: bfloat16 [768], replicated, may hold values from -0.3984375 to 0.3984375
- up_weight: bfloat16 [768, 3072], P(None, 'mp'), may hold values from -0.21875 to 0.21875
- up_bias: bfloat16 [3072], P('mp'), may hold values from -0.5 to 0.5
- down_weight: bfloat16 [3072, 768], P('mp'), may hold values from -0.109375 to 0.109375
- down_bias: bfloat16 [768], replicated, may hold values from -0.5 to 0.5
- out_cotangent: bfloat16 [64, 512, 768], P('dp', 'mp'), may hold values from -6 to 6
Outputs:
- layer_out: bfloat16 [64, 512, 768], P('dp', 'mp')
- grad_inputs: float32 [64, 512, 768], P('dp', 'mp')
- grad_ln1_gain: float32 [768], P(('dp', 'mp'))
- grad_ln1_bias: float32 [768], P(('dp', 'mp'))
- grad_value_weight: float32 [768, 768], P(('dp', 'mp'))
- grad_value_bias: float32 [768], P(('dp', 'mp'))
- grad_random_logits: float32 [12, 512, 512], P(None, 'mp', 'dp')
- grad_out_weight: float32 [768, 768], P(('dp', 'mp'))
- grad_out_bias: float32 [768], P(('dp', 'mp'))
- grad_ln2_gain: float32 [768], P(('dp', 'mp'))
- grad_ln2_bias: float32 [768], P(('dp', 'mp'))
- grad_up_weight: float32 [768, 3072], P('dp', 'mp')
- grad_up_bias: float32 [2, 1536], P('mp', 'dp')
- grad_down_weight: float32 [3072, 768], P('mp', 'dp')
- grad_down_bias: float32 [768], P(('dp', 'mp'))
The draws below stay inside these ranges and needn't reach their ends.
Inputs may be any that keep to these rules, and one draw needn't show every extreme that they name: `segment_ids`: in each row the ids start at 0 and never fall; of the 4 rows of each index of dp, one row is a single document, and another reaches the largest id.
All inputs are finite; a program needn't handle non-finite values.
Results may differ from the reference program's by a relative error of at most 0.015.
Values may be sent and summed in bfloat16 or wider, within the bound.
No kernel may reach another device: no remote copies, remote signals or barrier semaphores. Data moves between devices by JAX's collectives and lax.ppermute only.
A program may use at most 192 MiB of HBM per device.

```python
import math
import jax
import jax.numpy as jnp
from jax import lax

D = 768
H = 12
FF = 3072
L = 512
ROWS = 4
SEQS = 64
N_MP = 2


def draw_segment_ids(key, part):
    key = jax.random.fold_in(key, 7)
    first, second = jax.random.split(key)
    starts = jax.random.randint(first, (SEQS, L), 0, 96) == 0
    position = jnp.arange(L)[None, :]
    starts = starts & (position > 0)
    chosen = jax.random.randint(second, (SEQS // ROWS,), 0, ROWS)
    row_number = jnp.arange(SEQS)
    single = row_number % ROWS == chosen[row_number // ROWS]
    fuller = row_number % ROWS == (chosen[row_number // ROWS] + 1) % ROWS
    regular = (position % 32 == 0) & (position > 0)
    starts = starts | fuller[:, None] & regular
    starts = starts & jnp.logical_not(single)[:, None]
    ids = jnp.cumsum(starts.astype(jnp.int32), axis=1)
    return jnp.minimum(ids, L // 32 - 1).astype(jnp.int32)


def steps_of(key, shape, cuts, smallest, high):
    factor_of, own = 1.0, jax.random.fold_in(key, 6)
    for dim, shards_of in cuts:
        steps = jnp.exp(jax.random.uniform(jax.random.fold_in(own, dim), (shards_of,), jnp.float32, smallest / len(cuts), high / len(cuts)))
        factor_of = factor_of * jnp.repeat(steps, shape[dim] // shards_of).reshape([-1 if axis == dim else 1 for axis in range(len(shape))])
    return factor_of


def normal_values(rng, dims, deviation, reach, shards=(), held_as=jnp.bfloat16):
    entries = jax.random.normal(rng, dims, jnp.float32) * deviation
    if len(shards) > 0:
        entries = steps_of(rng, dims, shards, -0.22, 0.18) * entries
    return jnp.clip(entries, min=-reach, max=reach).astype(held_as)


def setup_inputs(seed: int = 0) -> dict:
    arg_keys = jax.random.split(jax.random.key(seed), 17)
    inputs = normal_values(arg_keys[0], (SEQS, L, D), 1.0, 6.0, ((0, 16), (1, 2)))
    segment_ids = draw_segment_ids(jax.random.fold_in(arg_keys[16], 71), 0)
    ln1_gain = jnp.clip(1.0 + 0.18 * jax.random.normal(arg_keys[2], (D,), jnp.float32), 0.099609375, 1.8984375).astype(jnp.bfloat16)
    ln1_bias = jnp.clip(jax.random.uniform(arg_keys[3], (D,), jnp.float32, -0.3984375, 0.3984375), -0.3984375, 0.3984375).astype(jnp.bfloat16)
    value_weight = normal_values(arg_keys[4], (D, D), D ** -0.5, 0.21875)
    value_bias = jnp.clip(jax.random.uniform(arg_keys[5], (D,), jnp.float32, -0.5, 0.5), -0.5, 0.5).astype(jnp.bfloat16)
    random_logits = normal_values(arg_keys[6], (H, L, L), 2.0, 8.0, ((1, 2),))
    out_weight = normal_values(arg_keys[7], (D, D), (D // 16) ** -0.5, 0.875)
    out_bias = jnp.clip(jax.random.uniform(arg_keys[8], (D,), jnp.float32, -0.5, 0.5), -0.5, 0.5).astype(jnp.bfloat16)
    ln2_gain = jnp.clip(1.0 + 0.18 * jax.random.normal(arg_keys[9], (D,), jnp.float32), 0.099609375, 1.8984375).astype(jnp.bfloat16)
    ln2_bias = jnp.clip(jax.random.uniform(arg_keys[10], (D,), jnp.float32, -0.3984375, 0.3984375), -0.3984375, 0.3984375).astype(jnp.bfloat16)
    up_weight = normal_values(arg_keys[11], (D, FF), D ** -0.5, 0.21875, ((1, 2),))
    up_bias = jnp.clip(jax.random.uniform(arg_keys[12], (FF,), jnp.float32, -0.5, 0.5) * steps_of(arg_keys[12], (FF,), ((0, 2),), -0.4, 0.0), -0.5, 0.5).astype(jnp.bfloat16)
    down_weight = normal_values(arg_keys[13], (FF, D), FF ** -0.5, 0.109375, ((0, 2),))
    down_bias = jnp.clip(jax.random.uniform(arg_keys[14], (D,), jnp.float32, -0.5, 0.5), -0.5, 0.5).astype(jnp.bfloat16)
    out_cotangent = normal_values(arg_keys[15], (SEQS, L, D), 1.0, 6.0, ((0, 16), (1, 2)))
    return dict(inputs=inputs, segment_ids=segment_ids, ln1_gain=ln1_gain, ln1_bias=ln1_bias, value_weight=value_weight, value_bias=value_bias, random_logits=random_logits, out_weight=out_weight, out_bias=out_bias, ln2_gain=ln2_gain, ln2_bias=ln2_bias, up_weight=up_weight, up_bias=up_bias, down_weight=down_weight, down_bias=down_bias, out_cotangent=out_cotangent)


@jax.custom_vjp
def low(v):
    return lax.optimization_barrier(v.astype(jnp.bfloat16)).astype(jnp.float32)

@jax.custom_vjp
def low_back(v):
    return v

def low_keep(v):
    return (low(v), None)

def low_pass(kept, grad):
    return (grad,)

def back_keep(v):
    return (v, None)

def back_low(kept, grad):
    return (low(grad),)
low.defvjp(low_keep, low_pass)
low_back.defvjp(back_keep, back_low)

def norm_layer(x, gain, shift):
    centred = x - lax.optimization_barrier(jnp.mean(x, -1, keepdims=True))
    scale = lax.rsqrt(lax.optimization_barrier(jnp.mean(centred * centred, -1, keepdims=True)) + 1e-05)
    return centred * scale * gain + shift

def smooth(t):
    return jax.nn.gelu(t, approximate=True)

def project(a, w):
    return jnp.einsum('gti,ij->gtj', a, w, precision=lax.Precision.HIGHEST)

def layer(params, x, segs):
    g1, s1, wv, bv, logits, wo, bo, g2, s2, wu, bu, wd, bd = params
    group = x.shape[0]
    heads = logits.shape[0]
    h1 = low(norm_layer(x, g1, s1))
    values = low(low_back(project(h1, wv) + bv))
    split = values.reshape(group, L, heads, D // heads)
    same = segs[:, :, None] == segs[:, None, :]
    scores = jnp.where(same[:, None], logits[None], -1e+30)
    peak = lax.optimization_barrier(jnp.max(scores, -1, keepdims=True))
    expo = jnp.exp(scores - peak)
    probs = low(expo / lax.optimization_barrier(jnp.sum(expo, -1, keepdims=True)))
    mixed = jnp.einsum('ghqk,gkhd->gqhd', probs, split, precision=lax.Precision.HIGHEST).reshape(group, L, D)
    mixed = low(low_back(mixed))
    resid = x + low_back(project(mixed, wo) + bo)
    h2 = low(norm_layer(resid, g2, s2))
    act = low(smooth(low_back(project(h2, wu) + bu)))
    return resid + project(act, wd) + bd

def reference(inputs, segment_ids, ln1_gain, ln1_bias, value_weight, value_bias, random_logits, out_weight, out_bias, ln2_gain, ln2_bias, up_weight, up_bias, down_weight, down_bias, out_cotangent):
    params = tuple((a.astype(jnp.float32) for a in (ln1_gain, ln1_bias, value_weight, value_bias, random_logits, out_weight, out_bias, ln2_gain, ln2_bias, up_weight, up_bias, down_weight, down_bias)))
    group = math.gcd(SEQS, 8)
    count = SEQS // group
    xs = inputs.astype(jnp.float32).reshape(count, group, L, D)
    segs = segment_ids.reshape(count, group, L)
    cotan = out_cotangent.astype(jnp.float32).reshape(count, group, L, D)

    def run(weights, x):
        step = jax.checkpoint(lambda pair: layer(weights, pair[0], pair[1]))
        return lax.map(step, (x, segs))
    out, pull = jax.vjp(run, params, xs)
    grads, grad_x = pull(cotan)
    g1, s1, wv, bv, logits, wo, bo, g2, s2, wu, bu, wd, bd = grads
    return (out.reshape(SEQS, L, D).astype(jnp.bfloat16), grad_x.reshape(SEQS, L, D), g1, s1, wv, bv, logits, wo, bo, g2, s2, wu, bu.reshape(N_MP, FF // N_MP), wd, bd)
```

```python
import functools

import jax
import jax.numpy as jnp
from jax import lax
from jax.experimental import pallas as pl
from jax.experimental.pallas import tpu as pltpu
from jax.sharding import PartitionSpec as P

F32 = jnp.float32
BF16 = jnp.bfloat16
GELU_A = 0.7978845608028654
GELU_B = GELU_A * 0.044715
MIB = 2**20


def mm(left, right, left_dim, right_dim):
    return lax.dot_general(
        left, right, (((left_dim,), (right_dim,)), ((), ())), preferred_element_type=F32
    )


def unit_rows(x):
    centred = x - jnp.mean(x, -1, keepdims=True)
    scale = lax.rsqrt(jnp.mean(centred * centred, -1, keepdims=True) + 1e-05)
    return centred * scale, scale


def norm_back(grad, unit, scale, gain):
    e = grad * gain
    return scale * (
        e - jnp.mean(e, -1, keepdims=True) - unit * jnp.mean(e * unit, -1, keepdims=True)
    )


def same_segment(offs, seg_col, seg_row, length):
    own = seg_col[0, pl.ds(pl.multiple_of(offs[0], length), length), :]
    return own == seg_row[0]


def whole(shape):
    return pl.BlockSpec(shape, lambda i, *_: (0,) * len(shape))


def by_row(first, shape):
    return pl.BlockSpec((1,) + shape, lambda i, *_: (first + i,) + (0,) * len(shape))


def mix_kernel(chained, offs, x_own, x_other, seg_col, seg_row, expo, wv, bv, wo, bo, g1, b1, g2, b2, *rest):
    h1, values, recip, mixed, resid, h2, h2t, ones = rest[7 if chained else 0 :]
    length = x_own.shape[1]
    heads = expo.shape[0]
    ones[:, 128:] = jnp.ones_like(ones[:, 128:])
    x = x_own[0].astype(F32)
    for block, off in ((x, offs[0]), (x_other[0].astype(F32), offs[1])):
        unit, _ = unit_rows(block)
        at = pl.ds(pl.multiple_of(off, length), length)
        h1[0, at, :] = (unit * g1[...] + b1[...]).astype(BF16)
    values[0] = (mm(h1[0], wv[...], 1, 0) + bv[...]).astype(BF16)
    mask = jnp.where(same_segment(offs, seg_col, seg_row, length), 1.0, 0.0).astype(BF16)
    low_lane = lax.broadcasted_iota(jnp.int32, (length, 128), 1) < 64
    for pair in range(heads // 2):
        lanes = slice(128 * pair, 128 * pair + 128)
        ones[:, :128] = values[0, :, lanes]
        first = mm(expo[2 * pair] * mask, ones[...], 1, 0)
        second = mm(expo[2 * pair + 1] * mask, ones[...], 1, 0)
        inverse = 1.0 / jnp.where(low_lane, first[:, 128:], second[:, 128:])
        recip[0, :, lanes] = inverse
        mixed[0, :, lanes] = jnp.where(low_lane, first[:, :128], second[:, :128]) * inverse
    r = x + mm(mixed[0].astype(BF16), wo[...], 1, 0) + bo[...]
    resid[0] = r
    unit, _ = unit_rows(r)
    low = (unit * g2[...] + b2[...]).astype(BF16)
    h2[0] = low
    h2t[...] = low.T


def mix_rows(first, count, offs, inputs, received, seg_col, seg_row, expo, weights, chain):
    rows, length, width = inputs.shape
    full = seg_row.shape[2]
    heads = expo.shape[0]
    shapes = [
        ((full, width), BF16),
        ((full, width), BF16),
        ((length, width), F32),
        ((length, width), F32),
        ((length, width), F32),
        ((length, width), BF16),
    ]
    out_specs = [by_row(first, s) for s, _ in shapes]
    out_specs.append(pl.BlockSpec((width, length), lambda i, *_: (0, first + i)))
    out_shape = [jax.ShapeDtypeStruct((rows,) + s, t) for s, t in shapes]
    out_shape.append(jax.ShapeDtypeStruct((width, rows * length), BF16))
    operands = [offs, inputs, received, seg_col, seg_row, expo, *weights]
    in_specs = [
        by_row(first, (length, width)),
        by_row(0, (length, width)),
        by_row(first, (full, 1)),
        by_row(first, (1, full)),
        whole(expo.shape),
        *[whole(w.shape) for w in weights],
    ]
    aliases = {}
    if chain is not None:
        aliases = {len(operands) + i: i for i in range(len(out_shape))}
        operands += list(chain)
        in_specs += [pl.BlockSpec(memory_space=pl.ANY)] * len(out_shape)
    flops = 2 * count * (2 * full * width * width // 2 * 2 + length * width * width + heads * length * full * 256)
    return pl.pallas_call(
        functools.partial(mix_kernel, chain is not None),
        grid_spec=pltpu.PrefetchScalarGridSpec(
            num_scalar_prefetch=1,
            grid=(count,),
            in_specs=in_specs,
            out_specs=out_specs,
            scratch_shapes=[pltpu.VMEM((full, 256), BF16)],
        ),
        out_shape=out_shape,
        input_output_aliases=aliases,
        compiler_params=pltpu.CompilerParams(vmem_limit_bytes=40 * MIB),
        cost_estimate=pl.CostEstimate(flops=flops, bytes_accessed=10 * MIB, transcendentals=0),
        name="mix_rows",
    )(*operands)


def gelu_pair(t):
    square = t * t
    curve = jnp.tanh(t * (GELU_A + GELU_B * square))
    half = 0.5 + 0.5 * curve
    act = t * half
    return act, half + act * (1.0 - curve) * (GELU_A + 3 * GELU_B * square)


def hidden_tile(h2, g, h2t, gt, wu, bu, wd, out, dh, grads, bias, act_s, pre_s, block):
    total = jnp.zeros(bias.shape, F32)
    for m in range(h2.shape[0] // block):
        at = pl.ds(m * block, block)
        pre = mm(h2[at, :], wu, 1, 0) + bu
        grad_act = mm(g[at, :], wd, 1, 1)
        act, slope = gelu_pair(pre)
        act_low = act.astype(BF16)
        grad_pre = grad_act * slope
        total += jnp.sum(grad_pre, 0, keepdims=True)
        pre_low = grad_pre.astype(BF16)
        act_s[at, :] = act_low
        pre_s[at, :] = pre_low
        out[at, :] += mm(act_low, wd, 1, 0)
        dh[at, :] += mm(pre_low, wu, 1, 1)
    bias[...] = total
    grads[0] = mm(h2t[...], pre_s[...], 1, 0).astype(BF16)
    grads[1] = mm(gt[...], act_s[...], 1, 0).astype(BF16)


def own_hidden_kernel(block, core, h2, g, h2t, gt, wu, bu, wd, out, dh, theirs, mine, b_theirs, b_mine, act_s, pre_s):
    step = pl.program_id(0)

    @pl.when(step == 0)
    def _():
        out[...] = jnp.zeros_like(out)
        dh[...] = jnp.zeros_like(dh)

    for at, grads, bias in ((0, theirs, b_theirs), (1, mine, b_mine)):

        @pl.when(step == at)
        def _(grads=grads, bias=bias):
            hidden_tile(h2, g, h2t, gt, wu[...], bu[...], wd[...], out, dh, grads, bias, act_s, pre_s, block)


def packed_tile(w, width):
    return w[:width, :], w[2 * width :, :][:1].astype(F32), w[width : 2 * width, :]


def other_hidden_kernel(block, h2, g, h2t, gt, w_mine, w_theirs, out0, dh0, out, dh, mine, theirs, b_mine, b_theirs, act_s, pre_s):
    step = pl.program_id(0)
    width = h2.shape[1]

    @pl.when(step == 0)
    def _():
        out[...] = out0[...]
        dh[...] = dh0[...]

    for at, w, grads, bias in ((0, w_mine, mine, b_mine), (1, w_theirs, theirs, b_theirs)):

        @pl.when(step == at)
        def _(w=w, grads=grads, bias=bias):
            hidden_tile(h2, g, h2t, gt, *packed_tile(w, width), out, dh, grads, bias, act_s, pre_s, block)


def hidden_params(positions, width, tile, steps):
    return dict(
        scratch_shapes=[pltpu.VMEM((positions, tile), BF16), pltpu.VMEM((positions, tile), BF16)],
    ), dict(
        compiler_params=pltpu.CompilerParams(vmem_limit_bytes=56 * MIB),
        cost_estimate=pl.CostEstimate(
            flops=12 * positions * width * tile * steps,
            bytes_accessed=24 * MIB,
            transcendentals=positions * tile * steps,
        ),
    )


def own_hidden(core, h2, g, h2t, gt, wu, bu, wd):
    positions, width = h2.shape
    tile = wu.shape[1] // 2
    scratch, call = hidden_params(positions, width, tile, 2)
    pick = lambda i, core: lax.rem(i + 1 + core[0], 2)
    return pl.pallas_call(
        functools.partial(own_hidden_kernel, 256),
        grid_spec=pltpu.PrefetchScalarGridSpec(
            num_scalar_prefetch=1,
            grid=(2,),
            in_specs=[
                whole(h2.shape),
                whole(g.shape),
                whole(h2t.shape),
                whole(gt.shape),
                pl.BlockSpec((width, tile), lambda i, core: (0, pick(i, core))),
                pl.BlockSpec((1, tile), lambda i, core: (0, pick(i, core))),
                pl.BlockSpec((tile, width), lambda i, core: (pick(i, core), 0)),
            ],
            out_specs=[whole((positions, width))] * 2 + [whole((2, width, tile))] * 2 + [whole((1, tile))] * 2,
            **scratch,
        ),
        out_shape=[jax.ShapeDtypeStruct((positions, width), F32)] * 2
        + [jax.ShapeDtypeStruct((2, width, tile), BF16)] * 2
        + [jax.ShapeDtypeStruct((1, tile), F32)] * 2,
        name="own_hidden",
        **call,
    )(core, h2, g, h2t, gt, wu, bu, wd)


def other_hidden(h2, g, h2t, gt, w_mine, w_theirs, out0, dh0):
    positions, width = h2.shape
    tile = w_mine.shape[1]
    scratch, call = hidden_params(positions, width, tile, 2)
    operands = (h2, g, h2t, gt, w_mine, w_theirs, out0, dh0)
    return pl.pallas_call(
        functools.partial(other_hidden_kernel, 256),
        grid=(2,),
        in_specs=[whole(a.shape) for a in operands],
        out_specs=[whole((positions, width))] * 2 + [whole((2, width, tile))] * 2 + [whole((1, tile))] * 2,
        out_shape=[jax.ShapeDtypeStruct((positions, width), F32)] * 2
        + [jax.ShapeDtypeStruct((2, width, tile), BF16)] * 2
        + [jax.ShapeDtypeStruct((1, tile), F32)] * 2,
        name="other_hidden",
        **scratch,
        **call,
    )(*operands)


def back_kernel(chained, offs, out_acc, dh, resid, g, mixed, recip, x_own, x_other, seg_col, seg_row, expo, wo, wv, g2, bd, *rest):
    layer_out, grad_resid, gm, gv, gh_own, gh_send, vec_two, vec_one, gmt, gvt, gh = rest[8 if chained else 0 :]
    length = x_own.shape[1]
    heads = expo.shape[0]
    r = resid[0]
    layer_out[0] = (r + out_acc[0] + bd[...]).astype(BF16)
    unit, scale = unit_rows(r)
    grad = dh[0]
    cot = g[0].astype(F32)
    total = cot + norm_back(grad, unit, scale, g2[...])
    grad_resid[0] = total
    grad_o = total.astype(BF16)
    vec_two[0, 0:1, :] = jnp.sum(grad_o.astype(F32), 0, keepdims=True)
    vec_two[0, 1:2, :] = jnp.sum(grad * unit, 0, keepdims=True)
    vec_two[0, 2:3, :] = jnp.sum(grad, 0, keepdims=True)
    vec_two[0, 3:4, :] = jnp.sum(cot, 0, keepdims=True)
    scaled = (mm(grad_o, wo[...], 1, 1).astype(BF16).astype(F32) * recip[0]).astype(BF16)
    gm[0] = scaled
    gmt[...] = scaled.T
    mask = jnp.where(same_segment(offs, seg_col, seg_row, length), 1.0, 0.0).astype(BF16)
    for head in range(heads):
        at = slice(64 * head, 64 * head + 64)
        gvt[at, :] = mm(gmt[at, :], expo[head] * mask, 1, 0).astype(BF16)
    values_grad = gvt[...].T
    gv[0] = values_grad
    gh[...] = mm(values_grad, wv[...], 1, 1)
    gain = jnp.zeros((1, gh.shape[1]), F32)
    for block, off in ((x_own, offs[0]), (x_other, offs[1])):
        unit, _ = unit_rows(block[0].astype(F32))
        gain += jnp.sum(gh[pl.ds(pl.multiple_of(off, length), length), :] * unit, 0, keepdims=True)
    vec_one[0, 0:1, :] = gain
    vec_one[0, 1:2, :] = jnp.sum(gh[...], 0, keepdims=True)
    vec_one[0, 2:3, :] = jnp.sum(values_grad.astype(F32), 0, keepdims=True)
    gh_own[0] = gh[pl.ds(pl.multiple_of(offs[0], length), length), :]
    gh_send[0] = gh[pl.ds(pl.multiple_of(offs[1], length), length), :].astype(BF16)


def back_rows(first, count, offs, row_arrays, received, seg_col, seg_row, expo, weights, chain):
    rows, length, width = row_arrays[0].shape
    full = seg_row.shape[2]
    shapes = [
        ((length, width), BF16),
        ((length, width), F32),
        ((length, width), BF16),
        ((full, width), BF16),
        ((length, width), F32),
        ((4, width), F32),
        ((3, width), F32),
    ]
    out_specs = [by_row(first, s) for s, _ in shapes]
    out_shape = [jax.ShapeDtypeStruct((rows,) + s, t) for s, t in shapes]
    out_specs.insert(5, by_row(0, (length, width)))
    out_shape.insert(5, jax.ShapeDtypeStruct((count, length, width), BF16))
    operands = [offs, *row_arrays, received, seg_col, seg_row, expo, *weights]
    in_specs = [by_row(first, (length, width)) for _ in row_arrays]
    in_specs += [
        by_row(0, (length, width)),
        by_row(first, (full, 1)),
        by_row(first, (1, full)),
        whole(expo.shape),
        *[whole(w.shape) for w in weights],
    ]
    aliases = {}
    if chain is not None:
        keep = [i for i in range(len(out_shape))]
        aliases = {len(operands) + i: i for i in keep if i != 5}
        operands += list(chain)
        in_specs += [pl.BlockSpec(memory_space=pl.ANY)] * len(out_shape)
    return pl.pallas_call(
        functools.partial(back_kernel, chain is not None),
        grid_spec=pltpu.PrefetchScalarGridSpec(
            num_scalar_prefetch=1,
            grid=(count,),
            in_specs=in_specs,
            out_specs=out_specs,
            scratch_shapes=[
                pltpu.VMEM((width, length), BF16),
                pltpu.VMEM((width, full), BF16),
                pltpu.VMEM((full, width), F32),
            ],
        ),
        out_shape=out_shape,
        input_output_aliases=aliases,
        compiler_params=pltpu.CompilerParams(vmem_limit_bytes=48 * MIB),
        cost_estimate=pl.CostEstimate(flops=4 * 10**9 * count, bytes_accessed=14 * MIB, transcendentals=0),
        name="back_rows",
    )(*operands)


def logits_kernel(offs, gm, mixed, values, seg_col, seg_row, expo, theirs, mine, ones, masks):
    step = pl.program_id(0)
    rows, length = gm.shape[:2]
    half = pl.num_programs(0) // 2

    @pl.when(step == 0)
    def _():
        ones[:, 128:] = jnp.ones_like(ones[:, 128:])
        own = pl.ds(pl.multiple_of(offs[0], length), length)
        for row in range(rows):
            masks[row] = jnp.where(seg_col[row, own, :] == seg_row[row], 1.0, 0.0)

    low_lane = lax.broadcasted_iota(jnp.int32, (length, 128), 1) < 64
    zero = jnp.zeros((length, 128), F32)
    sums = [None, None]
    for row in range(rows):
        ones[:, :128] = values[row]
        scaled = gm[row].astype(F32)
        product = scaled * mixed[row]
        high = product.astype(BF16).astype(F32)
        rest = product - high
        turned_high = pltpu.roll(high, 64, 1)
        turned_rest = pltpu.roll(rest, 64, 1)
        for head in range(2):
            keep = low_lane if head == 0 else jnp.logical_not(low_lane)
            left = jnp.concatenate(
                [
                    jnp.where(keep, scaled, zero).astype(BF16),
                    (-jnp.where(keep, high, turned_rest)).astype(BF16),
                ],
                axis=1,
            )
            part = mm(left, ones[...], 1, 1) * masks[row]
            sums[head] = part if sums[head] is None else sums[head] + part
    for head in range(2):
        grad = (expo[head].astype(F32) * sums[head]).astype(BF16).T

        @pl.when(step < half)
        def _(head=head, grad=grad):
            theirs[head] = grad

        @pl.when(step >= half)
        def _(head=head, grad=grad):
            mine[head] = grad


def logits_grad(offs, gm, mixed, values, seg_col, seg_row, expo):
    rows, length, width = gm.shape
    heads, _, full = expo.shape
    pairs = heads // 2
    half = pairs // 2
    pick = lambda i, offs: lax.rem(i + half * (1 + offs[2]), pairs)
    return pl.pallas_call(
        logits_kernel,
        grid_spec=pltpu.PrefetchScalarGridSpec(
            num_scalar_prefetch=1,
            grid=(pairs,),
            in_specs=[
                pl.BlockSpec((rows, length, 128), lambda i, offs: (0, 0, pick(i, offs))),
                pl.BlockSpec((rows, length, 128), lambda i, offs: (0, 0, pick(i, offs))),
                pl.BlockSpec((rows, full, 128), lambda i, offs: (0, 0, pick(i, offs))),
                whole(seg_col.shape),
                whole(seg_row.shape),
                pl.BlockSpec((2, length, full), lambda i, offs: (pick(i, offs), 0, 0)),
            ],
            out_specs=[
                pl.BlockSpec((2, full, length), lambda i, offs: (jnp.minimum(i, half - 1), 0, 0)),
                pl.BlockSpec((2, full, length), lambda i, offs: (jnp.maximum(i - half, 0), 0, 0)),
            ],
            scratch_shapes=[pltpu.VMEM((full, 256), BF16), pltpu.VMEM((rows, length, full), F32)],
        ),
        out_shape=[jax.ShapeDtypeStruct((heads // 2, full, length), BF16)] * 2,
        compiler_params=pltpu.CompilerParams(vmem_limit_bytes=40 * MIB),
        cost_estimate=pl.CostEstimate(
            flops=2 * rows * heads * length * full * 256, bytes_accessed=16 * MIB, transcendentals=0
        ),
        name="logits_grad",
    )(offs, gm, mixed, values, seg_col, seg_row, expo)


def square_kernel(core, mixed, grad_resid, h1, gv, vectors, theirs, mine):
    width = mixed.shape[1]
    out_w = mm(mixed[...].astype(BF16), grad_resid[...].astype(BF16), 0, 0).astype(BF16)
    value_w = mm(h1[...], gv[...], 0, 0).astype(BF16)
    for at, (first, second) in enumerate(((mine, theirs), (theirs, mine))):

        @pl.when(core[0] == at)
        def _(first=first, second=second):
            first[:, :width] = out_w
            second[:, :width] = value_w
            first[:, width:] = vectors[...]
            second[:, width:] = jnp.zeros_like(vectors)


def square_grads(core, mixed, grad_resid, h1, gv, vectors):
    width = mixed.shape[1]
    operands = (mixed, grad_resid, h1, gv, vectors)
    shape = (width, width + 128)
    return pl.pallas_call(
        square_kernel,
        grid_spec=pltpu.PrefetchScalarGridSpec(
            num_scalar_prefetch=1,
            grid=(1,),
            in_specs=[whole(a.shape) for a in operands],
            out_specs=[whole(shape)] * 2,
        ),
        out_shape=[jax.ShapeDtypeStruct(shape, BF16)] * 2,
        compiler_params=pltpu.CompilerParams(vmem_limit_bytes=48 * MIB),
        cost_estimate=pl.CostEstimate(
            flops=2 * width * width * (mixed.shape[0] + h1.shape[0]), bytes_accessed=16 * MIB, transcendentals=0
        ),
        name="square_grads",
    )(core, *operands)


def input_kernel(chained, x, grad_resid, gh_own, gh_received, g1, *rest):
    grad = rest[1 if chained else 0]
    unit, scale = unit_rows(x[0].astype(F32))
    total = gh_own[0] + gh_received[0].astype(F32)
    grad[0] = grad_resid[0] + norm_back(total, unit, scale, g1[...])


def input_rows(first, count, inputs, grad_resid, gh_own, gh_received, g1, chain):
    rows, length, width = inputs.shape
    operands = [inputs, grad_resid, gh_own, gh_received, g1]
    in_specs = [by_row(first, (length, width))] * 3 + [by_row(0, (length, width)), whole(g1.shape)]
    aliases = {}
    if chain is not None:
        aliases = {len(operands): 0}
        operands.append(chain)
        in_specs.append(pl.BlockSpec(memory_space=pl.ANY))
    return pl.pallas_call(
        functools.partial(input_kernel, chain is not None),
        grid=(count,),
        in_specs=in_specs,
        out_specs=by_row(first, (length, width)),
        out_shape=jax.ShapeDtypeStruct((rows, length, width), F32),
        input_output_aliases=aliases,
        compiler_params=pltpu.CompilerParams(vmem_limit_bytes=24 * MIB),
        cost_estimate=pl.CostEstimate(flops=10**7, bytes_accessed=4 * MIB, transcendentals=0),
        name="input_rows",
    )(*operands)


def swap(a, axis, size, bit):
    return lax.ppermute(a, axis, [(i, i ^ bit) for i in range(size)])


def total(parts):
    out = parts[0].astype(F32)
    for p in parts[1:]:
        out = out + p.astype(F32)
    return out


def halve(parts, dim, bit, axis, size, step):
    pick = lambda p, b: lax.dynamic_index_in_dim(p, b, dim, keepdims=False)
    sent = total([pick(p, 1 - bit) for p in parts]).astype(BF16)
    return [pick(p, bit) for p in parts] + [swap(sent, axis, size, step)]


def paired_shards(
    dp,
    mp,
    inputs,
    segment_ids,
    ln1_gain,
    ln1_bias,
    value_weight,
    value_bias,
    random_logits,
    out_weight,
    out_bias,
    ln2_gain,
    ln2_bias,
    up_weight,
    up_bias,
    down_weight,
    down_bias,
    out_cotangent,
):
    rows, length, width = inputs.shape
    heads = random_logits.shape[0]
    full = segment_ids.shape[1]
    positions = rows * length
    hidden = up_weight.shape[1]
    tile = hidden // 2
    me = lax.axis_index("mp")
    place = lax.axis_index("dp")
    bits = dp.bit_length() - 1
    bit = [lax.rem(lax.div(place, 1 << b), 2) for b in range(bits)]
    core = bit[0]
    core_at = core.reshape(1).astype(jnp.int32)
    offs = jnp.stack([me * length, (1 - me) * length, core]).astype(jnp.int32)
    row_vector = lambda v: v.astype(F32).reshape(1, -1)
    g1, b1, g2, b2 = (row_vector(v) for v in (ln1_gain, ln1_bias, ln2_gain, ln2_bias))
    bv, bo, bd = (row_vector(v) for v in (value_bias, out_bias, down_bias))

    received = [swap(inputs[r : r + 1], "mp", mp, 1) for r in range(rows)]
    column = core * tile
    packed = jnp.concatenate(
        [
            lax.dynamic_slice_in_dim(up_weight, column, tile, 1),
            lax.dynamic_slice_in_dim(down_weight, column, tile, 0),
            jnp.broadcast_to(lax.dynamic_slice_in_dim(up_bias, column, tile, 0)[None], (16, tile)),
        ],
        axis=0,
    )
    packed, _ = lax.optimization_barrier((packed, received[1]))
    w_mine = swap(packed, "mp", mp, 1)
    w_theirs = swap(w_mine, "dp", dp, 1)

    expo = jnp.exp(random_logits.astype(F32)).astype(BF16)
    seg_col = segment_ids[:, :, None]
    seg_row = segment_ids[:, None, :]
    g = out_cotangent.reshape(positions, width)
    gt = g.T

    chain = None
    for r in range(rows):
        chain = mix_rows(
            r,
            1,
            offs,
            inputs,
            received[r],
            seg_col,
            seg_row,
            expo,
            (value_weight, bv, out_weight, bo, g1, b1, g2, b2),
            chain,
        )
    h1, values, recip, mixed, resid, h2, h2t = chain
    h2 = h2.reshape(positions, width)
    out, dh, own_theirs, own_mine, b_own_theirs, b_own_mine = own_hidden(
        core_at, h2, g, h2t, gt, up_weight, row_vector(up_bias), down_weight
    )
    out, dh, other_mine, other_theirs, b_other_mine, b_other_theirs = other_hidden(
        h2, g, h2t, gt, w_mine, w_theirs, out, dh
    )

    shape = (rows, length, width)
    row_arrays = [out.reshape(shape), dh.reshape(shape), resid, out_cotangent, mixed, recip, inputs]
    chain = None
    passed = []
    for r in range(rows):
        chain = back_rows(
            r, 1, offs, row_arrays, received[r], seg_col, seg_row, expo, (out_weight, value_weight, g2, bd), chain
        )
        passed.append(swap(chain[5], "mp", mp, 1))
    layer_out, grad_resid, gm, gv, gh_own, _, vec_two, vec_one = chain

    logits_theirs, logits_mine = logits_grad(offs, gm, mixed, values, seg_col, seg_row, expo)

    by_core = lambda first, second: jnp.where(core == 0, first, second)
    in_order = lambda mine, theirs, dim: by_core(
        jnp.concatenate([mine, theirs], dim), jnp.concatenate([theirs, mine], dim)
    )
    bias_own = in_order(b_own_mine, b_own_theirs, 1)
    bias_other = in_order(b_other_mine, b_other_theirs, 1)
    bias_all = jnp.where(
        me == 0, jnp.concatenate([bias_own, bias_other], 0), jnp.concatenate([bias_other, bias_own], 0)
    )
    bias_columns = bias_all.reshape(mp, dp, hidden // dp).transpose(1, 0, 2).reshape(width, -1)
    vectors = jnp.concatenate([jnp.sum(vec_two, 0), jnp.sum(vec_one, 0)], 0).T
    used = vectors.shape[1]
    vectors = jnp.concatenate([vectors, bias_columns], 1).astype(BF16)
    vectors = jnp.pad(vectors, ((0, 0), (0, 128 - vectors.shape[1])))
    square_theirs, square_mine = square_grads(
        core_at,
        mixed.reshape(positions, width),
        grad_resid.reshape(positions, width),
        h1.reshape(rows * full, width),
        gv.reshape(rows * full, width),
        vectors,
    )

    def scatter(mine, theirs, lead, rest):
        parts = [mine, swap(theirs, "dp", dp, 1)]
        parts = [p.reshape(lead + (2,) * (bits - 1) + rest) for p in parts]
        for b in range(1, bits):
            parts = halve(parts, len(lead) + bits - 1 - b, bit[b], "dp", dp, 1 << b)
        return parts

    def over_cores(parts, dim):
        whole_sum = total(parts)
        pick = lambda b: lax.dynamic_index_in_dim(whole_sum, b, dim, keepdims=False)
        return pick(core), swap(pick(1 - core).astype(BF16), "dp", dp, 1).astype(F32)

    hidden_shape = (2, width // dp, tile)
    own = scatter(own_mine, own_theirs, (2,), hidden_shape)
    other = scatter(other_mine, other_theirs, (2,), hidden_shape)
    own.append(swap(total(other).astype(BF16), "mp", mp, 1))
    weight_parts = in_order(*over_cores(own, 1), 2)
    logit_parts = scatter(logits_mine, logits_theirs, (heads // 2,), (2, full // dp, length))
    logit_part = in_order(*over_cores(logit_parts, 1), 0).transpose(0, 2, 1)
    square = scatter(square_mine, square_theirs, (), (2, mp, width // (dp * mp), width + 128))
    square = halve(square, 1, me, "mp", mp, 1)
    kept, other_kept = over_cores(square, 0)
    first, second = by_core(kept, other_kept), by_core(other_kept, kept)
    vector_part = first[:, width:]
    column = lambda i: vector_part[:, i]

    chain = None
    for r in range(rows):
        chain = input_rows(r, 1, inputs, grad_resid, gh_own, passed[r], g1, chain)
    return (
        layer_out,
        chain,
        column(4),
        column(5),
        second[:, :width],
        column(6),
        logit_part,
        first[:, :width],
        column(0),
        column(1),
        column(2),
        weight_parts[0],
        vector_part[:, used : used + hidden // dp // (width // (dp * mp))].reshape(1, -1),
        weight_parts[1].T,
        column(3),
    )


def smooth(t):
    return jax.nn.gelu(t, approximate=True)


def contract_rows(left, right):
    return lax.dot_general(
        left, right, (((0,), (0,)), ((), ())), preferred_element_type=jnp.float32
    )


def contract_cols(left, right):
    return lax.dot_general(
        left, right, (((1,), (1,)), ((), ())), preferred_element_type=jnp.float32
    )


def normalize(x, gain, shift):
    centred = x - jnp.mean(x, -1, keepdims=True)
    scale = lax.rsqrt(jnp.mean(centred * centred, -1, keepdims=True) + 1e-05)
    unit = centred * scale
    return (unit * gain + shift, unit, scale)


def normalize_back(grad, unit, scale, gain):
    scaled = grad * gain
    inner = scale * (
        scaled
        - jnp.mean(scaled, -1, keepdims=True)
        - unit * jnp.mean(scaled * unit, -1, keepdims=True)
    )
    return (inner, jnp.sum(grad * unit, 0), jnp.sum(grad, 0))


def shards(
    inputs,
    segment_ids,
    ln1_gain,
    ln1_bias,
    value_weight,
    value_bias,
    random_logits,
    out_weight,
    out_bias,
    ln2_gain,
    ln2_bias,
    up_weight,
    up_bias,
    down_weight,
    down_bias,
    out_cotangent,
):
    seqs, local_len, width = inputs.shape
    heads = random_logits.shape[0]
    full_len = segment_ids.shape[1]
    head_dim = width // heads
    rows = seqs * local_len
    gain_one = ln1_gain.astype(jnp.float32)
    gain_two = ln2_gain.astype(jnp.float32)
    start_x = inputs.astype(jnp.float32).reshape(rows, width)
    normed_one, unit_one, scale_one = normalize(start_x, gain_one, ln1_bias.astype(jnp.float32))
    h1_low = normed_one.astype(jnp.bfloat16)
    values = (
        jnp.dot(h1_low, value_weight, preferred_element_type=jnp.float32)
        + value_bias.astype(jnp.float32)
    ).astype(jnp.bfloat16)
    gathered = lax.all_gather(values.reshape(seqs, local_len, width), "mp", axis=1, tiled=True)
    every_head = gathered.reshape(seqs, full_len, heads, head_dim)
    offset = lax.axis_index("mp") * local_len
    own_segs = lax.dynamic_slice_in_dim(segment_ids, offset, local_len, 1)
    same = own_segs[:, :, None] == segment_ids[:, None, :]
    scores = jnp.where(same[:, None], random_logits.astype(jnp.float32)[None], -1e30)
    peak = jnp.max(scores, -1, keepdims=True)
    expo = jnp.exp(scores - peak)
    total = jnp.sum(expo, -1, keepdims=True)
    probs = expo / total
    probs_low = probs.astype(jnp.bfloat16)
    mixed = jnp.einsum("shqk,skhd->sqhd", probs_low, every_head, preferred_element_type=jnp.float32)
    mixed_low = mixed.reshape(rows, width).astype(jnp.bfloat16)
    resid = (
        start_x
        + jnp.dot(mixed_low, out_weight, preferred_element_type=jnp.float32)
        + out_bias.astype(jnp.float32)
    )
    normed_two, unit_two, scale_two = normalize(resid, gain_two, ln2_bias.astype(jnp.float32))
    h2_low = normed_two.astype(jnp.bfloat16)
    grad_low = out_cotangent.reshape(rows, width)
    h2_full = lax.all_gather(
        h2_low.reshape(seqs, local_len, width), "mp", axis=1, tiled=True
    ).reshape(seqs * full_len, width)
    pre = jnp.dot(h2_full, up_weight, preferred_element_type=jnp.float32) + up_bias.astype(
        jnp.float32
    )
    act, gelu_pull = jax.vjp(smooth, pre)
    act_low = act.astype(jnp.bfloat16)
    partial_out = jnp.dot(act_low, down_weight, preferred_element_type=jnp.float32).reshape(
        seqs, full_len, width
    )
    ffn_out = lax.psum_scatter(
        partial_out.astype(jnp.bfloat16), "mp", scatter_dimension=1, tiled=True
    ).astype(jnp.float32).reshape(rows, width) + down_bias.astype(jnp.float32)
    final = resid + ffn_out
    grad_full = lax.all_gather(out_cotangent, "mp", axis=1, tiled=True).reshape(
        seqs * full_len, width
    )
    grad_down = contract_rows(act_low, grad_full)
    grad_act = contract_cols(grad_full, down_weight)
    grad_pre = gelu_pull(grad_act)[0].astype(jnp.bfloat16)
    grad_up_b = jnp.sum(grad_pre.astype(jnp.float32), 0)
    grad_up = contract_rows(h2_full, grad_pre)
    h2_terms = contract_cols(grad_pre, up_weight).reshape(seqs, full_len, width)
    grad_h2 = (
        lax.psum_scatter(h2_terms.astype(jnp.bfloat16), "mp", scatter_dimension=1, tiled=True)
        .astype(jnp.float32)
        .reshape(rows, width)
    )
    grad_final = grad_low.astype(jnp.float32)
    grad_down_b = jnp.sum(grad_final, 0)
    inner_two, gain_two_grad, shift_two_grad = normalize_back(
        grad_h2, unit_two, scale_two, gain_two
    )
    grad_resid = grad_final + inner_two
    grad_o_low = grad_resid.astype(jnp.bfloat16)
    grad_out_b = jnp.sum(grad_o_low.astype(jnp.float32), 0)
    grad_out_w = contract_rows(mixed_low, grad_o_low)
    grad_mixed = (
        contract_cols(grad_o_low, out_weight)
        .astype(jnp.bfloat16)
        .reshape(seqs, local_len, heads, head_dim)
    )
    grad_probs = jnp.einsum(
        "sqhd,skhd->shqk", grad_mixed, every_head, preferred_element_type=jnp.float32
    )
    grad_scores = probs * (grad_probs - jnp.sum(probs * grad_probs, -1, keepdims=True))
    grad_logits = jnp.sum(grad_scores, 0)
    value_terms = jnp.einsum(
        "shqk,sqhd->skhd", probs_low, grad_mixed, preferred_element_type=jnp.float32
    ).reshape(seqs, full_len, width)
    grad_values = (
        lax.psum_scatter(value_terms.astype(jnp.bfloat16), "mp", scatter_dimension=1, tiled=True)
        .astype(jnp.float32)
        .reshape(rows, width)
        .astype(jnp.bfloat16)
    )
    grad_value_b = jnp.sum(grad_values.astype(jnp.float32), 0)
    grad_value_w = contract_rows(h1_low, grad_values)
    inner_one, gain_one_grad, shift_one_grad = normalize_back(
        contract_cols(grad_values, value_weight), unit_one, scale_one, gain_one
    )
    grad_x = (grad_resid + inner_one).reshape(seqs, local_len, width)
    vectors = jnp.stack(
        [
            gain_one_grad,
            shift_one_grad,
            grad_value_b,
            grad_out_b,
            gain_two_grad,
            shift_two_grad,
            grad_down_b,
        ]
    )
    value_w_part, out_w_part, vector_part = (
        lax.psum_scatter(grad_value_w, ("dp", "mp"), scatter_dimension=0, tiled=True),
        lax.psum_scatter(grad_out_w, ("dp", "mp"), scatter_dimension=0, tiled=True),
        lax.psum_scatter(vectors, ("dp", "mp"), scatter_dimension=1, tiled=True),
    )
    up_part, up_b_part, down_part, logit_part = (
        lax.psum_scatter(
            grad_up.astype(jnp.bfloat16), "dp", scatter_dimension=0, tiled=True
        ).astype(jnp.float32),
        lax.psum_scatter(
            grad_up_b[None].astype(jnp.bfloat16), "dp", scatter_dimension=1, tiled=True
        ).astype(jnp.float32),
        lax.psum_scatter(
            grad_down.astype(jnp.bfloat16), "dp", scatter_dimension=1, tiled=True
        ).astype(jnp.float32),
        lax.psum_scatter(
            grad_logits.astype(jnp.bfloat16), "dp", scatter_dimension=2, tiled=True
        ).astype(jnp.float32),
    )
    return (
        final.astype(jnp.bfloat16).reshape(seqs, local_len, width),
        grad_x,
        vector_part[0],
        vector_part[1],
        value_w_part,
        vector_part[2],
        logit_part,
        out_w_part,
        vector_part[3],
        vector_part[4],
        vector_part[5],
        up_part,
        up_b_part,
        down_part,
        vector_part[6],
    )


def solution(mesh):
    in_specs = (
        P("dp", "mp", None),
        P("dp", None),
        P(),
        P(),
        P(),
        P(),
        P(None, "mp", None),
        P(),
        P(),
        P(),
        P(),
        P(None, "mp"),
        P("mp"),
        P("mp", None),
        P(),
        P("dp", "mp", None),
    )
    out_specs = (
        P("dp", "mp", None),
        P("dp", "mp", None),
        P(("dp", "mp")),
        P(("dp", "mp")),
        P(("dp", "mp"), None),
        P(("dp", "mp")),
        P(None, "mp", "dp"),
        P(("dp", "mp"), None),
        P(("dp", "mp")),
        P(("dp", "mp")),
        P(("dp", "mp")),
        P("dp", "mp"),
        P("mp", "dp"),
        P("mp", "dp"),
        P(("dp", "mp")),
    )
    dp, mp = mesh.shape["dp"], mesh.shape["mp"]
    body = functools.partial(paired_shards, dp, mp) if mp == 2 else shards
    return jax.shard_map(body, mesh=mesh, in_specs=in_specs, out_specs=out_specs, check_vma=False)
```

```python
import functools

import jax
import jax.numpy as jnp
from jax import lax
from jax.experimental import pallas as pl
from jax.experimental.pallas import tpu as pltpu
from jax.sharding import PartitionSpec as P

F32 = jnp.float32
BF16 = jnp.bfloat16
GELU_A = 0.7978845608028654
GELU_B = GELU_A * 0.044715
MIB = 2**20


def mm(left, right, left_dim, right_dim):
    return lax.dot_general(
        left, right, (((left_dim,), (right_dim,)), ((), ())), preferred_element_type=F32
    )


def unit_rows(x):
    centred = x - jnp.mean(x, -1, keepdims=True)
    scale = lax.rsqrt(jnp.mean(centred * centred, -1, keepdims=True) + 1e-05)
    return centred * scale, scale


def norm_back(grad, unit, scale, gain):
    e = grad * gain
    return scale * (
        e - jnp.mean(e, -1, keepdims=True) - unit * jnp.mean(e * unit, -1, keepdims=True)
    )


def same_document(first, seg_row, row, length):
    keys = seg_row[row].astype(F32)
    own = seg_row[row, :, pl.ds(pl.multiple_of(first, length), length)].astype(F32)
    queries = jnp.broadcast_to(own, (8, length)).T[:, :1]
    return jnp.where(queries == keys, 1.0, 0.0)


def turned(block, near, blocks):
    other = jnp.bitwise_xor(block, near)
    place = 0
    weight = blocks
    for b in range(blocks.bit_length() - 1):
        weight //= 2
        place = place + jnp.bitwise_and(lax.shift_right_logical(other, b), 1) * weight
    return place


def long_cost(us):
    return pl.CostEstimate(flops=int(us * 10**10), bytes_accessed=10**5, transcendentals=0)


IN_VMEM = pl.BlockSpec(memory_space=pltpu.VMEM)
ANYWHERE = pl.BlockSpec(memory_space=pl.ANY)


def in_hbm(operands):
    return [pltpu.with_memory_space_constraint(a, pltpu.HBM) for a in operands]


def in_vmem(operands):
    return [pltpu.with_memory_space_constraint(a, pltpu.VMEM) for a in operands]


TOKEN = pltpu.HBM((8, 128), F32)


def whole(shape):
    return pl.BlockSpec(shape, lambda i, *_: (0,) * len(shape))


def by_row(first, shape):
    return pl.BlockSpec((1,) + shape, lambda i, *_: (first + i,) + (0,) * len(shape))


def prep_kernel(*refs):
    *vectors, bias, small, hidden = refs
    for i, v in enumerate(vectors):
        small[i : i + 1, :] = v[...].astype(F32).reshape(1, -1)
    hidden[...] = bias[...].astype(F32).reshape(1, -1)


def prep(vectors, bias):
    return pl.pallas_call(
        prep_kernel,
        in_specs=[IN_VMEM] * (len(vectors) + 1),
        out_specs=[IN_VMEM] * 2,
        out_shape=[
            pltpu.HBM((8, vectors[0].shape[0]), F32),
            pltpu.HBM((1, bias.shape[0]), F32),
        ],
        name="prep",
    )(*vectors, bias)


def mix_kernel(offs, x_own, x_other, g, seg_row, expo, wv, wo, small, *rest):
    h1, values, recip, mixed, resid, h2, h2t, gt, token, ones = rest[-10:]
    g1, b1, g2, b2, bv, bo, _ = (small[i : i + 1, :] for i in range(7))
    token[...] = jnp.zeros_like(token)
    length = x_own.shape[1]
    heads = expo.shape[0]
    ones[:, 128:] = jnp.ones_like(ones[:, 128:])
    x = x_own[0].astype(F32)
    for block, off in ((x, offs[0]), (x_other[0].astype(F32), offs[1])):
        unit, _ = unit_rows(block)
        at = pl.ds(pl.multiple_of(off, length), length)
        h1[0, at, :] = (unit * g1 + b1).astype(BF16)
    values[0] = (mm(h1[0], wv[...], 1, 0) + bv).astype(BF16)
    mask = same_document(offs[0], seg_row, 0, length).astype(BF16)
    low_lane = lax.broadcasted_iota(jnp.int32, (length, 128), 1) < 64
    for pair in range(heads // 2):
        lanes = slice(128 * pair, 128 * pair + 128)
        ones[:, :128] = values[0, :, lanes]
        first = mm(expo[2 * pair] * mask, ones[...], 1, 0)
        second = mm(expo[2 * pair + 1] * mask, ones[...], 1, 0)
        inverse = 1.0 / jnp.where(low_lane, first[:, 128:], second[:, 128:])
        recip[0, :, lanes] = inverse
        mixed[0, :, lanes] = jnp.where(low_lane, first[:, :128], second[:, :128]) * inverse
    r = x + mm(mixed[0].astype(BF16), wo[...], 1, 0) + bo
    resid[0] = r
    unit, _ = unit_rows(r)
    low = (unit * g2 + b2).astype(BF16)
    h2[0] = low
    blocks, size, _ = h2t.shape
    for ref, source in ((h2t, low.T), (gt, g[0].T)):
        for j in range(blocks):
            ref[turned(j, offs[3], blocks)] = source[j * size : (j + 1) * size, :]


def mix_rows(first, count, offs, blocks, inputs, received, cotangent, seg_row, expo, weights, chain):
    rows, length, width = inputs.shape
    full = seg_row.shape[2]
    heads = expo.shape[0]
    shapes = [
        ((full, width), BF16),
        ((full, width), BF16),
        ((length, width), F32),
        ((length, width), F32),
        ((length, width), F32),
        ((length, width), BF16),
    ]
    out_specs = [by_row(first, s) for s, _ in shapes]
    turned_spec = pl.BlockSpec((blocks, width // blocks, length), lambda i, *_: (0, 0, first + i))
    out_specs += [turned_spec] * 2
    out_shape = [pltpu.HBM((rows,) + s, t) for s, t in shapes[:5]]
    out_shape += [pltpu.VMEM((rows,) + s, t) for s, t in shapes[5:]]
    out_shape += [pltpu.VMEM((blocks, width // blocks, rows * length), BF16)] * 2
    operands = [offs, *in_hbm([inputs]), received, *in_hbm([cotangent, seg_row, expo, *weights])]
    in_specs = [
        by_row(first, (length, width)),
        by_row(0, (length, width)),
        by_row(first, (length, width)),
        by_row(first, (1, full)),
        whole(expo.shape),
        *[whole(w.shape) for w in weights],
    ]
    aliases = {}
    if chain is not None:
        aliases = {len(operands) + i: i for i in range(len(out_shape))}
        operands += [*in_hbm(chain[:5]), *in_vmem(chain[5:8])]
        in_specs += [ANYWHERE] * len(out_shape)
    out_specs.append(whole((8, 128)))
    out_shape.append(TOKEN)
    return pl.pallas_call(
        mix_kernel,
        grid_spec=pltpu.PrefetchScalarGridSpec(
            num_scalar_prefetch=1,
            grid=(count,),
            in_specs=in_specs,
            out_specs=out_specs,
            scratch_shapes=[pltpu.VMEM((full, 256), BF16)],
        ),
        out_shape=out_shape,
        input_output_aliases=aliases,
        compiler_params=pltpu.CompilerParams(vmem_limit_bytes=32 * MIB),
        cost_estimate=long_cost(3 * count),
        name="mix_rows",
    )(*operands)


def gelu_pair(t):
    square = t * t
    curve = jnp.tanh(t * (GELU_A + GELU_B * square))
    half = 0.5 + 0.5 * curve
    act = t * half
    return act, half + act * (1.0 - curve) * (GELU_A + 3 * GELU_B * square)


def hidden_tile(h2, g, h2t, gt, wu, up_dim, bu, wd, sums, outs, act_s, pre_s, block):
    out0, dh0 = sums if sums else (None, None)
    out, dh = outs
    total = None
    for m in range(h2.shape[0] // block):
        at = pl.ds(m * block, block)
        pre = mm(h2[at, :], wu[...], 1, up_dim) + bu
        grad_act = mm(g[at, :], wd[...], 1, 1)
        act, slope = gelu_pair(pre)
        act_low = act.astype(BF16)
        grad_pre = grad_act * slope
        part = jnp.sum(grad_pre, 0, keepdims=True)
        total = part if total is None else total + part
        pre_low = grad_pre.astype(BF16)
        act_s[at, :] = act_low
        pre_s[at, :] = pre_low
        out_part = mm(act_low, wd[...], 1, 0)
        dh_part = mm(pre_low, wu[...], 1, 1 - up_dim)
        out[at, :] = out_part if sums is None else out0[at, :] + out_part
        dh[at, :] = dh_part if sums is None else dh0[at, :] + dh_part
    return total, lambda: (
        mm(h2t[...], pre_s[...], 1, 0).astype(BF16),
        mm(gt[...], act_s[...], 1, 0).astype(BF16),
    )


def own_hidden_kernel(block, first, at_ref, h2, g, h2t, gt, wu, bu, wd, *rest):
    out, dh, grads, bias, token, act_s, pre_s = rest[-7:]
    token[...] = jnp.zeros_like(token)
    sums = None
    if not first:
        out0, dh0, bias0 = rest[:3]
        sums = (out0, dh0)
    total, weights = hidden_tile(
        h2, g, h2t, gt, wu, 0, bu[...].astype(F32), wd, sums, (out, dh), act_s, pre_s, block
    )
    if first:
        bias[0:1, :] = total
    else:
        bias[...] = bias0[...]
        bias[1:2, :] = total
    for which, grad in enumerate(weights()):
        grads[which] = grad


def other_hidden_kernel(block, which, near, h2, g, h2t, gt, wx, wy, wcx, wcy, out0, dh0, bias0, *rest):
    out, dh, mine, theirs, bias, token, wu, wd, act_s, pre_s = rest[-10:]
    token[...] = jnp.zeros_like(token)
    near_y = near[0]
    part = wx.shape[0] // 2 - 8
    for first, pieces in ((0, (wx, wy)), (2, (wcx, wcy))):
        for turn, piece in enumerate(pieces):
            quarter = first + jnp.bitwise_xor(near_y, turn)
            at = pl.ds(pl.multiple_of(quarter * part, part), part)
            wu[at, :] = piece[:part, :]
            wd[at, :] = piece[part : 2 * part, :]
    rows = wx[2 * part :, :].astype(F32)
    lower, upper = rows[0:1, :], rows[1:2, :]
    swapped = near[1] == 1
    bu = jnp.concatenate(
        [
            row[:, (2 * b + which) * part : (2 * b + which + 1) * part]
            for row in (jnp.where(swapped, upper, lower), jnp.where(swapped, lower, upper))
            for b in range(2)
        ],
        axis=1,
    )
    total, weights = hidden_tile(
        h2, g, h2t, gt, wu, 1, bu, wd, (out0, dh0), (out, dh), act_s, pre_s, block
    )
    bias[...] = bias0[...]
    bias[2 + which : 3 + which, :] = total
    half = 2 * part
    for index, grad in enumerate(weights()):
        mine[0, index] = grad[:, :half]
        theirs[0, index] = grad[:, half:]


def hidden_call(positions, width, tile):
    return dict(
        compiler_params=pltpu.CompilerParams(vmem_limit_bytes=30 * MIB),
        cost_estimate=long_cost(5),
    )


def own_hidden(tile_at, fixed, wu, bu, wd, sums, *tokens):
    positions, width = fixed[0].shape
    tile = wu.shape[1] // 2
    operands = [*in_vmem(fixed), *in_hbm([wu, bu, wd]), *in_vmem(sums or ()), *tokens]
    aliases = {1 + len(fixed) + 3: 0, 1 + len(fixed) + 4: 1} if sums else {}
    weights = [
        pl.BlockSpec((width, tile), lambda i, at: (0, at[0])),
        pl.BlockSpec((1, tile), lambda i, at: (0, at[0])),
        pl.BlockSpec((tile, width), lambda i, at: (at[0], 0)),
    ]
    return pl.pallas_call(
        functools.partial(own_hidden_kernel, 256, sums is None),
        grid_spec=pltpu.PrefetchScalarGridSpec(
            num_scalar_prefetch=1,
            grid=(1,),
            in_specs=[IN_VMEM] * len(fixed) + weights + [IN_VMEM] * len(sums or ()) + [ANYWHERE] * len(tokens),
            out_specs=[IN_VMEM] * 2 + [whole((2, width, tile)), IN_VMEM, whole((8, 128))],
            scratch_shapes=[pltpu.VMEM((positions, tile), BF16)] * 2,
        ),
        out_shape=[pltpu.VMEM((positions, width), F32)] * 2
        + [pltpu.HBM((2, width, tile), BF16), pltpu.VMEM((8, tile), F32), TOKEN],
        input_output_aliases=aliases,
        name="own_hidden",
        **hidden_call(positions, width, tile),
    )(tile_at, *operands)


def other_hidden(which, near, fixed, pieces, sums, grads, *tokens):
    positions, width = fixed[0].shape
    tile = 4 * (pieces[0].shape[0] // 2 - 8)
    operands = [*in_vmem(fixed), *pieces, *in_vmem(sums)]
    extra = [*in_hbm(grads or ()), *tokens]
    aliases = {1 + len(operands) - 3: 0, 1 + len(operands) - 2: 1}
    if grads:
        aliases |= {1 + len(operands): 2, 2 + len(operands): 3}
    block = pl.BlockSpec((1, 2, width, tile // 2), lambda i, *_: (which, 0, 0, 0))
    return pl.pallas_call(
        functools.partial(other_hidden_kernel, 256, which),
        grid_spec=pltpu.PrefetchScalarGridSpec(
            num_scalar_prefetch=1,
            grid=(1,),
            in_specs=[IN_VMEM] * 4 + [whole(p.shape) for p in pieces] + [IN_VMEM] * 3 + [ANYWHERE] * len(extra),
            out_specs=[IN_VMEM] * 2 + [block] * 2 + [IN_VMEM, whole((8, 128))],
            scratch_shapes=[pltpu.VMEM((tile, width), BF16)] * 2 + [pltpu.VMEM((positions, tile), BF16)] * 2,
        ),
        out_shape=[pltpu.VMEM((positions, width), F32)] * 2
        + [pltpu.HBM((2, 2, width, tile // 2), BF16)] * 2
        + [pltpu.VMEM((8, tile), F32), TOKEN],
        input_output_aliases=aliases,
        name="other_hidden",
        **hidden_call(positions, width, tile),
    )(near, *operands, *extra)


def pack_kernel(at, up, down, bias, token, first, second):
    size = up.shape[1] // 2
    turned_up = up[...].T
    for p, out in enumerate((first, second)):
        rows = slice(p * size, (p + 1) * size)
        out[:size, :] = turned_up[rows, :]
        out[size : 2 * size, :] = down[rows, :]
        width = down.shape[1]
        both = jnp.concatenate([bias[:, :width], bias[:, width:], jnp.zeros((14, width), F32)], 0)
        out[2 * size :, :] = both.astype(BF16)


def pack(quarter, up, down, bias, token):
    width, hidden = up.shape
    part = hidden // 4
    shape = jax.ShapeDtypeStruct((part + 16, width), BF16)
    return pl.pallas_call(
        pack_kernel,
        grid_spec=pltpu.PrefetchScalarGridSpec(
            num_scalar_prefetch=1,
            grid=(1,),
            in_specs=[
                pl.BlockSpec((width, part), lambda i, at: (0, at[0])),
                pl.BlockSpec((part, width), lambda i, at: (at[0], 0)),
                whole(bias.shape),
                ANYWHERE,
            ],
            out_specs=[whole(shape.shape)] * 2,
        ),
        out_shape=[shape] * 2,
        compiler_params=pltpu.CompilerParams(vmem_limit_bytes=16 * MIB),
        cost_estimate=long_cost(1),
        name="pack",
    )(quarter, *in_hbm([up, down, bias, token]))


def resid_kernel(out_acc, dh, resid, g, recip, wo, small, *rest):
    layer_out, grad_resid, gm, vec = rest[-4:]
    g2, bd = small[2:3, :], small[6:7, :]
    r = resid[0]
    layer_out[0] = (r + out_acc[0] + bd).astype(BF16)
    unit, scale = unit_rows(r)
    grad = dh[0]
    cot = g[0].astype(F32)
    total = cot + norm_back(grad, unit, scale, g2)
    grad_resid[0] = total
    grad_o = total.astype(BF16)
    vec[0, 0:1, :] = jnp.sum(grad_o.astype(F32), 0, keepdims=True)
    vec[0, 1:2, :] = jnp.sum(grad * unit, 0, keepdims=True)
    vec[0, 2:3, :] = jnp.sum(grad, 0, keepdims=True)
    vec[0, 3:4, :] = jnp.sum(cot, 0, keepdims=True)
    gm[0] = (mm(grad_o, wo[...], 1, 1).astype(BF16).astype(F32) * recip[0]).astype(BF16)


def resid_rows(row_arrays, weights, *tokens):
    rows, length, width = row_arrays[0].shape
    shapes = [((length, width), BF16), ((length, width), F32), ((length, width), BF16), ((4, width), F32)]
    return pl.pallas_call(
        resid_kernel,
        grid=(rows,),
        in_specs=[by_row(0, (length, width)) for _ in row_arrays]
        + [whole(w.shape) for w in weights]
        + [ANYWHERE] * len(tokens),
        out_specs=[by_row(0, s) for s, _ in shapes],
        out_shape=[pltpu.HBM((rows,) + s, t) for s, t in shapes],
        compiler_params=pltpu.CompilerParams(vmem_limit_bytes=24 * MIB),
        cost_estimate=long_cost(3),
        name="resid_rows",
    )(*in_vmem(row_arrays[:2]), *in_hbm([*row_arrays[2:], *weights, *tokens]))


def back_kernel(offs, gm, x_own, x_first, x_second, seg_row, expo, wv, *rest):
    gv, gh_own, gh_send, vec_one, gmt, gvt, gh = rest[-7:]
    length = x_own.shape[1]
    heads = expo.shape[0]
    gmt[...] = gm[0].T
    mask = same_document(offs[0], seg_row, 0, length).astype(BF16)
    for head in range(heads):
        at = slice(64 * head, 64 * head + 64)
        gvt[at, :] = mm(gmt[at, :], expo[head] * mask, 1, 0).astype(BF16)
    values_grad = gvt[...].T
    gv[0] = values_grad
    gh[...] = mm(values_grad, wv[...], 1, 1)
    gain = jnp.zeros((1, gh.shape[1]), F32)
    x_other = jnp.where(pl.program_id(0) == 0, x_first[0], x_second[0])
    for block, off in ((x_own[0], offs[0]), (x_other, offs[1])):
        unit, _ = unit_rows(block.astype(F32))
        gain += jnp.sum(gh[pl.ds(pl.multiple_of(off, length), length), :] * unit, 0, keepdims=True)
    vec_one[0, 0:1, :] = gain
    vec_one[0, 1:2, :] = jnp.sum(gh[...], 0, keepdims=True)
    vec_one[0, 2:3, :] = jnp.sum(values_grad.astype(F32), 0, keepdims=True)
    gh_own[0] = gh[pl.ds(pl.multiple_of(offs[0], length), length), :]
    gh_send[0] = gh[pl.ds(pl.multiple_of(offs[1], length), length), :].astype(BF16)


def back_rows(first, count, offs, gm, inputs, received, seg_row, expo, wv, chain, *tokens):
    rows, length, width = inputs.shape
    full = seg_row.shape[2]
    shapes = [((full, width), BF16), ((length, width), F32), ((length, width), BF16), ((3, width), F32)]
    out_specs = [by_row(0 if i == 2 else first, s) for i, (s, _) in enumerate(shapes)]
    out_shape = [
        jax.ShapeDtypeStruct((count,) + s, t) if i == 2 else pltpu.HBM((rows,) + s, t)
        for i, (s, t) in enumerate(shapes)
    ]
    operands = [offs, *in_hbm([gm, inputs]), *received, *in_hbm([seg_row, expo, wv])]
    in_specs = [by_row(first, (length, width))] * 2
    in_specs += [
        whole((1, length, width)),
        whole((1, length, width)),
        by_row(first, (1, full)),
        whole(expo.shape),
        whole(wv.shape),
    ]
    aliases = {}
    if chain is not None:
        aliases = {len(operands) + i: i for i in range(len(out_shape)) if i != 2}
        operands += [*in_hbm(chain[:2]), chain[2], *in_hbm(chain[3:])]
        in_specs += [ANYWHERE] * len(out_shape)
    operands += tokens
    in_specs += [ANYWHERE] * len(tokens)
    return pl.pallas_call(
        back_kernel,
        grid_spec=pltpu.PrefetchScalarGridSpec(
            num_scalar_prefetch=1,
            grid=(count,),
            in_specs=in_specs,
            out_specs=out_specs,
            scratch_shapes=[
                pltpu.VMEM((width, length), BF16),
                pltpu.VMEM((width, full), BF16),
                pltpu.VMEM((full, width), F32),
            ],
        ),
        out_shape=out_shape,
        input_output_aliases=aliases,
        compiler_params=pltpu.CompilerParams(vmem_limit_bytes=32 * MIB),
        cost_estimate=long_cost(2 * count),
        name="back_rows",
    )(*operands)


def send_kernel(count, *refs):
    out = refs[-1]
    sum_of = refs[0][...].astype(F32)
    for part in refs[1:count]:
        sum_of = sum_of + part[...].astype(F32)
    out[...] = sum_of.astype(BF16)


def send_sum(parts, dim, half, index, *tokens):
    shape = parts[0].shape[:dim] + (half,) + parts[0].shape[dim + 1 :]
    place = tuple(index if d == dim else 0 for d in range(len(shape)))
    return pl.pallas_call(
        functools.partial(send_kernel, len(parts)),
        grid=(1,),
        in_specs=[pl.BlockSpec(shape, lambda i: place)] * len(parts) + [ANYWHERE] * len(tokens),
        out_specs=whole(shape),
        out_shape=jax.ShapeDtypeStruct(shape, BF16),
        compiler_params=pltpu.CompilerParams(vmem_limit_bytes=16 * MIB),
        cost_estimate=long_cost(0.5),
        name="send_sum",
    )(*in_hbm(parts[:1]), *parts[1:], *tokens)


def logits_kernel(offs, gm, mixed, values, seg_row, expo, *rest):
    theirs, mine, ones, masks = rest[-4:]
    step = pl.program_id(0)
    rows, length = gm.shape[:2]
    half = pl.num_programs(0) // 2

    @pl.when(step == 0)
    def _():
        ones[:, 128:] = jnp.ones_like(ones[:, 128:])
        for row in range(rows):
            masks[row] = same_document(offs[0], seg_row, row, length)

    low_lane = lax.broadcasted_iota(jnp.int32, (length, 128), 1) < 64
    zero = jnp.zeros((length, 128), F32)
    sums = [None, None]
    for row in range(rows):
        ones[:, :128] = values[row]
        scaled = gm[row].astype(F32)
        product = scaled * mixed[row]
        high = product.astype(BF16).astype(F32)
        rest = product - high
        turned_high = pltpu.roll(high, 64, 1)
        turned_rest = pltpu.roll(rest, 64, 1)
        for head in range(2):
            keep = low_lane if head == 0 else jnp.logical_not(low_lane)
            left = jnp.concatenate(
                [
                    jnp.where(keep, scaled, zero).astype(BF16),
                    (-jnp.where(keep, high, turned_rest)).astype(BF16),
                ],
                axis=1,
            )
            part = mm(left, ones[...], 1, 1) * masks[row]
            sums[head] = part if sums[head] is None else sums[head] + part
    for head in range(2):
        grad = (expo[head].astype(F32) * sums[head]).astype(BF16).T
        for ref, wanted in ((theirs, step < half), (mine, step >= half)):

            @pl.when(wanted)
            def _(head=head, grad=grad, ref=ref):
                blocks, _, size, _ = ref.shape
                for j in range(blocks):
                    ref[turned(j, offs[3], blocks), head] = grad[j * size : (j + 1) * size, :]


def logits_grad(offs, blocks, gm, mixed, values, seg_row, expo, *tokens):
    rows, length, width = gm.shape
    heads, _, full = expo.shape
    pairs = heads // 2
    half = pairs // 2
    pick = lambda i, offs: lax.rem(i + half * (1 + offs[2]), pairs)
    return pl.pallas_call(
        logits_kernel,
        grid_spec=pltpu.PrefetchScalarGridSpec(
            num_scalar_prefetch=1,
            grid=(pairs,),
            in_specs=[
                pl.BlockSpec((rows, length, 128), lambda i, offs: (0, 0, pick(i, offs))),
                pl.BlockSpec((rows, length, 128), lambda i, offs: (0, 0, pick(i, offs))),
                pl.BlockSpec((rows, full, 128), lambda i, offs: (0, 0, pick(i, offs))),
                whole(seg_row.shape),
                pl.BlockSpec((2, length, full), lambda i, offs: (pick(i, offs), 0, 0)),
            ]
            + [ANYWHERE] * len(tokens),
            out_specs=[
                pl.BlockSpec((blocks, 2, full // blocks, length), lambda i, offs: (0, jnp.minimum(i, half - 1), 0, 0)),
                pl.BlockSpec((blocks, 2, full // blocks, length), lambda i, offs: (0, jnp.maximum(i - half, 0), 0, 0)),
            ],
            scratch_shapes=[pltpu.VMEM((full, 256), BF16), pltpu.VMEM((rows, length, full), F32)],
        ),
        out_shape=[
            make((blocks, heads // 2, full // blocks, length), BF16)
            for make in (jax.ShapeDtypeStruct, pltpu.HBM)
        ],
        compiler_params=pltpu.CompilerParams(vmem_limit_bytes=32 * MIB),
        cost_estimate=long_cost(5),
        name="logits_grad",
    )(offs, *in_hbm([gm, mixed, values, seg_row, expo]), *tokens)


def square_kernel(at_ref, mixed, grad_resid, h1, gv, bias, vec_two, vec_one, *rest):
    theirs, mine = rest[-2:]
    width = mixed.shape[1]
    rows = vec_two.shape[0]
    core, near, me = at_ref[0], at_ref[1], at_ref[2]
    blocks, chunks, size, _ = mine.shape
    size -= 8
    out_w = mm(mixed[...].astype(BF16), grad_resid[...].astype(BF16), 0, 0)
    value_w = mm(h1[...], gv[...], 0, 0)
    vectors = [sum(ref[r, i : i + 1, :] for r in range(rows)) for ref, n in ((vec_two, 4), (vec_one, 3)) for i in range(n)]
    share = 2 * width // (2 * blocks)
    part = width // 4
    own_rows = [jnp.where(core == a, bias[1:2, :], bias[0:1, :]) for a in range(2)]
    pad = lambda v: jnp.concatenate([v, jnp.zeros((1, width - v.shape[1]), F32)], 1)
    none = jnp.zeros((8, width), F32)
    for j in range(blocks):
        to = turned(j, near, blocks)
        for chunk in range(chunks):
            index = 2 * j + chunk // 2
            a, start = divmod(index * share, width)
            b, inner = divmod(start, 2 * part)
            p, offset = divmod(inner, part)
            own = own_rows[a][:, start : start + share]
            row = bias[2 + p : 3 + p, :]
            at = b * part + offset
            first, second = row[:, at : at + share], row[:, width // 2 + at : width // 2 + at + share]
            other = jnp.where(core == a, first, second)
            hidden = jnp.where(me == chunk % 2, own, other)
            begin = (j * chunks + chunk) * size
            tail = [pad(v[:, begin : begin + size]) for v in vectors] + [pad(hidden)]
            here = slice(begin, begin + size)
            with_vectors = jnp.concatenate([out_w[here], *tail], 0).astype(BF16)
            without = jnp.concatenate([value_w[here], none], 0).astype(BF16)
            mine[to, chunk] = jnp.where(core == 0, with_vectors, without)
            theirs[to, chunk] = jnp.where(core == 0, without, with_vectors)


def square_grads(at, blocks, mixed, grad_resid, h1, gv, *rest):
    width = mixed.shape[1]
    operands = (mixed, grad_resid, h1, gv, *rest[:3])
    shape = (blocks, 4, width // (4 * blocks) + 8, width)
    return pl.pallas_call(
        square_kernel,
        grid_spec=pltpu.PrefetchScalarGridSpec(
            num_scalar_prefetch=1,
            grid=(1,),
            in_specs=[whole(a.shape) for a in operands] + [ANYWHERE] * len(rest[3:]),
            out_specs=[whole(shape)] * 2,
        ),
        out_shape=[jax.ShapeDtypeStruct(shape, BF16), pltpu.HBM(shape, BF16)],
        compiler_params=pltpu.CompilerParams(vmem_limit_bytes=40 * MIB),
        cost_estimate=long_cost(4),
        name="square_grads",
    )(at, *in_hbm(operands), *rest[3:])


def last_kernel(count, rows_first, at_ref, *refs):
    keep, send = refs[-2:]
    core = at_ref[0]
    sum_of = refs[0][...].astype(F32)
    for part in refs[1:count]:
        sum_of = sum_of + part[...].astype(F32)
    half = keep.shape[-2]
    shape = keep.shape
    low = sum_of[..., :half, :].reshape(shape)
    high = sum_of[..., half:, :].reshape(shape)
    keep[...] = jnp.where(core == 0, low, high)
    send[...] = jnp.where(core == 0, high, low).astype(BF16)


def last_split(at, parts, dim, rows, shape, *tokens):
    block = parts[0].shape[:dim] + (rows,) + parts[0].shape[dim + 1 :]
    return pl.pallas_call(
        functools.partial(last_kernel, len(parts), dim),
        grid_spec=pltpu.PrefetchScalarGridSpec(
            num_scalar_prefetch=1,
            grid=(1,),
            in_specs=[whole(block)] * len(parts) + [ANYWHERE] * len(tokens),
            out_specs=[whole(shape)] * 2,
        ),
        out_shape=[jax.ShapeDtypeStruct(shape, F32), jax.ShapeDtypeStruct(shape, BF16)],
        compiler_params=pltpu.CompilerParams(vmem_limit_bytes=16 * MIB),
        cost_estimate=long_cost(0.3),
        name="last_split",
    )(at, *in_hbm(parts[:1]), *parts[1:], *tokens)


def hidden_last_kernel(count, at_ref, *refs):
    keep, send = refs[-2:]
    core = at_ref[0]
    arrived = refs[count]
    half = keep.shape[1]
    part = arrived.shape[3] // 2
    for which in range(2):
        sum_of = refs[0][which].astype(F32)
        for p in refs[1:count]:
            sum_of = sum_of + p[which].astype(F32)
        extra = [arrived[p, which].astype(F32)[:, b * part : (b + 1) * part] for b in range(2) for p in range(2)]
        sum_of = sum_of + jnp.concatenate(extra, 1)
        low, high = sum_of[:half], sum_of[half:]
        keep[which] = jnp.where(core == 0, low, high)
        send[which] = jnp.where(core == 0, high, low).astype(BF16)


def hidden_last(at, parts, arrived, rows, *tokens):
    _, _, width = parts[0].shape
    shape = (2, rows // 2, width)
    return pl.pallas_call(
        functools.partial(hidden_last_kernel, len(parts)),
        grid_spec=pltpu.PrefetchScalarGridSpec(
            num_scalar_prefetch=1,
            grid=(1,),
            in_specs=[whole((2, rows, width))] * len(parts) + [whole(arrived.shape)] + [ANYWHERE] * len(tokens),
            out_specs=[whole(shape)] * 2,
        ),
        out_shape=[jax.ShapeDtypeStruct(shape, F32), jax.ShapeDtypeStruct(shape, BF16)],
        compiler_params=pltpu.CompilerParams(vmem_limit_bytes=16 * MIB),
        cost_estimate=long_cost(0.3),
        name="hidden_last",
    )(at, *in_hbm(parts[:1]), *parts[1:], arrived, *tokens)


def hidden_out_kernel(at_ref, kept, got, up, down):
    core = at_ref[0]
    for which, out in ((0, up), (1, down)):
        mine, theirs = kept[which], got[which].astype(F32)
        both = jnp.concatenate([jnp.where(core == 0, mine, theirs), jnp.where(core == 0, theirs, mine)], 1)
        out[...] = both if which == 0 else both.T


def logit_out_kernel(at_ref, kept, got, out):
    core = at_ref[0]
    half = kept.shape[0]
    for head in range(half):
        mine, theirs = kept[head], got[head].astype(F32)
        out[head] = jnp.where(core == 0, mine, theirs).T
        out[half + head] = jnp.where(core == 0, theirs, mine).T


def square_out_kernel(at_ref, kept, got, out_w, value_w, up_bias, *vectors):
    core = at_ref[0]
    size = out_w.shape[0]
    mine, theirs = kept[...], got[...].astype(F32)
    first = jnp.where(core == 0, mine, theirs)
    second = jnp.where(core == 0, theirs, mine)
    out_w[...] = first[:size]
    value_w[...] = second[:size]
    for i, v in enumerate(vectors):
        v[...] = first[size + i : size + i + 1, :size]
    up_bias[...] = first[size + 7 : size + 8, : up_bias.shape[1]]


def finish(kernel, at, kept, got, shapes, *tokens):
    return pl.pallas_call(
        kernel,
        grid_spec=pltpu.PrefetchScalarGridSpec(
            num_scalar_prefetch=1,
            grid=(1,),
            in_specs=[whole(kept.shape), whole(got.shape)],
            out_specs=[whole(s) for s in shapes],
        ),
        out_shape=[pltpu.HBM(s, F32) for s in shapes],
        compiler_params=pltpu.CompilerParams(vmem_limit_bytes=16 * MIB),
        cost_estimate=long_cost(0.3),
        name="finish",
    )(at, kept, got)


def input_kernel(chained, x, grad_resid, gh_own, gh_received, small, *rest):
    grad = rest[1 if chained else 0]
    unit, scale = unit_rows(x[0].astype(F32))
    total = gh_own[0] + gh_received[0].astype(F32)
    grad[0] = grad_resid[0] + norm_back(total, unit, scale, small[0:1, :])


def input_rows(first, count, inputs, grad_resid, gh_own, gh_received, small, chain):
    rows, length, width = inputs.shape
    operands = [*in_hbm([inputs, grad_resid, gh_own]), gh_received, *in_hbm([small])]
    in_specs = [by_row(first, (length, width))] * 3 + [by_row(0, (length, width)), whole(small.shape)]
    aliases = {}
    if chain is not None:
        aliases = {len(operands): 0}
        operands += in_hbm([chain])
        in_specs.append(pl.BlockSpec(memory_space=pl.ANY))
    return pl.pallas_call(
        functools.partial(input_kernel, chain is not None),
        grid=(count,),
        in_specs=in_specs,
        out_specs=by_row(first, (length, width)),
        out_shape=pltpu.HBM((rows, length, width), F32),
        input_output_aliases=aliases,
        compiler_params=pltpu.CompilerParams(vmem_limit_bytes=24 * MIB),
        cost_estimate=long_cost(1),
        name="input_rows",
    )(*operands)


def swap(a, axis, size, bit):
    return lax.ppermute(a, axis, [(i, i ^ bit) for i in range(size)])


class Scatter:
    def __init__(self, mine, received, dim, size):
        self.parts = [mine, received]
        self.dim, self.size, self.rows, self.step = dim, size, mine.shape[dim], 1

    def send(self, *tokens):
        self.rows //= 2
        self.out = send_sum(self.parts, self.dim, self.rows, 1, *tokens)
        return self.out

    def receive(self):
        self.parts.append(swap(self.out, "dp", self.size, 1 << self.step))
        self.step += 1
        return self.parts[-1]


def paired_shards(
    dp,
    mp,
    inputs,
    segment_ids,
    ln1_gain,
    ln1_bias,
    value_weight,
    value_bias,
    random_logits,
    out_weight,
    out_bias,
    ln2_gain,
    ln2_bias,
    up_weight,
    up_bias,
    down_weight,
    down_bias,
    out_cotangent,
):
    rows, length, width = inputs.shape
    heads = random_logits.shape[0]
    full = segment_ids.shape[1]
    positions = rows * length
    hidden = up_weight.shape[1]
    tile = hidden // 2
    me = lax.axis_index("mp")
    place = lax.axis_index("dp")
    bits = dp.bit_length() - 1
    bit = [lax.rem(lax.div(place, 1 << b), 2) for b in range(bits)]
    core = bit[0]
    near = lax.shift_right_logical(place, 1)
    blocks = dp // 2
    at = jnp.stack([core, near, me]).astype(jnp.int32)
    offs = jnp.stack([me * length, (1 - me) * length, core, near]).astype(jnp.int32)
    quarter = (2 * core + bit[1]).reshape(1).astype(jnp.int32)
    by_core = lambda first, second: jnp.where(core == 0, first, second)
    small, up_row = prep(
        [ln1_gain, ln1_bias, ln2_gain, ln2_bias, value_bias, out_bias, down_bias], up_bias
    )

    received = [swap(inputs[r : r + 1], "mp", mp, 1) for r in range(rows)]
    expo = jnp.exp(random_logits.astype(F32)).astype(BF16)
    seg_row = segment_ids[:, None, :]
    g = out_cotangent.reshape(positions, width)

    chain = None
    for r in range(rows):
        chain = mix_rows(
            r,
            1,
            offs,
            blocks,
            inputs,
            received[r],
            out_cotangent,
            seg_row,
            expo,
            (value_weight, out_weight, small),
            chain,
        )
        if r == 1:
            early = chain[-1]
    h1, values, recip, mixed, resid, h2, h2t, gt, _ = chain
    h2 = h2.reshape(positions, width)
    h2t = h2t.reshape(width, positions)
    gt = gt.reshape(width, positions)

    fetched = []
    for packed in pack(quarter, up_weight, down_weight, up_row, early):
        by_x = swap(packed, "mp", mp, 1)
        by_y = swap(by_x, "dp", dp, 2)
        fetched.append((by_x, by_y, swap(by_x, "dp", dp, 1), swap(by_y, "dp", dp, 1)))

    fixed = (h2, g, h2t, gt)
    tiles = [(1 - core).reshape(1).astype(jnp.int32), core.reshape(1).astype(jnp.int32)]
    weights = (up_weight, up_row, down_weight)
    *sums, own_theirs, bias, _ = own_hidden(tiles[0], fixed, *weights, None)
    *sums, own_mine, bias, _ = own_hidden(tiles[1], fixed, *weights, (*sums, bias), fetched[0][0])
    own = Scatter(own_mine, swap(own_theirs, "dp", dp, 1), 1, dp)
    near_y = jnp.stack([bit[1], core]).astype(jnp.int32)
    *sums, mine, theirs, bias, token = other_hidden(
        0, near_y, fixed, fetched[0], (*sums, bias), None, fetched[1][0]
    )
    token = own.send(token)
    own.receive()
    out, dh, mine, theirs, bias, _ = other_hidden(1, near_y, fixed, fetched[1], (*sums, bias), (mine, theirs), token)
    other = Scatter(mine, swap(theirs, "dp", dp, 1), 2, dp)

    shape = (rows, length, width)
    layer_out, grad_resid, gm, vec_two = resid_rows(
        [out.reshape(shape), dh.reshape(shape), resid, out_cotangent, recip], (out_weight, small)
    )
    token = other.send(vec_two)
    other.receive()
    logits_theirs, logits_mine = logits_grad(offs, blocks, gm, mixed, values, seg_row, expo, token)
    logit = Scatter(logits_mine, swap(logits_theirs, "dp", dp, 1), 0, dp)
    token = own.send(logits_mine)
    own.receive()
    back = lambda pair, chain, token: back_rows(
        2 * pair, 2, offs, gm, inputs, received[2 * pair : 2 * pair + 2], seg_row, expo, value_weight, chain, token
    )
    chain = back(0, None, token)
    passed = [swap(chain[2], "mp", mp, 1)]
    token = logit.send(chain[2])
    logit.receive()
    chain = back(1, chain, token)
    passed.append(swap(chain[2], "mp", mp, 1))
    gv, gh_own, _, vec_one = chain
    token = own.send(chain[2])
    own.receive()

    square_theirs, square_mine = square_grads(
        at,
        blocks,
        mixed.reshape(positions, width),
        grad_resid.reshape(positions, width),
        h1.reshape(rows * full, width),
        gv.reshape(rows * full, width),
        bias,
        vec_two,
        vec_one,
        token,
    )

    square = Scatter(square_mine, swap(square_theirs, "dp", dp, 1), 0, dp)

    def step(scatter, token):
        token = scatter.send(token)
        scatter.receive()
        return token

    chain = None
    give_inputs = lambda pair, chain: input_rows(
        2 * pair, 2, inputs, grad_resid, gh_own, passed[pair], small, chain
    )
    token = step(other, square_mine)
    token = step(square, token)
    token = step(logit, token)
    chain = give_inputs(0, None)
    token = step(other, token)
    token = step(square, token)
    token = step(logit, token)
    token = step(square, token)
    chain = give_inputs(1, chain)
    sent = send_sum(other.parts, 2, other.rows, 0, token)
    arrived = swap(sent, "mp", mp, 1)
    by_partner = lambda m: [lax.dynamic_slice_in_dim(p[0].reshape((2, mp) + p.shape[2:]), m, 1, 1) for p in square.parts]
    sent = sum(p.astype(F32) for p in by_partner(1 - me)).astype(BF16)
    square_parts = by_partner(me) + [swap(sent, "mp", mp, 1)]
    chunk = square_mine.shape[2]
    square_parts = [p.reshape(2 * chunk, width) for p in square_parts]

    kept, sent = last_split(at, logit.parts, 0, 1, (heads // 2, full // dp, length))
    (logit_part,) = finish(
        logit_out_kernel, at, kept, swap(sent, "dp", dp, 1), [(heads, length, full // dp)]
    )
    kept, sent = hidden_last(at, own.parts, arrived, own.rows)
    up_part, down_part = finish(
        hidden_out_kernel, at, kept, swap(sent, "dp", dp, 1), [(width // dp, hidden), (hidden, width // dp)]
    )
    kept, sent = last_split(at, square_parts, 0, 2 * chunk, (chunk, width))
    share = width // (dp * mp)
    out_part, value_part, up_bias_part, *vector = finish(
        square_out_kernel,
        at,
        kept,
        swap(sent, "dp", dp, 1),
        [(share, width), (share, width), (1, hidden // dp)] + [(1, share)] * 7,
    )
    bo_part, g2_part, b2_part, bd_part, g1_part, b1_part, bv_part = (v.reshape(-1) for v in vector)
    return (
        layer_out,
        chain,
        g1_part,
        b1_part,
        value_part,
        bv_part,
        logit_part,
        out_part,
        bo_part,
        g2_part,
        b2_part,
        up_part,
        up_bias_part,
        down_part,
        bd_part,
    )


def smooth(t):
    return jax.nn.gelu(t, approximate=True)


def contract_rows(left, right):
    return lax.dot_general(
        left, right, (((0,), (0,)), ((), ())), preferred_element_type=jnp.float32
    )


def contract_cols(left, right):
    return lax.dot_general(
        left, right, (((1,), (1,)), ((), ())), preferred_element_type=jnp.float32
    )


def normalize(x, gain, shift):
    centred = x - jnp.mean(x, -1, keepdims=True)
    scale = lax.rsqrt(jnp.mean(centred * centred, -1, keepdims=True) + 1e-05)
    unit = centred * scale
    return (unit * gain + shift, unit, scale)


def normalize_back(grad, unit, scale, gain):
    scaled = grad * gain
    inner = scale * (
        scaled
        - jnp.mean(scaled, -1, keepdims=True)
        - unit * jnp.mean(scaled * unit, -1, keepdims=True)
    )
    return (inner, jnp.sum(grad * unit, 0), jnp.sum(grad, 0))


def shards(
    inputs,
    segment_ids,
    ln1_gain,
    ln1_bias,
    value_weight,
    value_bias,
    random_logits,
    out_weight,
    out_bias,
    ln2_gain,
    ln2_bias,
    up_weight,
    up_bias,
    down_weight,
    down_bias,
    out_cotangent,
):
    seqs, local_len, width = inputs.shape
    heads = random_logits.shape[0]
    full_len = segment_ids.shape[1]
    head_dim = width // heads
    rows = seqs * local_len
    gain_one = ln1_gain.astype(jnp.float32)
    gain_two = ln2_gain.astype(jnp.float32)
    start_x = inputs.astype(jnp.float32).reshape(rows, width)
    normed_one, unit_one, scale_one = normalize(start_x, gain_one, ln1_bias.astype(jnp.float32))
    h1_low = normed_one.astype(jnp.bfloat16)
    values = (
        jnp.dot(h1_low, value_weight, preferred_element_type=jnp.float32)
        + value_bias.astype(jnp.float32)
    ).astype(jnp.bfloat16)
    gathered = lax.all_gather(values.reshape(seqs, local_len, width), "mp", axis=1, tiled=True)
    every_head = gathered.reshape(seqs, full_len, heads, head_dim)
    offset = lax.axis_index("mp") * local_len
    own_segs = lax.dynamic_slice_in_dim(segment_ids, offset, local_len, 1)
    same = own_segs[:, :, None] == segment_ids[:, None, :]
    scores = jnp.where(same[:, None], random_logits.astype(jnp.float32)[None], -1e30)
    peak = jnp.max(scores, -1, keepdims=True)
    expo = jnp.exp(scores - peak)
    total = jnp.sum(expo, -1, keepdims=True)
    probs = expo / total
    probs_low = probs.astype(jnp.bfloat16)
    mixed = jnp.einsum("shqk,skhd->sqhd", probs_low, every_head, preferred_element_type=jnp.float32)
    mixed_low = mixed.reshape(rows, width).astype(jnp.bfloat16)
    resid = (
        start_x
        + jnp.dot(mixed_low, out_weight, preferred_element_type=jnp.float32)
        + out_bias.astype(jnp.float32)
    )
    normed_two, unit_two, scale_two = normalize(resid, gain_two, ln2_bias.astype(jnp.float32))
    h2_low = normed_two.astype(jnp.bfloat16)
    grad_low = out_cotangent.reshape(rows, width)
    h2_full = lax.all_gather(
        h2_low.reshape(seqs, local_len, width), "mp", axis=1, tiled=True
    ).reshape(seqs * full_len, width)
    pre = jnp.dot(h2_full, up_weight, preferred_element_type=jnp.float32) + up_bias.astype(
        jnp.float32
    )
    act, gelu_pull = jax.vjp(smooth, pre)
    act_low = act.astype(jnp.bfloat16)
    partial_out = jnp.dot(act_low, down_weight, preferred_element_type=jnp.float32).reshape(
        seqs, full_len, width
    )
    ffn_out = lax.psum_scatter(
        partial_out.astype(jnp.bfloat16), "mp", scatter_dimension=1, tiled=True
    ).astype(jnp.float32).reshape(rows, width) + down_bias.astype(jnp.float32)
    final = resid + ffn_out
    grad_full = lax.all_gather(out_cotangent, "mp", axis=1, tiled=True).reshape(
        seqs * full_len, width
    )
    grad_down = contract_rows(act_low, grad_full)
    grad_act = contract_cols(grad_full, down_weight)
    grad_pre = gelu_pull(grad_act)[0].astype(jnp.bfloat16)
    grad_up_b = jnp.sum(grad_pre.astype(jnp.float32), 0)
    grad_up = contract_rows(h2_full, grad_pre)
    h2_terms = contract_cols(grad_pre, up_weight).reshape(seqs, full_len, width)
    grad_h2 = (
        lax.psum_scatter(h2_terms.astype(jnp.bfloat16), "mp", scatter_dimension=1, tiled=True)
        .astype(jnp.float32)
        .reshape(rows, width)
    )
    grad_final = grad_low.astype(jnp.float32)
    grad_down_b = jnp.sum(grad_final, 0)
    inner_two, gain_two_grad, shift_two_grad = normalize_back(
        grad_h2, unit_two, scale_two, gain_two
    )
    grad_resid = grad_final + inner_two
    grad_o_low = grad_resid.astype(jnp.bfloat16)
    grad_out_b = jnp.sum(grad_o_low.astype(jnp.float32), 0)
    grad_out_w = contract_rows(mixed_low, grad_o_low)
    grad_mixed = (
        contract_cols(grad_o_low, out_weight)
        .astype(jnp.bfloat16)
        .reshape(seqs, local_len, heads, head_dim)
    )
    grad_probs = jnp.einsum(
        "sqhd,skhd->shqk", grad_mixed, every_head, preferred_element_type=jnp.float32
    )
    grad_scores = probs * (grad_probs - jnp.sum(probs * grad_probs, -1, keepdims=True))
    grad_logits = jnp.sum(grad_scores, 0)
    value_terms = jnp.einsum(
        "shqk,sqhd->skhd", probs_low, grad_mixed, preferred_element_type=jnp.float32
    ).reshape(seqs, full_len, width)
    grad_values = (
        lax.psum_scatter(value_terms.astype(jnp.bfloat16), "mp", scatter_dimension=1, tiled=True)
        .astype(jnp.float32)
        .reshape(rows, width)
        .astype(jnp.bfloat16)
    )
    grad_value_b = jnp.sum(grad_values.astype(jnp.float32), 0)
    grad_value_w = contract_rows(h1_low, grad_values)
    inner_one, gain_one_grad, shift_one_grad = normalize_back(
        contract_cols(grad_values, value_weight), unit_one, scale_one, gain_one
    )
    grad_x = (grad_resid + inner_one).reshape(seqs, local_len, width)
    vectors = jnp.stack(
        [
            gain_one_grad,
            shift_one_grad,
            grad_value_b,
            grad_out_b,
            gain_two_grad,
            shift_two_grad,
            grad_down_b,
        ]
    )
    value_w_part, out_w_part, vector_part = (
        lax.psum_scatter(grad_value_w, ("dp", "mp"), scatter_dimension=0, tiled=True),
        lax.psum_scatter(grad_out_w, ("dp", "mp"), scatter_dimension=0, tiled=True),
        lax.psum_scatter(vectors, ("dp", "mp"), scatter_dimension=1, tiled=True),
    )
    up_part, up_b_part, down_part, logit_part = (
        lax.psum_scatter(
            grad_up.astype(jnp.bfloat16), "dp", scatter_dimension=0, tiled=True
        ).astype(jnp.float32),
        lax.psum_scatter(
            grad_up_b[None].astype(jnp.bfloat16), "dp", scatter_dimension=1, tiled=True
        ).astype(jnp.float32),
        lax.psum_scatter(
            grad_down.astype(jnp.bfloat16), "dp", scatter_dimension=1, tiled=True
        ).astype(jnp.float32),
        lax.psum_scatter(
            grad_logits.astype(jnp.bfloat16), "dp", scatter_dimension=2, tiled=True
        ).astype(jnp.float32),
    )
    return (
        final.astype(jnp.bfloat16).reshape(seqs, local_len, width),
        grad_x,
        vector_part[0],
        vector_part[1],
        value_w_part,
        vector_part[2],
        logit_part,
        out_w_part,
        vector_part[3],
        vector_part[4],
        vector_part[5],
        up_part,
        up_b_part,
        down_part,
        vector_part[6],
    )


def solution(mesh):
    in_specs = (
        P("dp", "mp", None),
        P("dp", None),
        P(),
        P(),
        P(),
        P(),
        P(None, "mp", None),
        P(),
        P(),
        P(),
        P(),
        P(None, "mp"),
        P("mp"),
        P("mp", None),
        P(),
        P("dp", "mp", None),
    )
    out_specs = (
        P("dp", "mp", None),
        P("dp", "mp", None),
        P(("dp", "mp")),
        P(("dp", "mp")),
        P(("dp", "mp"), None),
        P(("dp", "mp")),
        P(None, "mp", "dp"),
        P(("dp", "mp"), None),
        P(("dp", "mp")),
        P(("dp", "mp")),
        P(("dp", "mp")),
        P("dp", "mp"),
        P("mp", "dp"),
        P("mp", "dp"),
        P(("dp", "mp")),
    )
    dp, mp = mesh.shape["dp"], mesh.shape["mp"]
    body = functools.partial(paired_shards, dp, mp) if mp == 2 else shards
    return jax.shard_map(body, mesh=mesh, in_specs=in_specs, out_specs=out_specs, check_vma=False)
```

```python
import functools

import jax
import jax.numpy as jnp
from jax import lax
from jax.experimental import pallas as pl
from jax.experimental.pallas import tpu as pltpu
from jax.sharding import PartitionSpec as P

F32 = jnp.float32
BF16 = jnp.bfloat16
GELU_A = 0.7978845608028654
GELU_B = GELU_A * 0.044715
MIB = 2**20


def mm(left, right, left_dim, right_dim):
    return lax.dot_general(
        left, right, (((left_dim,), (right_dim,)), ((), ())), preferred_element_type=F32
    )


def unit_rows(x):
    centred = x - jnp.mean(x, -1, keepdims=True)
    scale = lax.rsqrt(jnp.mean(centred * centred, -1, keepdims=True) + 1e-05)
    return centred * scale, scale


def norm_back(grad, unit, scale, gain):
    e = grad * gain
    return scale * (
        e - jnp.mean(e, -1, keepdims=True) - unit * jnp.mean(e * unit, -1, keepdims=True)
    )


def same_document(first, seg_row, row, length):
    keys = seg_row[row].astype(F32)
    own = seg_row[row, :, pl.ds(pl.multiple_of(first, length), length)].astype(F32)
    queries = jnp.broadcast_to(own, (8, length)).T[:, :1]
    return jnp.where(queries == keys, 1.0, 0.0)


def turned(block, near, blocks):
    other = jnp.bitwise_xor(block, near)
    place = 0
    weight = blocks
    for b in range(blocks.bit_length() - 1):
        weight //= 2
        place = place + jnp.bitwise_and(lax.shift_right_logical(other, b), 1) * weight
    return place


def long_cost(us):
    return pl.CostEstimate(flops=int(us * 10**10), bytes_accessed=10**5, transcendentals=0)


IN_VMEM = pl.BlockSpec(memory_space=pltpu.VMEM)
ANYWHERE = pl.BlockSpec(memory_space=pl.ANY)


def in_hbm(operands):
    return [pltpu.with_memory_space_constraint(a, pltpu.HBM) for a in operands]


def in_vmem(operands):
    return [pltpu.with_memory_space_constraint(a, pltpu.VMEM) for a in operands]


TOKEN = pltpu.HBM((8, 128), F32)


def whole(shape):
    return pl.BlockSpec(shape, lambda i, *_: (0,) * len(shape))


def by_row(first, shape):
    return pl.BlockSpec((1,) + shape, lambda i, *_: (first + i,) + (0,) * len(shape))


def prep_kernel(*refs):
    *vectors, bias, small, hidden = refs
    for i, v in enumerate(vectors):
        small[i : i + 1, :] = v[...].astype(F32).reshape(1, -1)
    hidden[...] = bias[...].astype(F32).reshape(1, -1)


def prep(vectors, bias):
    return pl.pallas_call(
        prep_kernel,
        in_specs=[IN_VMEM] * (len(vectors) + 1),
        out_specs=[IN_VMEM] * 2,
        out_shape=[
            pltpu.HBM((8, vectors[0].shape[0]), F32),
            pltpu.HBM((1, bias.shape[0]), F32),
        ],
        name="prep",
    )(*vectors, bias)


def mix_kernel(offs, x_own, x_other, g, seg_row, expo, wv, wo, small, *rest):
    h1, values, recip, mixed, resid, h2, h2t, gt, token, ones = rest[-10:]
    g1, b1, g2, b2, bv, bo, _ = (small[i : i + 1, :] for i in range(7))
    token[...] = jnp.zeros_like(token)
    length = x_own.shape[1]
    heads = expo.shape[0]
    ones[:, 128:] = jnp.ones_like(ones[:, 128:])
    x = x_own[0].astype(F32)
    for block, off in ((x, offs[0]), (x_other[0].astype(F32), offs[1])):
        unit, _ = unit_rows(block)
        at = pl.ds(pl.multiple_of(off, length), length)
        h1[0, at, :] = (unit * g1 + b1).astype(BF16)
    values[0] = (mm(h1[0], wv[...], 1, 0) + bv).astype(BF16)
    mask = same_document(offs[0], seg_row, 0, length).astype(BF16)
    low_lane = lax.broadcasted_iota(jnp.int32, (length, 128), 1) < 64
    for pair in range(heads // 2):
        lanes = slice(128 * pair, 128 * pair + 128)
        ones[:, :128] = values[0, :, lanes]
        first = mm(expo[2 * pair] * mask, ones[...], 1, 0)
        second = mm(expo[2 * pair + 1] * mask, ones[...], 1, 0)
        inverse = 1.0 / jnp.where(low_lane, first[:, 128:], second[:, 128:])
        recip[0, :, lanes] = inverse
        mixed[0, :, lanes] = jnp.where(low_lane, first[:, :128], second[:, :128]) * inverse
    r = x + mm(mixed[0].astype(BF16), wo[...], 1, 0) + bo
    resid[0] = r
    unit, _ = unit_rows(r)
    low = (unit * g2 + b2).astype(BF16)
    h2[0] = low
    blocks, size, _ = h2t.shape
    for ref, source in ((h2t, low.T), (gt, g[0].T)):
        for j in range(blocks):
            ref[turned(j, offs[3], blocks)] = source[j * size : (j + 1) * size, :]


def mix_rows(first, count, offs, blocks, inputs, received, cotangent, seg_row, expo, weights, chain, *tokens):
    rows, length, width = inputs.shape
    full = seg_row.shape[2]
    heads = expo.shape[0]
    shapes = [
        ((full, width), BF16),
        ((full, width), BF16),
        ((length, width), F32),
        ((length, width), F32),
        ((length, width), F32),
        ((length, width), BF16),
    ]
    out_specs = [by_row(first, s) for s, _ in shapes]
    turned_spec = pl.BlockSpec((blocks, width // blocks, length), lambda i, *_: (0, 0, first + i))
    out_specs += [turned_spec] * 2
    out_shape = [pltpu.HBM((rows,) + s, t) for s, t in shapes[:5]]
    out_shape += [pltpu.VMEM((rows,) + s, t) for s, t in shapes[5:]]
    out_shape += [pltpu.VMEM((blocks, width // blocks, rows * length), BF16)] * 2
    operands = [offs, *in_hbm([inputs]), received, *in_hbm([cotangent, seg_row]), *in_vmem([expo, *weights])]
    in_specs = [
        by_row(first, (length, width)),
        by_row(0, (length, width)),
        by_row(first, (length, width)),
        by_row(first, (1, full)),
        *[IN_VMEM] * (1 + len(weights)),
    ]
    aliases = {}
    if chain is not None:
        aliases = {len(operands) + i: i for i in range(len(out_shape))}
        operands += [*in_hbm(chain[:5]), *in_vmem(chain[5:8])]
        in_specs += [ANYWHERE] * len(out_shape)
    operands += tokens
    in_specs += [ANYWHERE] * len(tokens)
    out_specs.append(whole((8, 128)))
    out_shape.append(TOKEN)
    return pl.pallas_call(
        mix_kernel,
        grid_spec=pltpu.PrefetchScalarGridSpec(
            num_scalar_prefetch=1,
            grid=(count,),
            in_specs=in_specs,
            out_specs=out_specs,
            scratch_shapes=[pltpu.VMEM((full, 256), BF16)],
        ),
        out_shape=out_shape,
        input_output_aliases=aliases,
        compiler_params=pltpu.CompilerParams(vmem_limit_bytes=32 * MIB),
        cost_estimate=long_cost(3 * count),
        name="mix_rows",
    )(*operands)


def gelu_pair(t):
    square = t * t
    curve = jnp.tanh(t * (GELU_A + GELU_B * square))
    half = 0.5 + 0.5 * curve
    act = t * half
    return act, half + act * (1.0 - curve) * (GELU_A + 3 * GELU_B * square)


def hidden_tile(h2, g, h2t, gt, wu, up_dim, bu, wd, sums, outs, act_s, pre_s, block):
    out0, dh0 = sums if sums else (None, None)
    out, dh = outs
    total = None
    for m in range(h2.shape[0] // block):
        at = pl.ds(m * block, block)
        pre = mm(h2[at, :], wu[...], 1, up_dim) + bu
        grad_act = mm(g[at, :], wd[...], 1, 1)
        act, slope = gelu_pair(pre)
        act_low = act.astype(BF16)
        grad_pre = grad_act * slope
        part = jnp.sum(grad_pre, 0, keepdims=True)
        total = part if total is None else total + part
        pre_low = grad_pre.astype(BF16)
        act_s[at, :] = act_low
        pre_s[at, :] = pre_low
        out_part = mm(act_low, wd[...], 1, 0)
        dh_part = mm(pre_low, wu[...], 1, 1 - up_dim)
        out[at, :] = out_part if sums is None else out0[at, :] + out_part
        dh[at, :] = dh_part if sums is None else dh0[at, :] + dh_part
    return total, lambda: (
        mm(h2t[...], pre_s[...], 1, 0).astype(BF16),
        mm(gt[...], act_s[...], 1, 0).astype(BF16),
    )


def own_hidden_kernel(block, first, at_ref, h2, g, h2t, gt, wu, bu, wd, *rest):
    out, dh, grads, bias, token, act_s, pre_s = rest[-7:]
    token[...] = jnp.zeros_like(token)
    sums = None
    if not first:
        out0, dh0, bias0 = rest[:3]
        sums = (out0, dh0)
    total, weights = hidden_tile(
        h2, g, h2t, gt, wu, 0, bu[...].astype(F32), wd, sums, (out, dh), act_s, pre_s, block
    )
    if first:
        bias[0:1, :] = total
    else:
        bias[...] = bias0[...]
        bias[1:2, :] = total
    half = grads.shape[3]
    for which, grad in enumerate(weights()):
        for p in range(2):
            grads[p, which] = grad[:, p * half : (p + 1) * half]


def other_hidden_kernel(block, which, near, h2, g, h2t, gt, wx, wy, wcx, wcy, out0, dh0, bias0, *rest):
    out, dh, mine, theirs, bias, token, wu, wd, act_s, pre_s = rest[-10:]
    token[...] = jnp.zeros_like(token)
    near_y = near[0]
    part = wx.shape[0] // 2 - 8
    for first, pieces in ((0, (wx, wy)), (2, (wcx, wcy))):
        for turn, piece in enumerate(pieces):
            quarter = first + jnp.bitwise_xor(near_y, turn)
            at = pl.ds(pl.multiple_of(quarter * part, part), part)
            wu[at, :] = piece[:part, :]
            wd[at, :] = piece[part : 2 * part, :]
    rows = wx[2 * part :, :].astype(F32)
    lanes = slice(2 * part * which, 2 * part * (which + 1))
    lower, upper = rows[0:1, lanes], rows[1:2, lanes]
    swapped = near[1] == 1
    bu = jnp.concatenate([jnp.where(swapped, upper, lower), jnp.where(swapped, lower, upper)], axis=1)
    total, weights = hidden_tile(
        h2, g, h2t, gt, wu, 1, bu, wd, (out0, dh0), (out, dh), act_s, pre_s, block
    )
    bias[...] = bias0[...]
    bias[2 + which : 3 + which, :] = total
    half = 2 * part
    for index, grad in enumerate(weights()):
        mine[index] = grad[:, :half]
        theirs[index] = grad[:, half:]


def hidden_call(positions, width, tile):
    return dict(
        compiler_params=pltpu.CompilerParams(vmem_limit_bytes=30 * MIB),
        cost_estimate=long_cost(5),
    )


def own_hidden(tile_at, fixed, wu, bu, wd, sums, *tokens):
    positions, width = fixed[0].shape
    tile = wu.shape[1] // 2
    operands = [*in_vmem(fixed), *in_hbm([wu, bu, wd]), *in_vmem(sums or ()), *tokens]
    aliases = {1 + len(fixed) + 3: 0, 1 + len(fixed) + 4: 1} if sums else {}
    weights = [
        pl.BlockSpec((width, tile), lambda i, at: (0, at[0])),
        pl.BlockSpec((1, tile), lambda i, at: (0, at[0])),
        pl.BlockSpec((tile, width), lambda i, at: (at[0], 0)),
    ]
    return pl.pallas_call(
        functools.partial(own_hidden_kernel, 256, sums is None),
        grid_spec=pltpu.PrefetchScalarGridSpec(
            num_scalar_prefetch=1,
            grid=(1,),
            in_specs=[IN_VMEM] * len(fixed) + weights + [IN_VMEM] * len(sums or ()) + [ANYWHERE] * len(tokens),
            out_specs=[IN_VMEM] * 2 + [whole((2, 2, width, tile // 2)), IN_VMEM, whole((8, 128))],
            scratch_shapes=[pltpu.VMEM((positions, tile), BF16)] * 2,
        ),
        out_shape=[pltpu.VMEM((positions, width), F32)] * 2
        + [pltpu.HBM((2, 2, width, tile // 2), BF16), pltpu.VMEM((8, tile), F32), TOKEN],
        input_output_aliases=aliases,
        name="own_hidden",
        **hidden_call(positions, width, tile),
    )(tile_at, *operands)


def other_hidden(which, near, fixed, pieces, sums, *tokens):
    positions, width = fixed[0].shape
    tile = 4 * (pieces[0].shape[0] // 2 - 8)
    operands = [*in_vmem(fixed), *pieces, *in_vmem(sums)]
    aliases = {1 + len(operands) - 3: 0, 1 + len(operands) - 2: 1}
    block = whole((2, width, tile // 2))
    return pl.pallas_call(
        functools.partial(other_hidden_kernel, 256, which),
        grid_spec=pltpu.PrefetchScalarGridSpec(
            num_scalar_prefetch=1,
            grid=(1,),
            in_specs=[IN_VMEM] * 4 + [whole(p.shape) for p in pieces] + [IN_VMEM] * 3 + [ANYWHERE] * len(tokens),
            out_specs=[IN_VMEM] * 2 + [block] * 2 + [IN_VMEM, whole((8, 128))],
            scratch_shapes=[pltpu.VMEM((tile, width), BF16)] * 2 + [pltpu.VMEM((positions, tile), BF16)] * 2,
        ),
        out_shape=[pltpu.VMEM((positions, width), F32)] * 2
        + [make((2, width, tile // 2), BF16) for make in (pltpu.HBM, jax.ShapeDtypeStruct)]
        + [pltpu.VMEM((8, tile), F32), TOKEN],
        input_output_aliases=aliases,
        name="other_hidden",
        **hidden_call(positions, width, tile),
    )(near, *operands, *tokens)


def pack_kernel(at, up, down, bias, token, out):
    size = up.shape[1] // 2
    width = down.shape[1]
    start = pl.multiple_of(at[2] * size, size)
    out[:size, :] = jnp.where(at[2] == 0, up[:, :size].T, up[:, size:].T)
    out[size : 2 * size, :] = down[pl.ds(start, size), :]
    both = jnp.concatenate([bias[:, :width], bias[:, width:], jnp.zeros((14, width), F32)], 0)
    out[2 * size :, :] = both.astype(BF16)


def pack(which, at, up, down, bias, token):
    width, hidden = up.shape
    part = hidden // 4
    return pl.pallas_call(
        pack_kernel,
        grid_spec=pltpu.PrefetchScalarGridSpec(
            num_scalar_prefetch=1,
            grid=(1,),
            in_specs=[
                pl.BlockSpec((width, part), lambda i, at: (0, at[which])),
                pl.BlockSpec((part, width), lambda i, at: (at[which], 0)),
                whole(bias.shape),
                ANYWHERE,
            ],
            out_specs=whole((part + 16, width)),
        ),
        out_shape=jax.ShapeDtypeStruct((part + 16, width), BF16),
        compiler_params=pltpu.CompilerParams(vmem_limit_bytes=16 * MIB),
        cost_estimate=long_cost(0.5),
        name="pack",
    )(at, *in_hbm([up, down, bias, token]))


def resid_kernel(out_acc, dh, resid, g, recip, wo, small, *rest):
    layer_out, grad_resid, grad_out, gm, vec = rest[-5:]
    g2, bd = small[2:3, :], small[6:7, :]
    r = resid[0]
    layer_out[0] = (r + out_acc[0] + bd).astype(BF16)
    unit, scale = unit_rows(r)
    grad = dh[0]
    cot = g[0].astype(F32)
    total = cot + norm_back(grad, unit, scale, g2)
    grad_resid[0] = total
    grad_o = total.astype(BF16)
    grad_out[0] = grad_o
    vec[0, 0:1, :] = jnp.sum(grad_o.astype(F32), 0, keepdims=True)
    vec[0, 1:2, :] = jnp.sum(grad * unit, 0, keepdims=True)
    vec[0, 2:3, :] = jnp.sum(grad, 0, keepdims=True)
    vec[0, 3:4, :] = jnp.sum(cot, 0, keepdims=True)
    gm[0] = (mm(grad_o, wo[...], 1, 1).astype(BF16).astype(F32) * recip[0]).astype(BF16)


def resid_rows(row_arrays, weights, *tokens):
    rows, length, width = row_arrays[0].shape
    low = ((length, width), BF16)
    shapes = [low, ((length, width), F32), low, low, ((4, width), F32)]
    return pl.pallas_call(
        resid_kernel,
        grid=(rows,),
        in_specs=[by_row(0, (length, width)) for _ in row_arrays]
        + [whole(w.shape) for w in weights]
        + [ANYWHERE] * len(tokens),
        out_specs=[by_row(0, s) for s, _ in shapes],
        out_shape=[pltpu.HBM((rows,) + s, t) for s, t in shapes],
        compiler_params=pltpu.CompilerParams(vmem_limit_bytes=24 * MIB),
        cost_estimate=long_cost(3),
        name="resid_rows",
    )(*in_vmem(row_arrays[:2]), *in_hbm([*row_arrays[2:], *weights, *tokens]))


def back_kernel(offs, gm, x_own, x_first, x_second, seg_row, expo, wv, *rest):
    gv, gh_own, gh_send, vec_one, gmt, gvt, gh = rest[-7:]
    length = x_own.shape[1]
    heads = expo.shape[0]
    gmt[...] = gm[0].T
    mask = same_document(offs[0], seg_row, 0, length).astype(BF16)
    for head in range(heads):
        at = slice(64 * head, 64 * head + 64)
        gvt[at, :] = mm(gmt[at, :], expo[head] * mask, 1, 0).astype(BF16)
    values_grad = gvt[...].T
    gv[0] = values_grad
    gh[...] = mm(values_grad, wv[...], 1, 1)
    gain = jnp.zeros((1, gh.shape[1]), F32)
    x_other = jnp.where(pl.program_id(0) == 0, x_first[0], x_second[0])
    for block, off in ((x_own[0], offs[0]), (x_other, offs[1])):
        unit, _ = unit_rows(block.astype(F32))
        gain += jnp.sum(gh[pl.ds(pl.multiple_of(off, length), length), :] * unit, 0, keepdims=True)
    vec_one[0, 0:1, :] = gain
    vec_one[0, 1:2, :] = jnp.sum(gh[...], 0, keepdims=True)
    vec_one[0, 2:3, :] = jnp.sum(values_grad.astype(F32), 0, keepdims=True)
    gh_own[0] = gh[pl.ds(pl.multiple_of(offs[0], length), length), :]
    gh_send[0] = gh[pl.ds(pl.multiple_of(offs[1], length), length), :].astype(BF16)


def back_rows(first, count, cost, offs, gm, inputs, received, seg_row, expo, wv, chain, *tokens):
    rows, length, width = inputs.shape
    full = seg_row.shape[2]
    shapes = [((full, width), BF16), ((length, width), F32), ((length, width), BF16), ((3, width), F32)]
    out_specs = [by_row(0 if i == 2 else first, s) for i, (s, _) in enumerate(shapes)]
    out_shape = [
        jax.ShapeDtypeStruct((count,) + s, t) if i == 2 else pltpu.HBM((rows,) + s, t)
        for i, (s, t) in enumerate(shapes)
    ]
    operands = [offs, *in_hbm([gm, inputs]), *received, *in_hbm([seg_row]), *in_vmem([expo, wv])]
    in_specs = [by_row(first, (length, width))] * 2
    in_specs += [
        whole((1, length, width)),
        whole((1, length, width)),
        by_row(first, (1, full)),
        IN_VMEM,
        IN_VMEM,
    ]
    aliases = {}
    if chain is not None:
        aliases = {len(operands) + i: i for i in range(len(out_shape)) if i != 2}
        operands += [*in_hbm(chain[:2]), chain[2], *in_hbm(chain[3:])]
        in_specs += [ANYWHERE] * len(out_shape)
    operands += tokens
    in_specs += [ANYWHERE] * len(tokens)
    return pl.pallas_call(
        back_kernel,
        grid_spec=pltpu.PrefetchScalarGridSpec(
            num_scalar_prefetch=1,
            grid=(count,),
            in_specs=in_specs,
            out_specs=out_specs,
            scratch_shapes=[
                pltpu.VMEM((width, length), BF16),
                pltpu.VMEM((width, full), BF16),
                pltpu.VMEM((full, width), F32),
            ],
        ),
        out_shape=out_shape,
        input_output_aliases=aliases,
        compiler_params=pltpu.CompilerParams(vmem_limit_bytes=32 * MIB),
        cost_estimate=long_cost(cost),
        name="back_rows",
    )(*operands)


def send_kernel(counts, *refs):
    out = refs[-1]
    start = 0
    for i, count in enumerate(counts):
        sum_of = refs[start][...].astype(F32)
        for part in refs[start + 1 : start + count]:
            sum_of = sum_of + part[...].astype(F32)
        start += count
        if len(counts) == 1:
            out[...] = sum_of.astype(BF16)
        else:
            out[i] = sum_of.astype(BF16)


def part_spec(part, dim, size, index):
    array, lead = part
    shape = array.shape if lead is None else array.shape[1:]
    shape = shape[:dim] + (size,) + shape[dim + 1 :]
    place = tuple(index if d == dim else 0 for d in range(len(shape)))
    if lead is None:
        return pl.BlockSpec(shape, lambda i, *_: place), shape
    return pl.BlockSpec((None,) + shape, lambda i, *_: (lead,) + place), shape


def send_sum(groups, dim, size, index, *tokens):
    parts = [p for group in groups for p in group]
    specs = [part_spec(p, dim, size, index) for p in parts]
    shape = specs[0][1]
    if len(groups) > 1:
        shape = (len(groups),) + shape
    return pl.pallas_call(
        functools.partial(send_kernel, [len(group) for group in groups]),
        grid=(1,),
        in_specs=[spec for spec, _ in specs] + [ANYWHERE] * len(tokens),
        out_specs=whole(shape),
        out_shape=jax.ShapeDtypeStruct(shape, BF16),
        compiler_params=pltpu.CompilerParams(vmem_limit_bytes=16 * MIB),
        cost_estimate=long_cost(0.2),
        name="send_sum",
    )(*[p for p, _ in parts], *tokens)


def logits_kernel(offs, gm, mixed, values, seg_row, expo, *rest):
    out, ones, masks = rest[-3:]
    step = pl.program_id(0)
    rows, length = gm.shape[:2]

    @pl.when(step == 0)
    def _():
        ones[:, 128:] = jnp.ones_like(ones[:, 128:])
        for row in range(rows):
            masks[row] = same_document(offs[0], seg_row, row, length)

    low_lane = lax.broadcasted_iota(jnp.int32, (length, 128), 1) < 64
    zero = jnp.zeros((length, 128), F32)
    sums = [None, None]
    for row in range(rows):
        ones[:, :128] = values[row]
        scaled = gm[row].astype(F32)
        product = scaled * mixed[row]
        high = product.astype(BF16).astype(F32)
        rest = product - high
        turned_rest = pltpu.roll(rest, 64, 1)
        left = []
        for head in range(2):
            keep = low_lane if head == 0 else jnp.logical_not(low_lane)
            left.append(
                jnp.concatenate(
                    [
                        jnp.where(keep, scaled, zero).astype(BF16),
                        (-jnp.where(keep, high, turned_rest)).astype(BF16),
                    ],
                    axis=1,
                )
            )
        both = mm(jnp.concatenate(left, 0), ones[...], 1, 1)
        for head in range(2):
            part = both[head * length : (head + 1) * length] * masks[row]
            sums[head] = part if sums[head] is None else sums[head] + part
    for head in range(2):
        grad = (expo[head].astype(F32) * sums[head]).astype(BF16).T
        blocks, _, size, _ = out.shape
        for j in range(blocks):
            out[turned(j, offs[3], blocks), head] = grad[j * size : (j + 1) * size, :]


def logits_grad(mine, offs, blocks, gm, mixed, values, seg_row, expo, *tokens):
    rows, length, width = gm.shape
    heads, _, full = expo.shape
    half = heads // 4
    pick = lambda i, offs: i + half * (offs[2] if mine else 1 - offs[2])
    shape = (blocks, heads // 2, full // blocks, length)
    return pl.pallas_call(
        logits_kernel,
        grid_spec=pltpu.PrefetchScalarGridSpec(
            num_scalar_prefetch=1,
            grid=(half,),
            in_specs=[
                pl.BlockSpec((rows, length, 128), lambda i, offs: (0, 0, pick(i, offs))),
                pl.BlockSpec((rows, length, 128), lambda i, offs: (0, 0, pick(i, offs))),
                pl.BlockSpec((rows, full, 128), lambda i, offs: (0, 0, pick(i, offs))),
                whole(seg_row.shape),
                pl.BlockSpec((2, length, full), lambda i, offs: (pick(i, offs), 0, 0)),
            ]
            + [ANYWHERE] * len(tokens),
            out_specs=pl.BlockSpec((blocks, 2, full // blocks, length), lambda i, offs: (0, i, 0, 0)),
            scratch_shapes=[pltpu.VMEM((full, 256), BF16), pltpu.VMEM((rows, length, full), F32)],
        ),
        out_shape=pltpu.HBM(shape, BF16) if mine else jax.ShapeDtypeStruct(shape, BF16),
        compiler_params=pltpu.CompilerParams(vmem_limit_bytes=32 * MIB),
        cost_estimate=long_cost(3),
        name="logits_grad",
    )(offs, *in_hbm([gm, mixed, values, seg_row, expo]), *tokens)


def square_kernel(at_ref, mixed, grad_o, h1, gv, bias, vec_two, vec_one, *rest):
    theirs, mine, out_sum, value_sum = rest[-4:]
    step = pl.program_id(0)
    out_part = mm(mixed[0].astype(BF16), grad_o[0], 0, 0)
    value_part = mm(h1[0], gv[0], 0, 0)

    @pl.when(step == 0)
    def _():
        out_sum[...] = out_part
        value_sum[...] = value_part

    @pl.when(step > 0)
    def _():
        out_sum[...] += out_part
        value_sum[...] += value_part

    @pl.when(step == pl.num_programs(0) - 1)
    def _():
        square_store(at_ref, out_sum, value_sum, bias, vec_two, vec_one, theirs, mine)


def square_store(at_ref, out_w, value_w, bias, vec_two, vec_one, theirs, mine):
    width = out_w.shape[1]
    rows = vec_two.shape[0]
    core, near, me = at_ref[0], at_ref[1], at_ref[2]
    blocks, chunks, size, _ = mine.shape
    size -= 8
    vectors = [sum(ref[r, i : i + 1, :] for r in range(rows)) for ref, n in ((vec_two, 4), (vec_one, 3)) for i in range(n)]
    share = 2 * width // (2 * blocks)
    part = width // 4
    own_rows = [jnp.where(core == a, bias[1:2, :], bias[0:1, :]) for a in range(2)]
    pad = lambda v: jnp.concatenate([v, jnp.zeros((1, width - v.shape[1]), F32)], 1)
    none = jnp.zeros((8, width), F32)
    for j in range(blocks):
        to = turned(j, near, blocks)
        for chunk in range(chunks):
            index = 2 * j + chunk // 2
            a, start = divmod(index * share, width)
            p, at = divmod(start, 2 * part)
            own = own_rows[a][:, start : start + share]
            row = bias[2 + p : 3 + p, :]
            first, second = row[:, at : at + share], row[:, width // 2 + at : width // 2 + at + share]
            other = jnp.where(core == a, first, second)
            hidden = jnp.where(me == chunk % 2, own, other)
            begin = (j * chunks + chunk) * size
            tail = [pad(v[:, begin : begin + size]) for v in vectors] + [pad(hidden)]
            here = slice(begin, begin + size)
            with_vectors = jnp.concatenate([out_w[here, :], *tail], 0).astype(BF16)
            without = jnp.concatenate([value_w[here, :], none], 0).astype(BF16)
            mine[to, chunk] = jnp.where(core == 0, with_vectors, without)
            theirs[to, chunk] = jnp.where(core == 0, without, with_vectors)


def square_grads(at, blocks, mixed, grad_o, h1, gv, *rest):
    rows, _, width = mixed.shape
    operands = (mixed, grad_o, h1, gv, *rest[:3])
    shape = (blocks, 4, width // (4 * blocks) + 8, width)
    return pl.pallas_call(
        square_kernel,
        grid_spec=pltpu.PrefetchScalarGridSpec(
            num_scalar_prefetch=1,
            grid=(rows,),
            in_specs=[by_row(0, a.shape[1:]) for a in operands[:4]]
            + [whole(a.shape) for a in operands[4:]]
            + [ANYWHERE] * len(rest[3:]),
            out_specs=[whole(shape)] * 2,
            scratch_shapes=[pltpu.VMEM((width, width), F32)] * 2,
        ),
        out_shape=[jax.ShapeDtypeStruct(shape, BF16), pltpu.HBM(shape, BF16)],
        compiler_params=pltpu.CompilerParams(vmem_limit_bytes=40 * MIB),
        cost_estimate=long_cost(4),
        name="square_grads",
    )(at, *in_hbm(operands), *rest[3:])


def partner_kernel(count, at_ref, *refs):
    keep, send = refs[-2:]
    me = at_ref[2]
    for core in range(2):
        for out, chunk in ((keep, 2 * core + me), (send, 2 * core + 1 - me)):
            sum_of = refs[0][0, chunk].astype(F32)
            for part in refs[1:count]:
                sum_of = sum_of + part[0, chunk].astype(F32)
            out[core] = sum_of.astype(out.dtype)


def partner_split(at, parts, *tokens):
    shape = (2,) + parts[0].shape[2:]
    block = (1,) + parts[0].shape[1:]
    return pl.pallas_call(
        functools.partial(partner_kernel, len(parts)),
        grid_spec=pltpu.PrefetchScalarGridSpec(
            num_scalar_prefetch=1,
            grid=(1,),
            in_specs=[whole(block)] * len(parts) + [ANYWHERE] * len(tokens),
            out_specs=[whole(shape)] * 2,
        ),
        out_shape=[jax.ShapeDtypeStruct(shape, F32), jax.ShapeDtypeStruct(shape, BF16)],
        compiler_params=pltpu.CompilerParams(vmem_limit_bytes=16 * MIB),
        cost_estimate=long_cost(0.01),
        name="partner_split",
    )(at, *in_hbm(parts[:1]), *parts[1:], *tokens)


def cover(*tokens):
    def kernel(*refs):
        refs[-1][...] = jnp.zeros_like(refs[-1])

    return pl.pallas_call(
        kernel,
        in_specs=[ANYWHERE] * len(tokens),
        out_specs=pl.BlockSpec((8, 128), lambda: (0, 0)),
        out_shape=TOKEN,
        compiler_params=pltpu.CompilerParams(vmem_limit_bytes=MIB),
        cost_estimate=long_cost(100),
        name="cover",
    )(*tokens)


def hold(a, *tokens):
    return pl.pallas_call(
        lambda *refs: None,
        in_specs=[ANYWHERE] * (1 + len(tokens)),
        out_specs=ANYWHERE,
        out_shape=jax.ShapeDtypeStruct(a.shape, a.dtype),
        input_output_aliases={0: 0},
        compiler_params=pltpu.CompilerParams(vmem_limit_bytes=MIB),
        cost_estimate=long_cost(0.01),
        name="hold",
    )(a, *tokens)


def last_kernel(count, rows_first, at_ref, *refs):
    keep, send = refs[-2:]
    core = at_ref[0]
    sum_of = refs[0][...].astype(F32)
    for part in refs[1:count]:
        sum_of = sum_of + part[...].astype(F32)
    half = keep.shape[-2]
    shape = keep.shape
    low = sum_of[..., :half, :].reshape(shape)
    high = sum_of[..., half:, :].reshape(shape)
    keep[...] = jnp.where(core == 0, low, high)
    send[...] = jnp.where(core == 0, high, low).astype(BF16)


def last_split(at, parts, dim, rows, shape, *tokens):
    block = parts[0].shape[:dim] + (rows,) + parts[0].shape[dim + 1 :]
    return pl.pallas_call(
        functools.partial(last_kernel, len(parts), dim),
        grid_spec=pltpu.PrefetchScalarGridSpec(
            num_scalar_prefetch=1,
            grid=(1,),
            in_specs=[whole(block)] * len(parts) + [ANYWHERE] * len(tokens),
            out_specs=[whole(shape)] * 2,
        ),
        out_shape=[jax.ShapeDtypeStruct(shape, F32), jax.ShapeDtypeStruct(shape, BF16)],
        compiler_params=pltpu.CompilerParams(vmem_limit_bytes=16 * MIB),
        cost_estimate=long_cost(0.2),
        name="last_split",
    )(at, *in_hbm(parts[:1]), *parts[1:], *tokens)


def hidden_last_kernel(count, at_ref, *refs):
    keep, send = refs[-2:]
    core = at_ref[0]
    half = keep.shape[1]
    for which in range(2):
        sums = []
        for refs_of in (refs[:count], refs[count : 2 * count]):
            sum_of = refs_of[0][which].astype(F32)
            for p in refs_of[1:]:
                sum_of = sum_of + p[which].astype(F32)
            sums.append(sum_of)
        sum_of = jnp.concatenate(sums, 1)
        low, high = sum_of[:half], sum_of[half:]
        keep[which] = jnp.where(core == 0, low, high)
        send[which] = jnp.where(core == 0, high, low).astype(BF16)


def hidden_last(at, first, second, rows, width, *tokens):
    shape = (2, rows // 2, width)
    parts = [*first, *second]
    return pl.pallas_call(
        functools.partial(hidden_last_kernel, len(first)),
        grid_spec=pltpu.PrefetchScalarGridSpec(
            num_scalar_prefetch=1,
            grid=(1,),
            in_specs=[part_spec(p, 1, rows, 0)[0] for p in parts] + [ANYWHERE] * len(tokens),
            out_specs=[whole(shape)] * 2,
        ),
        out_shape=[jax.ShapeDtypeStruct(shape, F32), jax.ShapeDtypeStruct(shape, BF16)],
        compiler_params=pltpu.CompilerParams(vmem_limit_bytes=16 * MIB),
        cost_estimate=long_cost(0.2),
        name="hidden_last",
    )(at, *[p for p, _ in parts], *tokens)


def hidden_out_kernel(at_ref, kept, got, *rest):
    up, down = rest[-2:]
    core = at_ref[0]
    for which, out in ((0, up), (1, down)):
        mine, theirs = kept[which], got[which].astype(F32)
        out[...] = jnp.concatenate([jnp.where(core == 0, mine, theirs), jnp.where(core == 0, theirs, mine)], 1)


def logit_out_kernel(at_ref, kept, got, *rest):
    out = rest[-1]
    core = at_ref[0]
    half = kept.shape[0]
    mine, theirs = kept[...], got[...].astype(F32)
    out[:half] = jnp.where(core == 0, mine, theirs)
    out[half:] = jnp.where(core == 0, theirs, mine)


def square_out_kernel(at_ref, kept, got, *rest):
    out_w, value_w, up_bias, *vectors = rest[-10:]
    core = at_ref[0]
    size = out_w.shape[0]
    mine, theirs = kept[...], got[...].astype(F32)
    first = jnp.where(core == 0, mine, theirs)
    second = jnp.where(core == 0, theirs, mine)
    out_w[...] = first[:size]
    value_w[...] = second[:size]
    for i, v in enumerate(vectors):
        v[...] = first[size + i : size + i + 1, :size]
    up_bias[...] = first[size + 7 : size + 8, : up_bias.shape[1]]


def finish(kernel, at, kept, got, shapes, *tokens):
    return pl.pallas_call(
        kernel,
        grid_spec=pltpu.PrefetchScalarGridSpec(
            num_scalar_prefetch=1,
            grid=(1,),
            in_specs=[whole(kept.shape), whole(got.shape)] + [ANYWHERE] * len(tokens),
            out_specs=[whole(s) for s in shapes],
        ),
        out_shape=[pltpu.HBM(s, F32) for s in shapes],
        compiler_params=pltpu.CompilerParams(vmem_limit_bytes=16 * MIB),
        cost_estimate=long_cost(0.2),
        name="finish",
    )(at, kept, got, *tokens)


def input_kernel(chained, x, grad_resid, gh_own, gh_received, small, *rest):
    grad, token = rest[-2:]
    token[...] = jnp.zeros_like(token)
    unit, scale = unit_rows(x[0].astype(F32))
    total = gh_own[0] + gh_received[0].astype(F32)
    grad[0] = grad_resid[0] + norm_back(total, unit, scale, small[0:1, :])


def input_rows(first, count, cost, inputs, grad_resid, gh_own, gh_received, small, chain, *tokens):
    rows, length, width = inputs.shape
    operands = [*in_hbm([inputs, grad_resid, gh_own]), gh_received, *in_hbm([small])]
    in_specs = [by_row(first, (length, width))] * 3 + [by_row(0, (length, width)), whole(small.shape)]
    aliases = {}
    if chain is not None:
        aliases = {len(operands): 0}
        operands += in_hbm([chain])
        in_specs.append(ANYWHERE)
    operands += tokens
    in_specs += [ANYWHERE] * len(tokens)
    return pl.pallas_call(
        functools.partial(input_kernel, chain is not None),
        grid=(count,),
        in_specs=in_specs,
        out_specs=[by_row(first, (length, width)), whole((8, 128))],
        out_shape=[pltpu.HBM((rows, length, width), F32), TOKEN],
        input_output_aliases=aliases,
        compiler_params=pltpu.CompilerParams(vmem_limit_bytes=24 * MIB),
        cost_estimate=long_cost(cost),
        name="input_rows",
    )(*operands)


def swap(a, axis, size, bit):
    return lax.ppermute(a, axis, [(i, i ^ bit) for i in range(size)])


class Scatter:
    def __init__(self, groups, dim, size):
        self.groups = [[p if isinstance(p, tuple) else (p, None) for p in parts] for parts in groups]
        array, lead = self.groups[0][0]
        self.dim, self.size, self.step = dim, size, 1
        self.rows = array.shape[dim + (lead is not None)]

    def send(self, *tokens):
        self.rows //= 2
        out = send_sum(self.groups, self.dim, self.rows, 1, *tokens)
        self.add(swap(out, "dp", self.size, 1 << self.step))
        self.step += 1
        return out

    def add(self, received):
        self.latest = received
        for i, parts in enumerate(self.groups):
            parts.append((received, i if len(self.groups) > 1 else None))

    def arrays(self):
        return [p for p, _ in self.groups[0]]


def paired_shards(
    dp,
    mp,
    inputs,
    segment_ids,
    ln1_gain,
    ln1_bias,
    value_weight,
    value_bias,
    random_logits,
    out_weight,
    out_bias,
    ln2_gain,
    ln2_bias,
    up_weight,
    up_bias,
    down_weight,
    down_bias,
    out_cotangent,
):
    rows, length, width = inputs.shape
    heads = random_logits.shape[0]
    full = segment_ids.shape[1]
    positions = rows * length
    hidden = up_weight.shape[1]
    tile = hidden // 2
    me = lax.axis_index("mp")
    place = lax.axis_index("dp")
    bits = dp.bit_length() - 1
    bit = [lax.rem(lax.div(place, 1 << b), 2) for b in range(bits)]
    core = bit[0]
    near = lax.shift_right_logical(place, 1)
    blocks = dp // 2
    at = jnp.stack([core, near, me]).astype(jnp.int32)
    offs = jnp.stack([me * length, (1 - me) * length, core, near]).astype(jnp.int32)
    quarter = jnp.stack([2 * core, 2 * core + 1, bit[1]]).astype(jnp.int32)
    by_core = lambda first, second: jnp.where(core == 0, first, second)
    small, up_row = prep(
        [ln1_gain, ln1_bias, ln2_gain, ln2_bias, value_bias, out_bias, down_bias], up_bias
    )

    received = [swap(inputs[r : r + 1], "mp", mp, 1) for r in range(rows)]
    expo = jnp.exp(random_logits.astype(F32)).astype(BF16)
    seg_row = segment_ids[:, None, :]
    g = out_cotangent.reshape(positions, width)

    chain = None
    packed = []
    for r in range(rows):
        chain = mix_rows(
            r,
            1,
            offs,
            blocks,
            inputs,
            received[r],
            out_cotangent,
            seg_row,
            expo,
            (value_weight, out_weight, small),
            chain,
            *packed[-1:],
        )
        if 1 <= r <= 2:
            packed.append(pack(r - 1, quarter, up_weight, down_weight, up_row, chain[-1]))
    h1, values, recip, mixed, resid, h2, h2t, gt, _ = chain
    h2 = h2.reshape(positions, width)
    h2t = h2t.reshape(width, positions)
    gt = gt.reshape(width, positions)

    def fetch(by_x):
        by_y = swap(by_x, "dp", dp, 2)
        return by_x, by_y

    def share(by_x, by_y):
        return by_x, by_y, swap(by_x, "dp", dp, 1), swap(by_y, "dp", dp, 1)

    by_x = [swap(message, "mp", mp, 1) for message in packed]
    fixed = (h2, g, h2t, gt)
    tiles = [(1 - core).reshape(1).astype(jnp.int32), core.reshape(1).astype(jnp.int32)]
    weights = (up_weight, up_row, down_weight)
    *sums, own_theirs, bias, token = own_hidden(tiles[0], fixed, *weights, None)
    fetched = [fetch(hold(by_x[0], token))]
    *sums, own_mine, bias, token = own_hidden(tiles[1], fixed, *weights, (*sums, bias), fetched[0][0])
    fetched.append(fetch(hold(by_x[1], token)))
    own_received = swap(own_theirs, "dp", dp, 1)
    own = Scatter([[(own_mine, i), (own_received, i)] for i in range(2)], 1, dp)
    near_y = jnp.stack([bit[1], core]).astype(jnp.int32)
    *sums, mine, theirs, bias, token = other_hidden(
        0, near_y, fixed, share(fetched[0][0], hold(fetched[0][1], token)), (*sums, bias)
    )
    others = [Scatter([[mine, swap(theirs, "dp", dp, 1)]], 1, dp)]
    sent = own.send(token)
    out, dh, mine, theirs, bias, token = other_hidden(
        1, near_y, fixed, share(fetched[1][0], hold(fetched[1][1], token)), (*sums, bias), sent
    )
    others.append(Scatter([[mine, swap(theirs, "dp", dp, 1)]], 1, dp))
    token = others[0].send(token)

    shape = (rows, length, width)
    layer_out, grad_resid, grad_o, gm, vec_two = resid_rows(
        [out.reshape(shape), dh.reshape(shape), resid, out_cotangent, recip], (out_weight, small), token
    )
    token = others[1].send(vec_two)
    back = lambda pair, cost, chain, token: back_rows(
        2 * pair,
        2,
        cost,
        offs,
        gm,
        inputs,
        received[2 * pair : 2 * pair + 2],
        seg_row,
        expo,
        value_weight,
        chain,
        token,
    )

    def to_partner(other, token):
        sent = send_sum(other.groups, 1, other.rows, 0, token)
        return sent, swap(sent, "mp", mp, 1)

    chain = back(0, 4, None, token)
    passed = [swap(chain[2], "mp", mp, 1)]
    token = chain[2]
    chain = back(1, 4, chain, token)
    gh_last = chain[2]
    gv, gh_own, _, vec_one = chain
    token, arrived = to_partner(others[0], gh_last)
    own.groups[0].append((arrived, None))
    square_theirs, square_mine = square_grads(
        at,
        blocks,
        mixed,
        grad_o,
        h1,
        gv,
        bias,
        vec_two,
        vec_one,
        token,
    )

    square = Scatter([[square_mine, swap(square_theirs, "dp", dp, 1)]], 0, dp)
    give_inputs = lambda pair, cost, chain, token: input_rows(
        2 * pair, 2, cost, inputs, grad_resid, gh_own, passed[pair], small, chain, token
    )
    token = cover(square_mine, others[1].latest, own.latest)
    token = square.send(token)
    token, arrived = to_partner(others[1], token)
    own.groups[1].append((arrived, None))
    gh_last = hold(gh_last, token)
    passed.append(swap(gh_last, "mp", mp, 1))
    grads = (offs, blocks, gm, mixed, values, seg_row, expo)
    logits_theirs = logits_grad(False, *grads, gh_last)
    logits_mine = logits_grad(True, *grads, logits_theirs)
    logit = Scatter([[logits_mine, swap(logits_theirs, "dp", dp, 1)]], 0, dp)
    token = logit.send(logits_mine)
    token = square.send(token)
    token = own.send(token)
    chain, token = give_inputs(0, 0.5, None, token)
    token = square.send(token)
    token = logit.send(token)
    square_kept, token = partner_split(at, square.arrays(), token)
    square_received = swap(token, "mp", mp, 1)
    token = own.send(token)
    chain, token = give_inputs(1, 0.5, chain, token)
    chunk = square_mine.shape[2]
    square_parts = [p.reshape(2 * chunk, width) for p in (square_kept, square_received)]
    square_kept, token = last_split(at, square_parts, 0, 2 * chunk, (chunk, width), token)
    square_received = swap(token, "dp", dp, 1)
    token = logit.send(token)
    part_size = width // (dp * mp)
    out_part, value_part, up_bias_part, *vector = finish(
        square_out_kernel,
        at,
        square_kept,
        square_received,
        [(part_size, width), (part_size, width), (1, hidden // dp)] + [(1, part_size)] * 7,
        token,
    )
    kept, token = hidden_last(at, *own.groups, own.rows, tile, out_part)
    hidden_received = swap(token, "dp", dp, 1)
    logit_kept, token = last_split(at, logit.arrays(), 0, 1, (heads // 2, full // dp, length), token)
    logit_received = swap(token, "dp", dp, 1)
    up_part, down_part = finish(
        hidden_out_kernel, at, kept, hidden_received, [(width // dp, hidden)] * 2, token
    )
    (logit_part,) = finish(
        logit_out_kernel, at, logit_kept, logit_received, [(heads, full // dp, length)], up_part
    )
    bo_part, g2_part, b2_part, bd_part, g1_part, b1_part, bv_part = (v.reshape(-1) for v in vector)
    return (
        layer_out,
        chain,
        g1_part,
        b1_part,
        value_part,
        bv_part,
        logit_part.transpose(0, 2, 1),
        out_part,
        bo_part,
        g2_part,
        b2_part,
        up_part,
        up_bias_part,
        down_part.T,
        bd_part,
    )


def smooth(t):
    return jax.nn.gelu(t, approximate=True)


def contract_rows(left, right):
    return lax.dot_general(
        left, right, (((0,), (0,)), ((), ())), preferred_element_type=jnp.float32
    )


def contract_cols(left, right):
    return lax.dot_general(
        left, right, (((1,), (1,)), ((), ())), preferred_element_type=jnp.float32
    )


def normalize(x, gain, shift):
    centred = x - jnp.mean(x, -1, keepdims=True)
    scale = lax.rsqrt(jnp.mean(centred * centred, -1, keepdims=True) + 1e-05)
    unit = centred * scale
    return (unit * gain + shift, unit, scale)


def normalize_back(grad, unit, scale, gain):
    scaled = grad * gain
    inner = scale * (
        scaled
        - jnp.mean(scaled, -1, keepdims=True)
        - unit * jnp.mean(scaled * unit, -1, keepdims=True)
    )
    return (inner, jnp.sum(grad * unit, 0), jnp.sum(grad, 0))


def shards(
    inputs,
    segment_ids,
    ln1_gain,
    ln1_bias,
    value_weight,
    value_bias,
    random_logits,
    out_weight,
    out_bias,
    ln2_gain,
    ln2_bias,
    up_weight,
    up_bias,
    down_weight,
    down_bias,
    out_cotangent,
):
    seqs, local_len, width = inputs.shape
    heads = random_logits.shape[0]
    full_len = segment_ids.shape[1]
    head_dim = width // heads
    rows = seqs * local_len
    gain_one = ln1_gain.astype(jnp.float32)
    gain_two = ln2_gain.astype(jnp.float32)
    start_x = inputs.astype(jnp.float32).reshape(rows, width)
    normed_one, unit_one, scale_one = normalize(start_x, gain_one, ln1_bias.astype(jnp.float32))
    h1_low = normed_one.astype(jnp.bfloat16)
    values = (
        jnp.dot(h1_low, value_weight, preferred_element_type=jnp.float32)
        + value_bias.astype(jnp.float32)
    ).astype(jnp.bfloat16)
    gathered = lax.all_gather(values.reshape(seqs, local_len, width), "mp", axis=1, tiled=True)
    every_head = gathered.reshape(seqs, full_len, heads, head_dim)
    offset = lax.axis_index("mp") * local_len
    own_segs = lax.dynamic_slice_in_dim(segment_ids, offset, local_len, 1)
    same = own_segs[:, :, None] == segment_ids[:, None, :]
    scores = jnp.where(same[:, None], random_logits.astype(jnp.float32)[None], -1e30)
    peak = jnp.max(scores, -1, keepdims=True)
    expo = jnp.exp(scores - peak)
    total = jnp.sum(expo, -1, keepdims=True)
    probs = expo / total
    probs_low = probs.astype(jnp.bfloat16)
    mixed = jnp.einsum("shqk,skhd->sqhd", probs_low, every_head, preferred_element_type=jnp.float32)
    mixed_low = mixed.reshape(rows, width).astype(jnp.bfloat16)
    resid = (
        start_x
        + jnp.dot(mixed_low, out_weight, preferred_element_type=jnp.float32)
        + out_bias.astype(jnp.float32)
    )
    normed_two, unit_two, scale_two = normalize(resid, gain_two, ln2_bias.astype(jnp.float32))
    h2_low = normed_two.astype(jnp.bfloat16)
    grad_low = out_cotangent.reshape(rows, width)
    h2_full = lax.all_gather(
        h2_low.reshape(seqs, local_len, width), "mp", axis=1, tiled=True
    ).reshape(seqs * full_len, width)
    pre = jnp.dot(h2_full, up_weight, preferred_element_type=jnp.float32) + up_bias.astype(
        jnp.float32
    )
    act, gelu_pull = jax.vjp(smooth, pre)
    act_low = act.astype(jnp.bfloat16)
    partial_out = jnp.dot(act_low, down_weight, preferred_element_type=jnp.float32).reshape(
        seqs, full_len, width
    )
    ffn_out = lax.psum_scatter(
        partial_out.astype(jnp.bfloat16), "mp", scatter_dimension=1, tiled=True
    ).astype(jnp.float32).reshape(rows, width) + down_bias.astype(jnp.float32)
    final = resid + ffn_out
    grad_full = lax.all_gather(out_cotangent, "mp", axis=1, tiled=True).reshape(
        seqs * full_len, width
    )
    grad_down = contract_rows(act_low, grad_full)
    grad_act = contract_cols(grad_full, down_weight)
    grad_pre = gelu_pull(grad_act)[0].astype(jnp.bfloat16)
    grad_up_b = jnp.sum(grad_pre.astype(jnp.float32), 0)
    grad_up = contract_rows(h2_full, grad_pre)
    h2_terms = contract_cols(grad_pre, up_weight).reshape(seqs, full_len, width)
    grad_h2 = (
        lax.psum_scatter(h2_terms.astype(jnp.bfloat16), "mp", scatter_dimension=1, tiled=True)
        .astype(jnp.float32)
        .reshape(rows, width)
    )
    grad_final = grad_low.astype(jnp.float32)
    grad_down_b = jnp.sum(grad_final, 0)
    inner_two, gain_two_grad, shift_two_grad = normalize_back(
        grad_h2, unit_two, scale_two, gain_two
    )
    grad_resid = grad_final + inner_two
    grad_o_low = grad_resid.astype(jnp.bfloat16)
    grad_out_b = jnp.sum(grad_o_low.astype(jnp.float32), 0)
    grad_out_w = contract_rows(mixed_low, grad_o_low)
    grad_mixed = (
        contract_cols(grad_o_low, out_weight)
        .astype(jnp.bfloat16)
        .reshape(seqs, local_len, heads, head_dim)
    )
    grad_probs = jnp.einsum(
        "sqhd,skhd->shqk", grad_mixed, every_head, preferred_element_type=jnp.float32
    )
    grad_scores = probs * (grad_probs - jnp.sum(probs * grad_probs, -1, keepdims=True))
    grad_logits = jnp.sum(grad_scores, 0)
    value_terms = jnp.einsum(
        "shqk,sqhd->skhd", probs_low, grad_mixed, preferred_element_type=jnp.float32
    ).reshape(seqs, full_len, width)
    grad_values = (
        lax.psum_scatter(value_terms.astype(jnp.bfloat16), "mp", scatter_dimension=1, tiled=True)
        .astype(jnp.float32)
        .reshape(rows, width)
        .astype(jnp.bfloat16)
    )
    grad_value_b = jnp.sum(grad_values.astype(jnp.float32), 0)
    grad_value_w = contract_rows(h1_low, grad_values)
    inner_one, gain_one_grad, shift_one_grad = normalize_back(
        contract_cols(grad_values, value_weight), unit_one, scale_one, gain_one
    )
    grad_x = (grad_resid + inner_one).reshape(seqs, local_len, width)
    vectors = jnp.stack(
        [
            gain_one_grad,
            shift_one_grad,
            grad_value_b,
            grad_out_b,
            gain_two_grad,
            shift_two_grad,
            grad_down_b,
        ]
    )
    value_w_part, out_w_part, vector_part = (
        lax.psum_scatter(grad_value_w, ("dp", "mp"), scatter_dimension=0, tiled=True),
        lax.psum_scatter(grad_out_w, ("dp", "mp"), scatter_dimension=0, tiled=True),
        lax.psum_scatter(vectors, ("dp", "mp"), scatter_dimension=1, tiled=True),
    )
    up_part, up_b_part, down_part, logit_part = (
        lax.psum_scatter(
            grad_up.astype(jnp.bfloat16), "dp", scatter_dimension=0, tiled=True
        ).astype(jnp.float32),
        lax.psum_scatter(
            grad_up_b[None].astype(jnp.bfloat16), "dp", scatter_dimension=1, tiled=True
        ).astype(jnp.float32),
        lax.psum_scatter(
            grad_down.astype(jnp.bfloat16), "dp", scatter_dimension=1, tiled=True
        ).astype(jnp.float32),
        lax.psum_scatter(
            grad_logits.astype(jnp.bfloat16), "dp", scatter_dimension=2, tiled=True
        ).astype(jnp.float32),
    )
    return (
        final.astype(jnp.bfloat16).reshape(seqs, local_len, width),
        grad_x,
        vector_part[0],
        vector_part[1],
        value_w_part,
        vector_part[2],
        logit_part,
        out_w_part,
        vector_part[3],
        vector_part[4],
        vector_part[5],
        up_part,
        up_b_part,
        down_part,
        vector_part[6],
    )


def solution(mesh):
    in_specs = (
        P("dp", "mp", None),
        P("dp", None),
        P(),
        P(),
        P(),
        P(),
        P(None, "mp", None),
        P(),
        P(),
        P(),
        P(),
        P(None, "mp"),
        P("mp"),
        P("mp", None),
        P(),
        P("dp", "mp", None),
    )
    out_specs = (
        P("dp", "mp", None),
        P("dp", "mp", None),
        P(("dp", "mp")),
        P(("dp", "mp")),
        P(("dp", "mp"), None),
        P(("dp", "mp")),
        P(None, "mp", "dp"),
        P(("dp", "mp"), None),
        P(("dp", "mp")),
        P(("dp", "mp")),
        P(("dp", "mp")),
        P("dp", "mp"),
        P("mp", "dp"),
        P("mp", "dp"),
        P(("dp", "mp")),
    )
    dp, mp = mesh.shape["dp"], mesh.shape["mp"]
    body = functools.partial(paired_shards, dp, mp) if mp == 2 else shards
    return jax.shard_map(body, mesh=mesh, in_specs=in_specs, out_specs=out_specs, check_vma=False)
```

```python
import functools

import jax
import jax.numpy as jnp
from jax import lax
from jax.experimental import pallas as pl
from jax.experimental.pallas import tpu as pltpu
from jax.sharding import PartitionSpec as P

F32 = jnp.float32
BF16 = jnp.bfloat16
GELU_A = 0.7978845608028654
GELU_B = GELU_A * 0.044715
MIB = 2**20


def mm(left, right, left_dim, right_dim):
    return lax.dot_general(
        left, right, (((left_dim,), (right_dim,)), ((), ())), preferred_element_type=F32
    )


def unit_rows(x):
    centred = x - jnp.mean(x, -1, keepdims=True)
    scale = lax.rsqrt(jnp.mean(centred * centred, -1, keepdims=True) + 1e-05)
    return centred * scale, scale


def norm_back(grad, unit, scale, gain):
    e = grad * gain
    return scale * (
        e - jnp.mean(e, -1, keepdims=True) - unit * jnp.mean(e * unit, -1, keepdims=True)
    )


def same_document(first, seg_row, row, length):
    keys = seg_row[row].astype(F32)
    own = seg_row[row, :, pl.ds(pl.multiple_of(first, length), length)].astype(F32)
    queries = jnp.broadcast_to(own, (8, length)).T[:, :1]
    return jnp.where(queries == keys, 1.0, 0.0)


def turned(block, near, blocks):
    other = jnp.bitwise_xor(block, near)
    place = 0
    weight = blocks
    for b in range(blocks.bit_length() - 1):
        weight //= 2
        place = place + jnp.bitwise_and(lax.shift_right_logical(other, b), 1) * weight
    return place


def long_cost(us):
    return pl.CostEstimate(flops=int(us * 10**10), bytes_accessed=10**5, transcendentals=0)


IN_VMEM = pl.BlockSpec(memory_space=pltpu.VMEM)
ANYWHERE = pl.BlockSpec(memory_space=pl.ANY)


def in_hbm(operands):
    return [pltpu.with_memory_space_constraint(a, pltpu.HBM) for a in operands]


def in_vmem(operands):
    return [pltpu.with_memory_space_constraint(a, pltpu.VMEM) for a in operands]


TOKEN = pltpu.HBM((8, 128), F32)


def whole(shape):
    return pl.BlockSpec(shape, lambda i, *_: (0,) * len(shape))


def by_row(first, shape):
    return pl.BlockSpec((1,) + shape, lambda i, *_: (first + i,) + (0,) * len(shape))


def prep_kernel(*refs):
    *vectors, bias, small, hidden = refs
    for i, v in enumerate(vectors):
        small[i : i + 1, :] = v[...].astype(F32).reshape(1, -1)
    hidden[...] = bias[...].astype(F32).reshape(1, -1)


def prep(vectors, bias):
    return pl.pallas_call(
        prep_kernel,
        in_specs=[IN_VMEM] * (len(vectors) + 1),
        out_specs=[IN_VMEM] * 2,
        out_shape=[
            pltpu.HBM((8, vectors[0].shape[0]), F32),
            pltpu.HBM((1, bias.shape[0]), F32),
        ],
        name="prep",
    )(*vectors, bias)


def mix_kernel(offs, x_own, x_other, g, seg_row, expo, wv, wo, small, *rest):
    h1, values, recip, mixed, resid, h2, h2t, gt, token, ones = rest[-10:]
    g1, b1, g2, b2, bv, bo, _ = (small[i : i + 1, :] for i in range(7))
    token[...] = jnp.zeros_like(token)
    length = x_own.shape[1]
    heads = expo.shape[0]
    ones[:, 128:] = jnp.ones_like(ones[:, 128:])
    x = x_own[0].astype(F32)
    for block, off in ((x, offs[0]), (x_other[0].astype(F32), offs[1])):
        unit, _ = unit_rows(block)
        at = pl.ds(pl.multiple_of(off, length), length)
        h1[0, at, :] = (unit * g1 + b1).astype(BF16)
    values[0] = (mm(h1[0], wv[...], 1, 0) + bv).astype(BF16)
    mask = same_document(offs[0], seg_row, 0, length).astype(BF16)
    low_lane = lax.broadcasted_iota(jnp.int32, (length, 128), 1) < 64
    for pair in range(heads // 2):
        lanes = slice(128 * pair, 128 * pair + 128)
        ones[:, :128] = values[0, :, lanes]
        first = mm(expo[2 * pair] * mask, ones[...], 1, 0)
        second = mm(expo[2 * pair + 1] * mask, ones[...], 1, 0)
        inverse = 1.0 / jnp.where(low_lane, first[:, 128:], second[:, 128:])
        recip[0, :, lanes] = inverse
        mixed[0, :, lanes] = jnp.where(low_lane, first[:, :128], second[:, :128]) * inverse
    r = x + mm(mixed[0].astype(BF16), wo[...], 1, 0) + bo
    resid[0] = r
    unit, _ = unit_rows(r)
    low = (unit * g2 + b2).astype(BF16)
    h2[0] = low
    blocks, size, _ = h2t.shape
    for ref, source in ((h2t, low.T), (gt, g[0].T)):
        for j in range(blocks):
            ref[turned(j, offs[3], blocks)] = source[j * size : (j + 1) * size, :]


def mix_rows(first, count, offs, blocks, inputs, received, cotangent, seg_row, expo, weights, chain, *tokens):
    rows, length, width = inputs.shape
    full = seg_row.shape[2]
    heads = expo.shape[0]
    shapes = [
        ((full, width), BF16),
        ((full, width), BF16),
        ((length, width), F32),
        ((length, width), F32),
        ((length, width), F32),
        ((length, width), BF16),
    ]
    out_specs = [by_row(first, s) for s, _ in shapes]
    turned_spec = pl.BlockSpec((blocks, width // blocks, length), lambda i, *_: (0, 0, first + i))
    out_specs += [turned_spec] * 2
    out_shape = [pltpu.HBM((rows,) + s, t) for s, t in shapes[:2]]
    out_shape += [pltpu.VMEM((rows,) + s, t) for s, t in shapes[2:]]
    out_shape += [pltpu.VMEM((blocks, width // blocks, rows * length), BF16)] * 2
    operands = [offs, *in_hbm([inputs]), received, *in_hbm([cotangent, seg_row]), *in_vmem([expo, *weights])]
    in_specs = [
        by_row(first, (length, width)),
        by_row(0, (length, width)),
        by_row(first, (length, width)),
        by_row(first, (1, full)),
        *[IN_VMEM] * (1 + len(weights)),
    ]
    aliases = {}
    if chain is not None:
        aliases = {len(operands) + i: i for i in range(len(out_shape))}
        operands += [*in_hbm(chain[:2]), *in_vmem(chain[2:8])]
        in_specs += [ANYWHERE] * len(out_shape)
    operands += tokens
    in_specs += [ANYWHERE] * len(tokens)
    out_specs.append(whole((8, 128)))
    out_shape.append(TOKEN)
    return pl.pallas_call(
        mix_kernel,
        grid_spec=pltpu.PrefetchScalarGridSpec(
            num_scalar_prefetch=1,
            grid=(count,),
            in_specs=in_specs,
            out_specs=out_specs,
            scratch_shapes=[pltpu.VMEM((full, 256), BF16)],
        ),
        out_shape=out_shape,
        input_output_aliases=aliases,
        compiler_params=pltpu.CompilerParams(vmem_limit_bytes=32 * MIB),
        cost_estimate=long_cost(3 * count),
        name="mix_rows",
    )(*operands)


def gelu_pair(t):
    square = t * t
    curve = jnp.tanh(t * (GELU_A + GELU_B * square))
    half = 0.5 + 0.5 * curve
    act = t * half
    return act, half + act * (1.0 - curve) * (GELU_A + 3 * GELU_B * square)


def hidden_tile(h2, g, h2t, gt, wu, up_dim, bu, wd, sums, outs, act_s, pre_s, block):
    out0, dh0 = sums if sums else (None, None)
    out, dh = outs
    total = None
    for m in range(h2.shape[0] // block):
        at = pl.ds(m * block, block)
        pre = mm(h2[at, :], wu[...], 1, up_dim) + bu
        grad_act = mm(g[at, :], wd[...], 1, 1)
        act, slope = gelu_pair(pre)
        act_low = act.astype(BF16)
        grad_pre = grad_act * slope
        part = jnp.sum(grad_pre, 0, keepdims=True)
        total = part if total is None else total + part
        pre_low = grad_pre.astype(BF16)
        act_s[at, :] = act_low
        pre_s[at, :] = pre_low
        out_part = mm(act_low, wd[...], 1, 0)
        dh_part = mm(pre_low, wu[...], 1, 1 - up_dim)
        out[at, :] = out_part if sums is None else out0[at, :] + out_part
        dh[at, :] = dh_part if sums is None else dh0[at, :] + dh_part
    return total, lambda: (
        mm(h2t[...], pre_s[...], 1, 0).astype(BF16),
        mm(gt[...], act_s[...], 1, 0).astype(BF16),
    )


def own_hidden_kernel(block, first, at_ref, h2, g, h2t, gt, wu, bu, wd, *rest):
    out, dh, grads, bias, token, act_s, pre_s = rest[-7:]
    token[...] = jnp.zeros_like(token)
    sums = None
    if not first:
        out0, dh0, bias0 = rest[:3]
        sums = (out0, dh0)
    total, weights = hidden_tile(
        h2, g, h2t, gt, wu, 0, bu[...].astype(F32), wd, sums, (out, dh), act_s, pre_s, block
    )
    if first:
        bias[0:1, :] = total
    else:
        bias[...] = bias0[...]
        bias[1:2, :] = total
    half = grads.shape[3]
    for which, grad in enumerate(weights()):
        for p in range(2):
            grads[p, which] = grad[:, p * half : (p + 1) * half]


def other_hidden_kernel(block, which, near, h2, g, h2t, gt, wx, wy, wcx, wcy, out0, dh0, bias0, *rest):
    out, dh, mine, theirs, bias, token, wu, wd, act_s, pre_s = rest[-10:]
    token[...] = jnp.zeros_like(token)
    near_y = near[0]
    part = wx.shape[0] // 2 - 8
    for first, pieces in ((0, (wx, wy)), (2, (wcx, wcy))):
        for turn, piece in enumerate(pieces):
            quarter = first + jnp.bitwise_xor(near_y, turn)
            at = pl.ds(pl.multiple_of(quarter * part, part), part)
            wu[at, :] = piece[:part, :]
            wd[at, :] = piece[part : 2 * part, :]
    rows = wx[2 * part :, :].astype(F32)
    lanes = slice(2 * part * which, 2 * part * (which + 1))
    lower, upper = rows[0:1, lanes], rows[1:2, lanes]
    swapped = near[1] == 1
    bu = jnp.concatenate([jnp.where(swapped, upper, lower), jnp.where(swapped, lower, upper)], axis=1)
    total, weights = hidden_tile(
        h2, g, h2t, gt, wu, 1, bu, wd, (out0, dh0), (out, dh), act_s, pre_s, block
    )
    bias[...] = bias0[...]
    bias[2 + which : 3 + which, :] = total
    half = 2 * part
    for index, grad in enumerate(weights()):
        mine[index] = grad[:, :half]
        theirs[index] = grad[:, half:]


def hidden_call(positions, width, tile):
    return dict(
        compiler_params=pltpu.CompilerParams(vmem_limit_bytes=19 * MIB),
        cost_estimate=long_cost(5),
    )


def own_hidden(tile_at, fixed, wu, bu, wd, sums, *tokens):
    positions, width = fixed[0].shape
    tile = wu.shape[1] // 2
    operands = [*in_vmem(fixed), *in_hbm([wu, bu, wd]), *in_vmem(sums or ()), *tokens]
    aliases = {1 + len(fixed) + 3: 0, 1 + len(fixed) + 4: 1} if sums else {}
    weights = [
        pl.BlockSpec((width, tile), lambda i, at: (0, at[0])),
        pl.BlockSpec((1, tile), lambda i, at: (0, at[0])),
        pl.BlockSpec((tile, width), lambda i, at: (at[0], 0)),
    ]
    return pl.pallas_call(
        functools.partial(own_hidden_kernel, 256, sums is None),
        grid_spec=pltpu.PrefetchScalarGridSpec(
            num_scalar_prefetch=1,
            grid=(1,),
            in_specs=[IN_VMEM] * len(fixed) + weights + [IN_VMEM] * len(sums or ()) + [ANYWHERE] * len(tokens),
            out_specs=[IN_VMEM] * 2 + [whole((2, 2, width, tile // 2)), IN_VMEM, whole((8, 128))],
            scratch_shapes=[pltpu.VMEM((positions, tile), BF16)] * 2,
        ),
        out_shape=[pltpu.VMEM((positions, width), F32)] * 2
        + [pltpu.HBM((2, 2, width, tile // 2), BF16), pltpu.VMEM((8, tile), F32), TOKEN],
        input_output_aliases=aliases,
        name="own_hidden",
        **hidden_call(positions, width, tile),
    )(tile_at, *operands)


def other_hidden(which, near, fixed, pieces, sums, *tokens):
    positions, width = fixed[0].shape
    tile = 4 * (pieces[0].shape[0] // 2 - 8)
    operands = [*in_vmem(fixed), *pieces, *in_vmem(sums)]
    aliases = {1 + len(operands) - 3: 0, 1 + len(operands) - 2: 1}
    block = whole((2, width, tile // 2))
    return pl.pallas_call(
        functools.partial(other_hidden_kernel, 256, which),
        grid_spec=pltpu.PrefetchScalarGridSpec(
            num_scalar_prefetch=1,
            grid=(1,),
            in_specs=[IN_VMEM] * 4 + [whole(p.shape) for p in pieces] + [IN_VMEM] * 3 + [ANYWHERE] * len(tokens),
            out_specs=[IN_VMEM] * 2 + [block] * 2 + [IN_VMEM, whole((8, 128))],
            scratch_shapes=[pltpu.VMEM((tile, width), BF16)] * 2 + [pltpu.VMEM((positions, tile), BF16)] * 2,
        ),
        out_shape=[pltpu.VMEM((positions, width), F32)] * 2
        + [make((2, width, tile // 2), BF16) for make in (pltpu.HBM, jax.ShapeDtypeStruct)]
        + [pltpu.VMEM((8, tile), F32), TOKEN],
        input_output_aliases=aliases,
        name="other_hidden",
        **hidden_call(positions, width, tile),
    )(near, *operands, *tokens)


def pack_kernel(at, up, down, bias, token, out):
    size = up.shape[1] // 2
    width = down.shape[1]
    start = pl.multiple_of(at[2] * size, size)
    out[:size, :] = jnp.where(at[2] == 0, up[:, :size].T, up[:, size:].T)
    out[size : 2 * size, :] = down[pl.ds(start, size), :]
    both = jnp.concatenate([bias[:, :width], bias[:, width:], jnp.zeros((14, width), F32)], 0)
    out[2 * size :, :] = both.astype(BF16)


def pack(which, at, up, down, bias, token):
    width, hidden = up.shape
    part = hidden // 4
    return pl.pallas_call(
        pack_kernel,
        grid_spec=pltpu.PrefetchScalarGridSpec(
            num_scalar_prefetch=1,
            grid=(1,),
            in_specs=[
                pl.BlockSpec((width, part), lambda i, at: (0, at[which])),
                pl.BlockSpec((part, width), lambda i, at: (at[which], 0)),
                whole(bias.shape),
                ANYWHERE,
            ],
            out_specs=whole((part + 16, width)),
        ),
        out_shape=jax.ShapeDtypeStruct((part + 16, width), BF16),
        compiler_params=pltpu.CompilerParams(vmem_limit_bytes=16 * MIB),
        cost_estimate=long_cost(0.5),
        name="pack",
    )(at, *in_hbm([up, down, bias, token]))


def resid_kernel(out_acc, dh, resid, g, recip, wo, small, *rest):
    layer_out, grad_resid, grad_out, gm, vec = rest[-5:]
    g2, bd = small[2:3, :], small[6:7, :]
    r = resid[0]
    at = pl.program_id(0)
    layer_out[0] = (r + out_acc[at] + bd).astype(BF16)
    unit, scale = unit_rows(r)
    grad = dh[at]
    cot = g[0].astype(F32)
    total = cot + norm_back(grad, unit, scale, g2)
    grad_resid[0] = total
    grad_o = total.astype(BF16)
    grad_out[0] = grad_o
    vec[0, 0:1, :] = jnp.sum(grad_o.astype(F32), 0, keepdims=True)
    vec[0, 1:2, :] = jnp.sum(grad * unit, 0, keepdims=True)
    vec[0, 2:3, :] = jnp.sum(grad, 0, keepdims=True)
    vec[0, 3:4, :] = jnp.sum(cot, 0, keepdims=True)
    gm[0] = (mm(grad_o, wo[...], 1, 1).astype(BF16).astype(F32) * recip[0]).astype(BF16)


def resid_rows(row_arrays, weights, *tokens):
    rows, length, width = row_arrays[0].shape
    low = ((length, width), BF16)
    shapes = [low, ((length, width), F32), low, low, ((4, width), F32)]
    return pl.pallas_call(
        resid_kernel,
        grid=(rows,),
        in_specs=[IN_VMEM] * 2
        + [by_row(0, (length, width)) for _ in row_arrays[2:]]
        + [whole(w.shape) for w in weights]
        + [ANYWHERE] * len(tokens),
        out_specs=[by_row(0, s) for s, _ in shapes],
        out_shape=[
            (pltpu.VMEM if i in (2, 3) else pltpu.HBM)((rows,) + s, t) for i, (s, t) in enumerate(shapes)
        ],
        compiler_params=pltpu.CompilerParams(vmem_limit_bytes=24 * MIB),
        cost_estimate=long_cost(3),
        name="resid_rows",
    )(*in_vmem(row_arrays[:3]), *in_hbm(row_arrays[3:4]), *in_vmem(row_arrays[4:]), *in_hbm(weights), *tokens)


def back_kernel(count, offs, gm, x_own, seg_row, expo, wv, *rest):
    gv, gh_own, gh_send, vec_one, gmt, gvt, gh = rest[-7:]
    x_others = rest[:count]
    length = x_own.shape[1]
    heads = expo.shape[0]
    gmt[...] = gm[0].T
    mask = same_document(offs[0], seg_row, 0, length).astype(BF16)
    for head in range(heads):
        at = slice(64 * head, 64 * head + 64)
        gvt[at, :] = mm(gmt[at, :], expo[head] * mask, 1, 0).astype(BF16)
    values_grad = gvt[...].T
    gv[0] = values_grad
    gh[...] = mm(values_grad, wv[...], 1, 1)
    gain = jnp.zeros((1, gh.shape[1]), F32)
    x_other = x_others[0][0]
    for i, x in enumerate(x_others[1:]):
        x_other = jnp.where(pl.program_id(0) > i, x[0], x_other)
    for block, off in ((x_own[0], offs[0]), (x_other, offs[1])):
        unit, _ = unit_rows(block.astype(F32))
        gain += jnp.sum(gh[pl.ds(pl.multiple_of(off, length), length), :] * unit, 0, keepdims=True)
    vec_one[0, 0:1, :] = gain
    vec_one[0, 1:2, :] = jnp.sum(gh[...], 0, keepdims=True)
    vec_one[0, 2:3, :] = jnp.sum(values_grad.astype(F32), 0, keepdims=True)
    gh_own[0] = gh[pl.ds(pl.multiple_of(offs[0], length), length), :]
    gh_send[0] = gh[pl.ds(pl.multiple_of(offs[1], length), length), :].astype(BF16)


def back_rows(offs, gm, inputs, received, seg_row, expo, wv, *tokens):
    rows, length, width = inputs.shape
    full = seg_row.shape[2]
    shapes = [((full, width), BF16), ((length, width), F32), ((length, width), BF16), ((3, width), F32)]
    operands = [*in_vmem([gm]), *in_hbm([inputs, seg_row]), *in_vmem([expo, wv]), *received, *tokens]
    return pl.pallas_call(
        functools.partial(back_kernel, rows),
        grid_spec=pltpu.PrefetchScalarGridSpec(
            num_scalar_prefetch=1,
            grid=(rows,),
            in_specs=[by_row(0, (length, width))] * 2
            + [by_row(0, (1, full)), IN_VMEM, IN_VMEM]
            + [whole((1, length, width))] * rows
            + [ANYWHERE] * len(tokens),
            out_specs=[by_row(0, s) for s, _ in shapes],
            scratch_shapes=[
                pltpu.VMEM((width, length), BF16),
                pltpu.VMEM((width, full), BF16),
                pltpu.VMEM((full, width), F32),
            ],
        ),
        out_shape=[
            make((rows,) + s, t)
            for make, (s, t) in zip((pltpu.VMEM, pltpu.HBM, jax.ShapeDtypeStruct, pltpu.HBM), shapes)
        ],
        compiler_params=pltpu.CompilerParams(vmem_limit_bytes=32 * MIB),
        cost_estimate=long_cost(6),
        name="back_rows",
    )(offs, *operands)


def send_kernel(counts, *refs):
    out = refs[-1]
    start = 0
    for i, count in enumerate(counts):
        sum_of = refs[start][...].astype(F32)
        for part in refs[start + 1 : start + count]:
            sum_of = sum_of + part[...].astype(F32)
        start += count
        if len(counts) == 1:
            out[...] = sum_of.astype(BF16)
        else:
            out[i] = sum_of.astype(BF16)


def part_spec(part, dim, size, index):
    array, lead = part
    shape = array.shape if lead is None else array.shape[1:]
    shape = shape[:dim] + (size,) + shape[dim + 1 :]
    place = tuple(index if d == dim else 0 for d in range(len(shape)))
    if lead is None:
        return pl.BlockSpec(shape, lambda i, *_: place), shape
    return pl.BlockSpec((None,) + shape, lambda i, *_: (lead,) + place), shape


def send_sum(groups, dim, size, index, *tokens):
    parts = [p for group in groups for p in group]
    specs = [part_spec(p, dim, size, index) for p in parts]
    shape = specs[0][1]
    if len(groups) > 1:
        shape = (len(groups),) + shape
    return pl.pallas_call(
        functools.partial(send_kernel, [len(group) for group in groups]),
        grid=(1,),
        in_specs=[spec for spec, _ in specs] + [ANYWHERE] * len(tokens),
        out_specs=whole(shape),
        out_shape=jax.ShapeDtypeStruct(shape, BF16),
        compiler_params=pltpu.CompilerParams(vmem_limit_bytes=16 * MIB),
        cost_estimate=long_cost(0.2),
        name="send_sum",
    )(*[p for p, _ in parts], *tokens)


def logits_kernel(offs, gm, mixed, values, seg_row, expo, *rest):
    out, ones, masks = rest[-3:]
    step = pl.program_id(0)
    rows, length = gm.shape[:2]

    @pl.when(step == 0)
    def _():
        ones[:, 128:] = jnp.ones_like(ones[:, 128:])
        for row in range(rows):
            masks[row] = same_document(offs[0], seg_row, row, length)

    low_lane = lax.broadcasted_iota(jnp.int32, (length, 128), 1) < 64
    zero = jnp.zeros((length, 128), F32)
    sums = [None, None]
    for row in range(rows):
        ones[:, :128] = values[row]
        scaled = gm[row].astype(F32)
        product = scaled * mixed[row]
        high = product.astype(BF16).astype(F32)
        rest = product - high
        turned_rest = pltpu.roll(rest, 64, 1)
        left = []
        for head in range(2):
            keep = low_lane if head == 0 else jnp.logical_not(low_lane)
            left.append(
                jnp.concatenate(
                    [
                        jnp.where(keep, scaled, zero).astype(BF16),
                        (-jnp.where(keep, high, turned_rest)).astype(BF16),
                    ],
                    axis=1,
                )
            )
        both = mm(jnp.concatenate(left, 0), ones[...], 1, 1)
        for head in range(2):
            part = both[head * length : (head + 1) * length] * masks[row]
            sums[head] = part if sums[head] is None else sums[head] + part
    for head in range(2):
        grad = (expo[head].astype(F32) * sums[head]).astype(BF16).T
        blocks, _, size, _ = out.shape
        for j in range(blocks):
            out[turned(j, offs[3], blocks), head] = grad[j * size : (j + 1) * size, :]


def logits_grad(mine, offs, blocks, gm, mixed, values, seg_row, expo, *tokens):
    rows, length, width = gm.shape
    heads, _, full = expo.shape
    half = heads // 4
    pick = lambda i, offs: i + half * (offs[2] if mine else 1 - offs[2])
    shape = (blocks, heads // 2, full // blocks, length)
    return pl.pallas_call(
        logits_kernel,
        grid_spec=pltpu.PrefetchScalarGridSpec(
            num_scalar_prefetch=1,
            grid=(half,),
            in_specs=[
                pl.BlockSpec((rows, length, 128), lambda i, offs: (0, 0, pick(i, offs))),
                pl.BlockSpec((rows, length, 128), lambda i, offs: (0, 0, pick(i, offs))),
                pl.BlockSpec((rows, full, 128), lambda i, offs: (0, 0, pick(i, offs))),
                whole(seg_row.shape),
                pl.BlockSpec((2, length, full), lambda i, offs: (pick(i, offs), 0, 0)),
            ]
            + [ANYWHERE] * len(tokens),
            out_specs=pl.BlockSpec((blocks, 2, full // blocks, length), lambda i, offs: (0, i, 0, 0)),
            scratch_shapes=[pltpu.VMEM((full, 256), BF16), pltpu.VMEM((rows, length, full), F32)],
        ),
        out_shape=pltpu.HBM(shape, BF16) if mine else jax.ShapeDtypeStruct(shape, BF16),
        compiler_params=pltpu.CompilerParams(vmem_limit_bytes=32 * MIB),
        cost_estimate=long_cost(3),
        name="logits_grad",
    )(offs, *in_vmem([gm, mixed]), *in_hbm([values, seg_row]), *in_vmem([expo]), *tokens)


def square_kernel(at_ref, mixed, grad_o, h1, gv, bias, vec_two, vec_one, *rest):
    theirs, mine, out_sum, value_sum = rest[-4:]
    step = pl.program_id(0)
    out_part = mm(mixed[0].astype(BF16), grad_o[0], 0, 0)
    value_part = mm(h1[0], gv[0], 0, 0)

    @pl.when(step == 0)
    def _():
        out_sum[...] = out_part
        value_sum[...] = value_part

    @pl.when(step > 0)
    def _():
        out_sum[...] += out_part
        value_sum[...] += value_part

    @pl.when(step == pl.num_programs(0) - 1)
    def _():
        square_store(at_ref, out_sum, value_sum, bias, vec_two, vec_one, theirs, mine)


def square_store(at_ref, out_w, value_w, bias, vec_two, vec_one, theirs, mine):
    width = out_w.shape[1]
    rows = vec_two.shape[0]
    core, near, me = at_ref[0], at_ref[1], at_ref[2]
    blocks, chunks, size, _ = mine.shape
    size -= 8
    vectors = [sum(ref[r, i : i + 1, :] for r in range(rows)) for ref, n in ((vec_two, 4), (vec_one, 3)) for i in range(n)]
    share = 2 * width // (2 * blocks)
    part = width // 4
    own_rows = [jnp.where(core == a, bias[1:2, :], bias[0:1, :]) for a in range(2)]
    pad = lambda v: jnp.concatenate([v, jnp.zeros((1, width - v.shape[1]), F32)], 1)
    none = jnp.zeros((8, width), F32)
    for j in range(blocks):
        to = turned(j, near, blocks)
        for chunk in range(chunks):
            index = 2 * j + chunk // 2
            a, start = divmod(index * share, width)
            p, at = divmod(start, 2 * part)
            own = own_rows[a][:, start : start + share]
            row = bias[2 + p : 3 + p, :]
            first, second = row[:, at : at + share], row[:, width // 2 + at : width // 2 + at + share]
            other = jnp.where(core == a, first, second)
            hidden = jnp.where(me == chunk % 2, own, other)
            begin = (j * chunks + chunk) * size
            tail = [pad(v[:, begin : begin + size]) for v in vectors] + [pad(hidden)]
            here = slice(begin, begin + size)
            with_vectors = jnp.concatenate([out_w[here, :], *tail], 0).astype(BF16)
            without = jnp.concatenate([value_w[here, :], none], 0).astype(BF16)
            mine[to, chunk] = jnp.where(core == 0, with_vectors, without)
            theirs[to, chunk] = jnp.where(core == 0, without, with_vectors)


def square_grads(at, blocks, mixed, grad_o, h1, gv, *rest):
    rows, _, width = mixed.shape
    operands = (mixed, grad_o, h1, gv, *rest[:3])
    shape = (blocks, 4, width // (4 * blocks) + 8, width)
    return pl.pallas_call(
        square_kernel,
        grid_spec=pltpu.PrefetchScalarGridSpec(
            num_scalar_prefetch=1,
            grid=(rows,),
            in_specs=[by_row(0, a.shape[1:]) for a in operands[:4]]
            + [whole(a.shape) for a in operands[4:]]
            + [ANYWHERE] * len(rest[3:]),
            out_specs=[whole(shape)] * 2,
            scratch_shapes=[pltpu.VMEM((width, width), F32)] * 2,
        ),
        out_shape=[jax.ShapeDtypeStruct(shape, BF16), pltpu.HBM(shape, BF16)],
        compiler_params=pltpu.CompilerParams(vmem_limit_bytes=40 * MIB),
        cost_estimate=long_cost(4),
        name="square_grads",
    )(at, *in_vmem(operands[:2]), *in_hbm(operands[2:3]), *in_vmem(operands[3:4]), *in_hbm(operands[4:]), *rest[3:])


def partner_kernel(count, at_ref, *refs):
    keep, send = refs[-2:]
    me = at_ref[2]
    for core in range(2):
        for out, chunk in ((keep, 2 * core + me), (send, 2 * core + 1 - me)):
            sum_of = refs[0][0, chunk].astype(F32)
            for part in refs[1:count]:
                sum_of = sum_of + part[0, chunk].astype(F32)
            out[core] = sum_of.astype(out.dtype)


def partner_split(at, parts, *tokens):
    shape = (2,) + parts[0].shape[2:]
    block = (1,) + parts[0].shape[1:]
    return pl.pallas_call(
        functools.partial(partner_kernel, len(parts)),
        grid_spec=pltpu.PrefetchScalarGridSpec(
            num_scalar_prefetch=1,
            grid=(1,),
            in_specs=[whole(block)] * len(parts) + [ANYWHERE] * len(tokens),
            out_specs=[whole(shape)] * 2,
        ),
        out_shape=[jax.ShapeDtypeStruct(shape, F32), jax.ShapeDtypeStruct(shape, BF16)],
        compiler_params=pltpu.CompilerParams(vmem_limit_bytes=16 * MIB),
        cost_estimate=long_cost(0.01),
        name="partner_split",
    )(at, *in_hbm(parts[:1]), *parts[1:], *tokens)


def cover(*tokens):
    def kernel(*refs):
        refs[-1][...] = jnp.zeros_like(refs[-1])

    return pl.pallas_call(
        kernel,
        in_specs=[ANYWHERE] * len(tokens),
        out_specs=pl.BlockSpec((8, 128), lambda: (0, 0)),
        out_shape=TOKEN,
        compiler_params=pltpu.CompilerParams(vmem_limit_bytes=MIB),
        cost_estimate=long_cost(100),
        name="cover",
    )(*tokens)


def hold(a, *tokens):
    return pl.pallas_call(
        lambda *refs: None,
        in_specs=[ANYWHERE] * (1 + len(tokens)),
        out_specs=ANYWHERE,
        out_shape=pltpu.VMEM(a.shape, a.dtype),
        input_output_aliases={0: 0},
        compiler_params=pltpu.CompilerParams(vmem_limit_bytes=MIB),
        cost_estimate=long_cost(0.01),
        name="hold",
    )(*in_vmem([a]), *tokens)


def last_kernel(count, rows_first, at_ref, *refs):
    keep, send = refs[-2:]
    core = at_ref[0]
    sum_of = refs[0][...].astype(F32)
    for part in refs[1:count]:
        sum_of = sum_of + part[...].astype(F32)
    half = keep.shape[-2]
    shape = keep.shape
    low = sum_of[..., :half, :].reshape(shape)
    high = sum_of[..., half:, :].reshape(shape)
    keep[...] = jnp.where(core == 0, low, high)
    send[...] = jnp.where(core == 0, high, low).astype(BF16)


def last_split(at, parts, dim, rows, shape, *tokens):
    block = parts[0].shape[:dim] + (rows,) + parts[0].shape[dim + 1 :]
    return pl.pallas_call(
        functools.partial(last_kernel, len(parts), dim),
        grid_spec=pltpu.PrefetchScalarGridSpec(
            num_scalar_prefetch=1,
            grid=(1,),
            in_specs=[whole(block)] * len(parts) + [ANYWHERE] * len(tokens),
            out_specs=[whole(shape)] * 2,
        ),
        out_shape=[jax.ShapeDtypeStruct(shape, F32), jax.ShapeDtypeStruct(shape, BF16)],
        compiler_params=pltpu.CompilerParams(vmem_limit_bytes=16 * MIB),
        cost_estimate=long_cost(0.2),
        name="last_split",
    )(at, *in_hbm(parts[:1]), *parts[1:], *tokens)


def hidden_last_kernel(count, at_ref, *refs):
    keep, send = refs[-2:]
    core = at_ref[0]
    half = keep.shape[1]
    for which in range(2):
        sums = []
        for refs_of in (refs[:count], refs[count : 2 * count]):
            sum_of = refs_of[0][which].astype(F32)
            for p in refs_of[1:]:
                sum_of = sum_of + p[which].astype(F32)
            sums.append(sum_of)
        sum_of = jnp.concatenate(sums, 1)
        low, high = sum_of[:half], sum_of[half:]
        keep[which] = jnp.where(core == 0, low, high)
        send[which] = jnp.where(core == 0, high, low).astype(BF16)


def hidden_last(at, first, second, rows, width, *tokens):
    shape = (2, rows // 2, width)
    parts = [*first, *second]
    return pl.pallas_call(
        functools.partial(hidden_last_kernel, len(first)),
        grid_spec=pltpu.PrefetchScalarGridSpec(
            num_scalar_prefetch=1,
            grid=(1,),
            in_specs=[part_spec(p, 1, rows, 0)[0] for p in parts] + [ANYWHERE] * len(tokens),
            out_specs=[whole(shape)] * 2,
        ),
        out_shape=[jax.ShapeDtypeStruct(shape, F32), jax.ShapeDtypeStruct(shape, BF16)],
        compiler_params=pltpu.CompilerParams(vmem_limit_bytes=16 * MIB),
        cost_estimate=long_cost(0.2),
        name="hidden_last",
    )(at, *[p for p, _ in parts], *tokens)


def hidden_out_kernel(at_ref, kept, got, *rest):
    up, down = rest[-2:]
    core = at_ref[0]
    for which, out in ((0, up), (1, down)):
        mine, theirs = kept[which], got[which].astype(F32)
        out[...] = jnp.concatenate([jnp.where(core == 0, mine, theirs), jnp.where(core == 0, theirs, mine)], 1)


def logit_out_kernel(at_ref, kept, got, *rest):
    out = rest[-1]
    core = at_ref[0]
    half = kept.shape[0]
    mine, theirs = kept[...], got[...].astype(F32)
    out[:half] = jnp.where(core == 0, mine, theirs)
    out[half:] = jnp.where(core == 0, theirs, mine)


def square_out_kernel(at_ref, kept, got, *rest):
    out_w, value_w, up_bias, *vectors = rest[-10:]
    core = at_ref[0]
    size = out_w.shape[0]
    mine, theirs = kept[...], got[...].astype(F32)
    first = jnp.where(core == 0, mine, theirs)
    second = jnp.where(core == 0, theirs, mine)
    out_w[...] = first[:size]
    value_w[...] = second[:size]
    for i, v in enumerate(vectors):
        v[...] = first[size + i : size + i + 1, :size]
    up_bias[...] = first[size + 7 : size + 8, : up_bias.shape[1]]


def finish(kernel, at, kept, got, shapes, *tokens):
    return pl.pallas_call(
        kernel,
        grid_spec=pltpu.PrefetchScalarGridSpec(
            num_scalar_prefetch=1,
            grid=(1,),
            in_specs=[whole(kept.shape), whole(got.shape)] + [ANYWHERE] * len(tokens),
            out_specs=[whole(s) for s in shapes],
        ),
        out_shape=[pltpu.HBM(s, F32) for s in shapes],
        compiler_params=pltpu.CompilerParams(vmem_limit_bytes=16 * MIB),
        cost_estimate=long_cost(0.2),
        name="finish",
    )(at, kept, got, *tokens)


def input_kernel(x, grad_resid, gh_own, gh_received, small, *rest):
    grad, token = rest[-2:]
    token[...] = jnp.zeros_like(token)
    unit, scale = unit_rows(x[0].astype(F32))
    total = gh_own[0] + gh_received[0].astype(F32)
    grad[0] = grad_resid[0] + norm_back(total, unit, scale, small[0:1, :])


def input_rows(inputs, grad_resid, gh_own, gh_received, small, *tokens):
    rows, length, width = inputs.shape
    return pl.pallas_call(
        input_kernel,
        grid=(rows,),
        in_specs=[by_row(0, (length, width))] * 4 + [whole(small.shape)] + [ANYWHERE] * len(tokens),
        out_specs=[by_row(0, (length, width)), whole((8, 128))],
        out_shape=[pltpu.HBM((rows, length, width), F32), TOKEN],
        compiler_params=pltpu.CompilerParams(vmem_limit_bytes=24 * MIB),
        cost_estimate=long_cost(0.5),
        name="input_rows",
    )(*in_hbm([inputs, grad_resid, gh_own]), gh_received, *in_hbm([small]), *tokens)


def swap(a, axis, size, bit):
    return lax.ppermute(a, axis, [(i, i ^ bit) for i in range(size)])


class Scatter:
    def __init__(self, groups, dim, size):
        self.groups = [[p if isinstance(p, tuple) else (p, None) for p in parts] for parts in groups]
        array, lead = self.groups[0][0]
        self.dim, self.size, self.step = dim, size, 1
        self.rows = array.shape[dim + (lead is not None)]

    def send(self, *tokens):
        self.rows //= 2
        out = send_sum(self.groups, self.dim, self.rows, 1, *tokens)
        self.add(swap(out, "dp", self.size, 1 << self.step))
        self.step += 1
        return out

    def add(self, received):
        self.latest = received
        for i, parts in enumerate(self.groups):
            parts.append((received, i if len(self.groups) > 1 else None))

    def split(self):
        return [Part([parts], self) for parts in self.groups]

    def arrays(self):
        return [p for p, _ in self.groups[0]]


class Part(Scatter):
    def __init__(self, groups, whole):
        self.groups = groups
        self.dim, self.size, self.step, self.rows = whole.dim, whole.size, whole.step, whole.rows


def paired_shards(
    dp,
    mp,
    inputs,
    segment_ids,
    ln1_gain,
    ln1_bias,
    value_weight,
    value_bias,
    random_logits,
    out_weight,
    out_bias,
    ln2_gain,
    ln2_bias,
    up_weight,
    up_bias,
    down_weight,
    down_bias,
    out_cotangent,
):
    rows, length, width = inputs.shape
    heads = random_logits.shape[0]
    full = segment_ids.shape[1]
    positions = rows * length
    hidden = up_weight.shape[1]
    tile = hidden // 2
    me = lax.axis_index("mp")
    place = lax.axis_index("dp")
    bits = dp.bit_length() - 1
    bit = [lax.rem(lax.div(place, 1 << b), 2) for b in range(bits)]
    core = bit[0]
    near = lax.shift_right_logical(place, 1)
    blocks = dp // 2
    at = jnp.stack([core, near, me]).astype(jnp.int32)
    offs = jnp.stack([me * length, (1 - me) * length, core, near]).astype(jnp.int32)
    quarter = jnp.stack([2 * core, 2 * core + 1, bit[1]]).astype(jnp.int32)
    by_core = lambda first, second: jnp.where(core == 0, first, second)
    small, up_row = prep(
        [ln1_gain, ln1_bias, ln2_gain, ln2_bias, value_bias, out_bias, down_bias], up_bias
    )

    received = [swap(inputs[r : r + 1], "mp", mp, 1) for r in range(rows)]
    expo = jnp.exp(random_logits.astype(F32)).astype(BF16)
    seg_row = segment_ids[:, None, :]
    g = out_cotangent.reshape(positions, width)

    chain = None
    packed = []
    for r in range(rows):
        chain = mix_rows(
            r,
            1,
            offs,
            blocks,
            inputs,
            received[r],
            out_cotangent,
            seg_row,
            expo,
            (value_weight, out_weight, small),
            chain,
            *packed[-1:],
        )
        if 1 <= r <= 2:
            packed.append(pack(r - 1, quarter, up_weight, down_weight, up_row, chain[-1]))
    h1, values, recip, mixed, resid, h2, h2t, gt, _ = chain
    h2 = h2.reshape(positions, width)
    h2t = h2t.reshape(width, positions)
    gt = gt.reshape(width, positions)

    def fetch(by_x):
        by_y = swap(by_x, "dp", dp, 2)
        return by_x, by_y

    def share(by_x, by_y):
        return by_x, by_y, swap(by_x, "dp", dp, 1), swap(by_y, "dp", dp, 1)

    by_x = [swap(message, "mp", mp, 1) for message in packed]
    fixed = (h2, g, h2t, gt)
    tiles = [(1 - core).reshape(1).astype(jnp.int32), core.reshape(1).astype(jnp.int32)]
    *sums, own_theirs, bias, token = own_hidden(tiles[0], fixed, up_weight, up_row, down_weight, None)
    fetched = [fetch(hold(by_x[0], token))]
    *sums, own_mine, bias, token = own_hidden(
        tiles[1], fixed, up_weight, up_row, down_weight, (*sums, bias), fetched[0][0]
    )
    fetched.append(fetch(hold(by_x[1], token)))
    own_received = swap(own_theirs, "dp", dp, 1)
    own = Scatter([[(own_mine, i), (own_received, i)] for i in range(2)], 1, dp)
    near_y = jnp.stack([bit[1], core]).astype(jnp.int32)
    *sums, mine, theirs, bias, token = other_hidden(
        0, near_y, fixed, share(fetched[0][0], hold(fetched[0][1], token)), (*sums, bias)
    )
    others = [Scatter([[mine, swap(theirs, "dp", dp, 1)]], 1, dp)]
    sent = own.send(token)
    out, dh, mine, theirs, bias, token = other_hidden(
        1, near_y, fixed, share(fetched[1][0], hold(fetched[1][1], sent)), (*sums, bias), sent
    )
    others.append(Scatter([[mine, swap(theirs, "dp", dp, 1)]], 1, dp))
    token = others[0].send(token)

    shape = (rows, length, width)
    layer_out, grad_resid, grad_o, gm, vec_two = resid_rows(
        [out.reshape(shape), dh.reshape(shape), resid, out_cotangent, recip], (out_weight, small), token
    )
    token = others[1].send(vec_two)
    def to_partner(other, token):
        sent = send_sum(other.groups, 1, other.rows, 0, token)
        return sent, swap(sent, "mp", mp, 1)

    gv, gh_own, gh_sent, vec_one = back_rows(offs, gm, inputs, received, seg_row, expo, value_weight, token)
    token, arrived = to_partner(others[0], gh_sent)
    own = own.split()
    own[0].add(arrived)
    square_theirs, square_mine = square_grads(
        at,
        blocks,
        mixed,
        grad_o,
        h1,
        gv,
        bias,
        vec_two,
        vec_one,
        token,
    )

    square = Scatter([[square_mine, swap(square_theirs, "dp", dp, 1)]], 0, dp)
    token = cover(square_mine, others[1].latest)
    token, arrived = to_partner(others[1], token)
    own[1].add(arrived)
    token = own[0].send(token)
    token = square.send(token)
    gh_sent = hold(gh_sent, token)
    gh_received = swap(gh_sent, "mp", mp, 1)
    grads = (offs, blocks, gm, mixed, values, seg_row, expo)
    logits_theirs = logits_grad(False, *grads, gh_sent)
    token = own[0].send(logits_theirs)
    logits_mine = logits_grad(True, *grads, token)
    logit = Scatter([[logits_mine, swap(logits_theirs, "dp", dp, 1)]], 0, dp)
    token = logit.send(logits_mine, own[0].latest)
    token = square.send(token)
    token = own[1].send(token)
    token = square.send(token)
    token = logit.send(token)
    token = own[1].send(token)
    grad_inputs, token = input_rows(inputs, grad_resid, gh_own, gh_received, small, token)
    square_kept, token = partner_split(at, square.arrays(), token)
    square_received = swap(token, "mp", mp, 1)
    token = logit.send(token)
    kept, token = hidden_last(at, own[0].groups[0], own[1].groups[0], own[0].rows, tile, token)
    hidden_received = swap(token, "dp", dp, 1)
    chunk = square_mine.shape[2]
    square_parts = [p.reshape(2 * chunk, width) for p in (square_kept, square_received)]
    square_kept, token = last_split(at, square_parts, 0, 2 * chunk, (chunk, width), token)
    square_received = swap(token, "dp", dp, 1)
    up_part, down_part = finish(
        hidden_out_kernel, at, kept, hidden_received, [(width // dp, hidden)] * 2, token
    )
    part_size = width // (dp * mp)
    out_part, value_part, up_bias_part, *vector = finish(
        square_out_kernel,
        at,
        square_kept,
        square_received,
        [(part_size, width), (part_size, width), (1, hidden // dp)] + [(1, part_size)] * 7,
        up_part,
    )
    logit_kept, token = last_split(at, logit.arrays(), 0, 1, (heads // 2, full // dp, length), out_part)
    logit_received = swap(token, "dp", dp, 1)
    (logit_part,) = finish(
        logit_out_kernel, at, logit_kept, logit_received, [(heads, full // dp, length)]
    )
    bo_part, g2_part, b2_part, bd_part, g1_part, b1_part, bv_part = (v.reshape(-1) for v in vector)
    return (
        layer_out,
        grad_inputs,
        g1_part,
        b1_part,
        value_part,
        bv_part,
        logit_part.transpose(0, 2, 1),
        out_part,
        bo_part,
        g2_part,
        b2_part,
        up_part,
        up_bias_part,
        down_part.T,
        bd_part,
    )


def smooth(t):
    return jax.nn.gelu(t, approximate=True)


def contract_rows(left, right):
    return lax.dot_general(
        left, right, (((0,), (0,)), ((), ())), preferred_element_type=jnp.float32
    )


def contract_cols(left, right):
    return lax.dot_general(
        left, right, (((1,), (1,)), ((), ())), preferred_element_type=jnp.float32
    )


def normalize(x, gain, shift):
    centred = x - jnp.mean(x, -1, keepdims=True)
    scale = lax.rsqrt(jnp.mean(centred * centred, -1, keepdims=True) + 1e-05)
    unit = centred * scale
    return (unit * gain + shift, unit, scale)


def normalize_back(grad, unit, scale, gain):
    scaled = grad * gain
    inner = scale * (
        scaled
        - jnp.mean(scaled, -1, keepdims=True)
        - unit * jnp.mean(scaled * unit, -1, keepdims=True)
    )
    return (inner, jnp.sum(grad * unit, 0), jnp.sum(grad, 0))


def shards(
    inputs,
    segment_ids,
    ln1_gain,
    ln1_bias,
    value_weight,
    value_bias,
    random_logits,
    out_weight,
    out_bias,
    ln2_gain,
    ln2_bias,
    up_weight,
    up_bias,
    down_weight,
    down_bias,
    out_cotangent,
):
    seqs, local_len, width = inputs.shape
    heads = random_logits.shape[0]
    full_len = segment_ids.shape[1]
    head_dim = width // heads
    rows = seqs * local_len
    gain_one = ln1_gain.astype(jnp.float32)
    gain_two = ln2_gain.astype(jnp.float32)
    start_x = inputs.astype(jnp.float32).reshape(rows, width)
    normed_one, unit_one, scale_one = normalize(start_x, gain_one, ln1_bias.astype(jnp.float32))
    h1_low = normed_one.astype(jnp.bfloat16)
    values = (
        jnp.dot(h1_low, value_weight, preferred_element_type=jnp.float32)
        + value_bias.astype(jnp.float32)
    ).astype(jnp.bfloat16)
    gathered = lax.all_gather(values.reshape(seqs, local_len, width), "mp", axis=1, tiled=True)
    every_head = gathered.reshape(seqs, full_len, heads, head_dim)
    offset = lax.axis_index("mp") * local_len
    own_segs = lax.dynamic_slice_in_dim(segment_ids, offset, local_len, 1)
    same = own_segs[:, :, None] == segment_ids[:, None, :]
    scores = jnp.where(same[:, None], random_logits.astype(jnp.float32)[None], -1e30)
    peak = jnp.max(scores, -1, keepdims=True)
    expo = jnp.exp(scores - peak)
    total = jnp.sum(expo, -1, keepdims=True)
    probs = expo / total
    probs_low = probs.astype(jnp.bfloat16)
    mixed = jnp.einsum("shqk,skhd->sqhd", probs_low, every_head, preferred_element_type=jnp.float32)
    mixed_low = mixed.reshape(rows, width).astype(jnp.bfloat16)
    resid = (
        start_x
        + jnp.dot(mixed_low, out_weight, preferred_element_type=jnp.float32)
        + out_bias.astype(jnp.float32)
    )
    normed_two, unit_two, scale_two = normalize(resid, gain_two, ln2_bias.astype(jnp.float32))
    h2_low = normed_two.astype(jnp.bfloat16)
    grad_low = out_cotangent.reshape(rows, width)
    h2_full = lax.all_gather(
        h2_low.reshape(seqs, local_len, width), "mp", axis=1, tiled=True
    ).reshape(seqs * full_len, width)
    pre = jnp.dot(h2_full, up_weight, preferred_element_type=jnp.float32) + up_bias.astype(
        jnp.float32
    )
    act, gelu_pull = jax.vjp(smooth, pre)
    act_low = act.astype(jnp.bfloat16)
    partial_out = jnp.dot(act_low, down_weight, preferred_element_type=jnp.float32).reshape(
        seqs, full_len, width
    )
    ffn_out = lax.psum_scatter(
        partial_out.astype(jnp.bfloat16), "mp", scatter_dimension=1, tiled=True
    ).astype(jnp.float32).reshape(rows, width) + down_bias.astype(jnp.float32)
    final = resid + ffn_out
    grad_full = lax.all_gather(out_cotangent, "mp", axis=1, tiled=True).reshape(
        seqs * full_len, width
    )
    grad_down = contract_rows(act_low, grad_full)
    grad_act = contract_cols(grad_full, down_weight)
    grad_pre = gelu_pull(grad_act)[0].astype(jnp.bfloat16)
    grad_up_b = jnp.sum(grad_pre.astype(jnp.float32), 0)
    grad_up = contract_rows(h2_full, grad_pre)
    h2_terms = contract_cols(grad_pre, up_weight).reshape(seqs, full_len, width)
    grad_h2 = (
        lax.psum_scatter(h2_terms.astype(jnp.bfloat16), "mp", scatter_dimension=1, tiled=True)
        .astype(jnp.float32)
        .reshape(rows, width)
    )
    grad_final = grad_low.astype(jnp.float32)
    grad_down_b = jnp.sum(grad_final, 0)
    inner_two, gain_two_grad, shift_two_grad = normalize_back(
        grad_h2, unit_two, scale_two, gain_two
    )
    grad_resid = grad_final + inner_two
    grad_o_low = grad_resid.astype(jnp.bfloat16)
    grad_out_b = jnp.sum(grad_o_low.astype(jnp.float32), 0)
    grad_out_w = contract_rows(mixed_low, grad_o_low)
    grad_mixed = (
        contract_cols(grad_o_low, out_weight)
        .astype(jnp.bfloat16)
        .reshape(seqs, local_len, heads, head_dim)
    )
    grad_probs = jnp.einsum(
        "sqhd,skhd->shqk", grad_mixed, every_head, preferred_element_type=jnp.float32
    )
    grad_scores = probs * (grad_probs - jnp.sum(probs * grad_probs, -1, keepdims=True))
    grad_logits = jnp.sum(grad_scores, 0)
    value_terms = jnp.einsum(
        "shqk,sqhd->skhd", probs_low, grad_mixed, preferred_element_type=jnp.float32
    ).reshape(seqs, full_len, width)
    grad_values = (
        lax.psum_scatter(value_terms.astype(jnp.bfloat16), "mp", scatter_dimension=1, tiled=True)
        .astype(jnp.float32)
        .reshape(rows, width)
        .astype(jnp.bfloat16)
    )
    grad_value_b = jnp.sum(grad_values.astype(jnp.float32), 0)
    grad_value_w = contract_rows(h1_low, grad_values)
    inner_one, gain_one_grad, shift_one_grad = normalize_back(
        contract_cols(grad_values, value_weight), unit_one, scale_one, gain_one
    )
    grad_x = (grad_resid + inner_one).reshape(seqs, local_len, width)
    vectors = jnp.stack(
        [
            gain_one_grad,
            shift_one_grad,
            grad_value_b,
            grad_out_b,
            gain_two_grad,
            shift_two_grad,
            grad_down_b,
        ]
    )
    value_w_part, out_w_part, vector_part = (
        lax.psum_scatter(grad_value_w, ("dp", "mp"), scatter_dimension=0, tiled=True),
        lax.psum_scatter(grad_out_w, ("dp", "mp"), scatter_dimension=0, tiled=True),
        lax.psum_scatter(vectors, ("dp", "mp"), scatter_dimension=1, tiled=True),
    )
    up_part, up_b_part, down_part, logit_part = (
        lax.psum_scatter(
            grad_up.astype(jnp.bfloat16), "dp", scatter_dimension=0, tiled=True
        ).astype(jnp.float32),
        lax.psum_scatter(
            grad_up_b[None].astype(jnp.bfloat16), "dp", scatter_dimension=1, tiled=True
        ).astype(jnp.float32),
        lax.psum_scatter(
            grad_down.astype(jnp.bfloat16), "dp", scatter_dimension=1, tiled=True
        ).astype(jnp.float32),
        lax.psum_scatter(
            grad_logits.astype(jnp.bfloat16), "dp", scatter_dimension=2, tiled=True
        ).astype(jnp.float32),
    )
    return (
        final.astype(jnp.bfloat16).reshape(seqs, local_len, width),
        grad_x,
        vector_part[0],
        vector_part[1],
        value_w_part,
        vector_part[2],
        logit_part,
        out_w_part,
        vector_part[3],
        vector_part[4],
        vector_part[5],
        up_part,
        up_b_part,
        down_part,
        vector_part[6],
    )


def solution(mesh):
    in_specs = (
        P("dp", "mp", None),
        P("dp", None),
        P(),
        P(),
        P(),
        P(),
        P(None, "mp", None),
        P(),
        P(),
        P(),
        P(),
        P(None, "mp"),
        P("mp"),
        P("mp", None),
        P(),
        P("dp", "mp", None),
    )
    out_specs = (
        P("dp", "mp", None),
        P("dp", "mp", None),
        P(("dp", "mp")),
        P(("dp", "mp")),
        P(("dp", "mp"), None),
        P(("dp", "mp")),
        P(None, "mp", "dp"),
        P(("dp", "mp"), None),
        P(("dp", "mp")),
        P(("dp", "mp")),
        P(("dp", "mp")),
        P("dp", "mp"),
        P("mp", "dp"),
        P("mp", "dp"),
        P(("dp", "mp")),
    )
    dp, mp = mesh.shape["dp"], mesh.shape["mp"]
    body = functools.partial(paired_shards, dp, mp) if mp == 2 else shards
    return jax.shard_map(body, mesh=mesh, in_specs=in_specs, out_specs=out_specs, check_vma=False)
```

```python
import functools

import jax
import jax.numpy as jnp
from jax import lax
from jax.experimental import pallas as pl
from jax.experimental.pallas import tpu as pltpu
from jax.sharding import PartitionSpec as P

F32 = jnp.float32
BF16 = jnp.bfloat16
GELU_A = 0.7978845608028654
GELU_B = GELU_A * 0.044715
MIB = 2**20


def mm(left, right, left_dim, right_dim):
    return lax.dot_general(
        left, right, (((left_dim,), (right_dim,)), ((), ())), preferred_element_type=F32
    )


def unit_rows(x):
    centred = x - jnp.mean(x, -1, keepdims=True)
    scale = lax.rsqrt(jnp.mean(centred * centred, -1, keepdims=True) + 1e-05)
    return centred * scale, scale


def norm_back(grad, unit, scale, gain):
    e = grad * gain
    return scale * (
        e - jnp.mean(e, -1, keepdims=True) - unit * jnp.mean(e * unit, -1, keepdims=True)
    )


def same_document(first, seg_row, row, length):
    keys = seg_row[row].astype(F32)
    own = seg_row[row, :, pl.ds(pl.multiple_of(first, length), length)].astype(F32)
    queries = jnp.broadcast_to(own, (8, length)).T[:, :1]
    return jnp.where(queries == keys, 1.0, 0.0)


def turned(block, near, blocks):
    other = jnp.bitwise_xor(block, near)
    place = 0
    weight = blocks
    for b in range(blocks.bit_length() - 1):
        weight //= 2
        place = place + jnp.bitwise_and(lax.shift_right_logical(other, b), 1) * weight
    return place


def long_cost(us):
    return pl.CostEstimate(flops=int(us * 10**10), bytes_accessed=10**5, transcendentals=0)


IN_VMEM = pl.BlockSpec(memory_space=pltpu.VMEM)
ANYWHERE = pl.BlockSpec(memory_space=pl.ANY)


def in_hbm(operands):
    return [pltpu.with_memory_space_constraint(a, pltpu.HBM) for a in operands]


def in_vmem(operands):
    return [pltpu.with_memory_space_constraint(a, pltpu.VMEM) for a in operands]


TOKEN = pltpu.HBM((8, 128), F32)


def whole(shape):
    return pl.BlockSpec(shape, lambda i, *_: (0,) * len(shape))


def by_row(first, shape):
    return pl.BlockSpec((1,) + shape, lambda i, *_: (first + i,) + (0,) * len(shape))


def prep_kernel(*refs):
    *vectors, bias, small, hidden = refs
    for i, v in enumerate(vectors):
        small[i : i + 1, :] = v[...].astype(F32).reshape(1, -1)
    hidden[...] = bias[...].astype(F32).reshape(1, -1)


def prep(vectors, bias):
    return pl.pallas_call(
        prep_kernel,
        in_specs=[IN_VMEM] * (len(vectors) + 1),
        out_specs=[IN_VMEM] * 2,
        out_shape=[
            pltpu.HBM((8, vectors[0].shape[0]), F32),
            pltpu.HBM((1, bias.shape[0]), F32),
        ],
        name="prep",
    )(*vectors, bias)


def mix_kernel(offs, x_own, x_other, g, seg_row, expo, wv, wo, small, *rest):
    h1, values, recip, mixed, resid, h2, h2t, gt, token, ones = rest[-10:]
    g1, b1, g2, b2, bv, bo, _ = (small[i : i + 1, :] for i in range(7))
    token[...] = jnp.zeros_like(token)
    length = x_own.shape[1]
    heads = expo.shape[0]
    ones[:, 128:] = jnp.ones_like(ones[:, 128:])
    x = x_own[0].astype(F32)
    for block, off in ((x, offs[0]), (x_other[0].astype(F32), offs[1])):
        unit, _ = unit_rows(block)
        at = pl.ds(pl.multiple_of(off, length), length)
        h1[0, at, :] = (unit * g1 + b1).astype(BF16)
    values[0] = (mm(h1[0], wv[...], 1, 0) + bv).astype(BF16)
    mask = same_document(offs[0], seg_row, 0, length).astype(BF16)
    low_lane = lax.broadcasted_iota(jnp.int32, (length, 128), 1) < 64
    for pair in range(heads // 2):
        lanes = slice(128 * pair, 128 * pair + 128)
        ones[:, :128] = values[0, :, lanes]
        first = mm(expo[2 * pair] * mask, ones[...], 1, 0)
        second = mm(expo[2 * pair + 1] * mask, ones[...], 1, 0)
        inverse = 1.0 / jnp.where(low_lane, first[:, 128:], second[:, 128:])
        recip[0, :, lanes] = inverse.astype(BF16)
        both = jnp.where(low_lane, first[:, :128], second[:, :128]) * inverse
        mixed[0, :, lanes] = both.astype(BF16)
    r = x + mm(mixed[0], wo[...], 1, 0) + bo
    resid[0] = r
    unit, _ = unit_rows(r)
    low = (unit * g2 + b2).astype(BF16)
    h2[0] = low
    blocks, size, _ = h2t.shape
    for ref, source in ((h2t, low.T), (gt, g[0].T)):
        for j in range(blocks):
            ref[turned(j, offs[3], blocks)] = source[j * size : (j + 1) * size, :]


def mix_rows(first, count, offs, blocks, inputs, received, cotangent, seg_row, expo, weights, chain, *tokens):
    rows, length, width = inputs.shape
    full = seg_row.shape[2]
    heads = expo.shape[0]
    shapes = [
        ((full, width), BF16),
        ((full, width), BF16),
        ((length, width), BF16),
        ((length, width), BF16),
        ((length, width), F32),
        ((length, width), BF16),
    ]
    out_specs = [by_row(first, s) for s, _ in shapes]
    turned_spec = pl.BlockSpec((blocks, width // blocks, length), lambda i, *_: (0, 0, first + i))
    out_specs += [turned_spec] * 2
    out_shape = [pltpu.HBM((rows,) + s, t) for s, t in shapes[:4]]
    out_shape += [pltpu.VMEM((rows,) + s, t) for s, t in shapes[4:]]
    out_shape += [pltpu.VMEM((blocks, width // blocks, rows * length), BF16)] * 2
    operands = [offs, *in_hbm([inputs]), received, *in_hbm([cotangent, seg_row]), *in_vmem([expo, *weights])]
    in_specs = [
        by_row(first, (length, width)),
        by_row(0, (length, width)),
        by_row(first, (length, width)),
        by_row(first, (1, full)),
        *[IN_VMEM] * (1 + len(weights)),
    ]
    aliases = {}
    if chain is not None:
        aliases = {len(operands) + i: i for i in range(len(out_shape))}
        operands += [*in_hbm(chain[:4]), *in_vmem(chain[4:8])]
        in_specs += [ANYWHERE] * len(out_shape)
    operands += tokens
    in_specs += [ANYWHERE] * len(tokens)
    out_specs.append(whole((8, 128)))
    out_shape.append(TOKEN)
    return pl.pallas_call(
        mix_kernel,
        grid_spec=pltpu.PrefetchScalarGridSpec(
            num_scalar_prefetch=1,
            grid=(count,),
            in_specs=in_specs,
            out_specs=out_specs,
            scratch_shapes=[pltpu.VMEM((full, 256), BF16)],
        ),
        out_shape=out_shape,
        input_output_aliases=aliases,
        compiler_params=pltpu.CompilerParams(vmem_limit_bytes=32 * MIB),
        cost_estimate=long_cost(3 * count),
        name="mix_rows",
    )(*operands)


def gelu_pair(t):
    square = t * t
    curve = jnp.tanh(t * (GELU_A + GELU_B * square))
    half = 0.5 + 0.5 * curve
    act = t * half
    return act, half + act * (1.0 - curve) * (GELU_A + 3 * GELU_B * square)


def hidden_tile(h2, g, h2t, gt, wu, up_dim, bu, wd, sums, outs, act_s, pre_s, block):
    out0, dh0 = sums if sums else (None, None)
    out, dh = outs
    total = None
    for m in range(h2.shape[0] // block):
        at = pl.ds(m * block, block)
        pre = mm(h2[at, :], wu[...], 1, up_dim) + bu
        grad_act = mm(g[at, :], wd[...], 1, 1)
        act, slope = gelu_pair(pre)
        act_low = act.astype(BF16)
        grad_pre = grad_act * slope
        part = jnp.sum(grad_pre, 0, keepdims=True)
        total = part if total is None else total + part
        pre_low = grad_pre.astype(BF16)
        act_s[at, :] = act_low
        pre_s[at, :] = pre_low
        out_part = mm(act_low, wd[...], 1, 0)
        dh_part = mm(pre_low, wu[...], 1, 1 - up_dim)
        out[at, :] = out_part if sums is None else out0[at, :] + out_part
        dh[at, :] = dh_part if sums is None else dh0[at, :] + dh_part
    return total, lambda: (
        mm(h2t[...], pre_s[...], 1, 0).astype(BF16),
        mm(gt[...], act_s[...], 1, 0).astype(BF16),
    )


def own_hidden_kernel(block, first, at_ref, h2, g, h2t, gt, wu, bu, wd, *rest):
    out, dh, grads, bias, token, act_s, pre_s = rest[-7:]
    token[...] = jnp.zeros_like(token)
    sums = None
    if not first:
        out0, dh0, bias0 = rest[:3]
        sums = (out0, dh0)
    total, weights = hidden_tile(
        h2, g, h2t, gt, wu, 0, bu[...].astype(F32), wd, sums, (out, dh), act_s, pre_s, block
    )
    if first:
        bias[0:1, :] = total
    else:
        bias[...] = bias0[...]
        bias[1:2, :] = total
    half = grads.shape[3]
    for which, grad in enumerate(weights()):
        for p in range(2):
            grads[p, which] = grad[:, p * half : (p + 1) * half]


def other_hidden_kernel(block, which, near, h2, g, h2t, gt, wx, wy, wcx, wcy, out0, dh0, bias0, *rest):
    out, dh, mine, theirs, bias, token, wu, wd, act_s, pre_s = rest[-10:]
    token[...] = jnp.zeros_like(token)
    near_y = near[0]
    part = wx.shape[0] // 2 - 8
    for first, pieces in ((0, (wx, wy)), (2, (wcx, wcy))):
        for turn, piece in enumerate(pieces):
            quarter = first + jnp.bitwise_xor(near_y, turn)
            at = pl.ds(pl.multiple_of(quarter * part, part), part)
            wu[at, :] = piece[:part, :]
            wd[at, :] = piece[part : 2 * part, :]
    rows = wx[2 * part :, :].astype(F32)
    lanes = slice(2 * part * which, 2 * part * (which + 1))
    lower, upper = rows[0:1, lanes], rows[1:2, lanes]
    swapped = near[1] == 1
    bu = jnp.concatenate([jnp.where(swapped, upper, lower), jnp.where(swapped, lower, upper)], axis=1)
    total, weights = hidden_tile(
        h2, g, h2t, gt, wu, 1, bu, wd, (out0, dh0), (out, dh), act_s, pre_s, block
    )
    bias[...] = bias0[...]
    bias[2 + which : 3 + which, :] = total
    half = 2 * part
    for index, grad in enumerate(weights()):
        mine[index] = grad[:, :half]
        theirs[index] = grad[:, half:]


def hidden_call(positions, width, tile):
    return dict(
        compiler_params=pltpu.CompilerParams(vmem_limit_bytes=19 * MIB),
        cost_estimate=long_cost(5),
    )


def own_hidden(tile_at, fixed, wu, bu, wd, sums, *tokens):
    positions, width = fixed[0].shape
    tile = wu.shape[1] // 2
    operands = [*in_vmem(fixed), *in_hbm([wu, bu, wd]), *in_vmem(sums or ()), *tokens]
    aliases = {1 + len(fixed) + 3: 0, 1 + len(fixed) + 4: 1} if sums else {}
    weights = [
        pl.BlockSpec((width, tile), lambda i, at: (0, at[0])),
        pl.BlockSpec((1, tile), lambda i, at: (0, at[0])),
        pl.BlockSpec((tile, width), lambda i, at: (at[0], 0)),
    ]
    return pl.pallas_call(
        functools.partial(own_hidden_kernel, 256, sums is None),
        grid_spec=pltpu.PrefetchScalarGridSpec(
            num_scalar_prefetch=1,
            grid=(1,),
            in_specs=[IN_VMEM] * len(fixed) + weights + [IN_VMEM] * len(sums or ()) + [ANYWHERE] * len(tokens),
            out_specs=[IN_VMEM] * 2 + [whole((2, 2, width, tile // 2)), IN_VMEM, whole((8, 128))],
            scratch_shapes=[pltpu.VMEM((positions, tile), BF16)] * 2,
        ),
        out_shape=[pltpu.VMEM((positions, width), F32)] * 2
        + [pltpu.HBM((2, 2, width, tile // 2), BF16), pltpu.VMEM((8, tile), F32), TOKEN],
        input_output_aliases=aliases,
        name="own_hidden",
        **hidden_call(positions, width, tile),
    )(tile_at, *operands)


def other_hidden(which, near, fixed, pieces, sums, *tokens):
    positions, width = fixed[0].shape
    tile = 4 * (pieces[0].shape[0] // 2 - 8)
    operands = [*in_vmem(fixed), *pieces, *in_vmem(sums)]
    aliases = {1 + len(operands) - 3: 0, 1 + len(operands) - 2: 1}
    block = whole((2, width, tile // 2))
    return pl.pallas_call(
        functools.partial(other_hidden_kernel, 256, which),
        grid_spec=pltpu.PrefetchScalarGridSpec(
            num_scalar_prefetch=1,
            grid=(1,),
            in_specs=[IN_VMEM] * 4 + [whole(p.shape) for p in pieces] + [IN_VMEM] * 3 + [ANYWHERE] * len(tokens),
            out_specs=[IN_VMEM] * 2 + [block] * 2 + [IN_VMEM, whole((8, 128))],
            scratch_shapes=[pltpu.VMEM((tile, width), BF16)] * 2 + [pltpu.VMEM((positions, tile), BF16)] * 2,
        ),
        out_shape=[pltpu.VMEM((positions, width), F32)] * 2
        + [make((2, width, tile // 2), BF16) for make in (pltpu.HBM, jax.ShapeDtypeStruct)]
        + [pltpu.VMEM((8, tile), F32), TOKEN],
        input_output_aliases=aliases,
        name="other_hidden",
        **hidden_call(positions, width, tile),
    )(near, *operands, *tokens)


def pack_kernel(at, up, down, bias, token, out):
    size = up.shape[1] // 2
    width = down.shape[1]
    start = pl.multiple_of(at[2] * size, size)
    out[:size, :] = jnp.where(at[2] == 0, up[:, :size].T, up[:, size:].T)
    out[size : 2 * size, :] = down[pl.ds(start, size), :]
    both = jnp.concatenate([bias[:, :width], bias[:, width:], jnp.zeros((14, width), F32)], 0)
    out[2 * size :, :] = both.astype(BF16)


def pack(which, at, up, down, bias, token):
    width, hidden = up.shape
    part = hidden // 4
    return pl.pallas_call(
        pack_kernel,
        grid_spec=pltpu.PrefetchScalarGridSpec(
            num_scalar_prefetch=1,
            grid=(1,),
            in_specs=[
                pl.BlockSpec((width, part), lambda i, at: (0, at[which])),
                pl.BlockSpec((part, width), lambda i, at: (at[which], 0)),
                whole(bias.shape),
                ANYWHERE,
            ],
            out_specs=whole((part + 16, width)),
        ),
        out_shape=jax.ShapeDtypeStruct((part + 16, width), BF16),
        compiler_params=pltpu.CompilerParams(vmem_limit_bytes=16 * MIB),
        cost_estimate=long_cost(0.5),
        name="pack",
    )(at, *in_hbm([up, down, bias, token]))


def resid_kernel(out_acc, dh, resid, g, recip, wo, small, *rest):
    layer_out, grad_resid, grad_out, gm, vec = rest[-5:]
    g2, bd = small[2:3, :], small[6:7, :]
    r = resid[0]
    at = pl.program_id(0)
    layer_out[0] = (r + out_acc[at] + bd).astype(BF16)
    unit, scale = unit_rows(r)
    grad = dh[at]
    cot = g[0].astype(F32)
    total = cot + norm_back(grad, unit, scale, g2)
    grad_resid[0] = total
    grad_o = total.astype(BF16)
    grad_out[0] = grad_o
    vec[0, 0:1, :] = jnp.sum(grad_o.astype(F32), 0, keepdims=True)
    vec[0, 1:2, :] = jnp.sum(grad * unit, 0, keepdims=True)
    vec[0, 2:3, :] = jnp.sum(grad, 0, keepdims=True)
    vec[0, 3:4, :] = jnp.sum(cot, 0, keepdims=True)
    gm[0] = (mm(grad_o, wo[...], 1, 1).astype(BF16).astype(F32) * recip[0].astype(F32)).astype(BF16)


def resid_rows(row_arrays, weights, *tokens):
    rows, length, width = row_arrays[0].shape
    low = ((length, width), BF16)
    shapes = [low, ((length, width), F32), low, low, ((4, width), F32)]
    return pl.pallas_call(
        resid_kernel,
        grid=(rows,),
        in_specs=[IN_VMEM] * 2
        + [by_row(0, (length, width)) for _ in row_arrays[2:]]
        + [whole(w.shape) for w in weights]
        + [ANYWHERE] * len(tokens),
        out_specs=[by_row(0, s) for s, _ in shapes],
        out_shape=[
            (pltpu.VMEM if i in (2, 3) else pltpu.HBM)((rows,) + s, t) for i, (s, t) in enumerate(shapes)
        ],
        compiler_params=pltpu.CompilerParams(vmem_limit_bytes=24 * MIB),
        cost_estimate=long_cost(3),
        name="resid_rows",
    )(*in_vmem(row_arrays[:3]), *in_hbm([*row_arrays[3:], *weights]), *tokens)


def back_kernel(count, offs, gm, x_own, seg_row, expo, wv, *rest):
    gv, gh_own, gh_send, vec_one, gmt, gvt, gh = rest[-7:]
    x_others = rest[:count]
    length = x_own.shape[1]
    heads = expo.shape[0]
    gmt[...] = gm[0].T
    mask = same_document(offs[0], seg_row, 0, length).astype(BF16)
    for head in range(heads):
        at = slice(64 * head, 64 * head + 64)
        gvt[at, :] = mm(gmt[at, :], expo[head] * mask, 1, 0).astype(BF16)
    values_grad = gvt[...].T
    gv[0] = values_grad
    gh[...] = mm(values_grad, wv[...], 1, 1)
    gain = jnp.zeros((1, gh.shape[1]), F32)
    x_other = x_others[0][0]
    for i, x in enumerate(x_others[1:]):
        x_other = jnp.where(pl.program_id(0) > i, x[0], x_other)
    for block, off in ((x_own[0], offs[0]), (x_other, offs[1])):
        unit, _ = unit_rows(block.astype(F32))
        gain += jnp.sum(gh[pl.ds(pl.multiple_of(off, length), length), :] * unit, 0, keepdims=True)
    vec_one[0, 0:1, :] = gain
    vec_one[0, 1:2, :] = jnp.sum(gh[...], 0, keepdims=True)
    vec_one[0, 2:3, :] = jnp.sum(values_grad.astype(F32), 0, keepdims=True)
    gh_own[0] = gh[pl.ds(pl.multiple_of(offs[0], length), length), :]
    gh_send[0] = gh[pl.ds(pl.multiple_of(offs[1], length), length), :].astype(BF16)


def back_rows(offs, gm, inputs, received, seg_row, expo, wv, *tokens):
    rows, length, width = inputs.shape
    full = seg_row.shape[2]
    shapes = [((full, width), BF16), ((length, width), F32), ((length, width), BF16), ((3, width), F32)]
    operands = [*in_vmem([gm]), *in_hbm([inputs, seg_row]), *in_vmem([expo, wv]), *received, *tokens]
    return pl.pallas_call(
        functools.partial(back_kernel, rows),
        grid_spec=pltpu.PrefetchScalarGridSpec(
            num_scalar_prefetch=1,
            grid=(rows,),
            in_specs=[by_row(0, (length, width))] * 2
            + [by_row(0, (1, full)), IN_VMEM, IN_VMEM]
            + [whole((1, length, width))] * rows
            + [ANYWHERE] * len(tokens),
            out_specs=[by_row(0, s) for s, _ in shapes],
            scratch_shapes=[
                pltpu.VMEM((width, length), BF16),
                pltpu.VMEM((width, full), BF16),
                pltpu.VMEM((full, width), F32),
            ],
        ),
        out_shape=[
            make((rows,) + s, t)
            for make, (s, t) in zip((pltpu.VMEM, pltpu.HBM, jax.ShapeDtypeStruct, pltpu.HBM), shapes)
        ],
        compiler_params=pltpu.CompilerParams(vmem_limit_bytes=32 * MIB),
        cost_estimate=long_cost(6),
        name="back_rows",
    )(offs, *operands)


def send_kernel(counts, *refs):
    out = refs[-1]
    start = 0
    for i, count in enumerate(counts):
        sum_of = refs[start][...].astype(F32)
        for part in refs[start + 1 : start + count]:
            sum_of = sum_of + part[...].astype(F32)
        start += count
        if len(counts) == 1:
            out[...] = sum_of.astype(BF16)
        else:
            out[i] = sum_of.astype(BF16)


def part_spec(part, dim, size, index):
    array, lead = part
    shape = array.shape if lead is None else array.shape[1:]
    shape = shape[:dim] + (size,) + shape[dim + 1 :]
    place = tuple(index if d == dim else 0 for d in range(len(shape)))
    if lead is None:
        return pl.BlockSpec(shape, lambda i, *_: place), shape
    return pl.BlockSpec((None,) + shape, lambda i, *_: (lead,) + place), shape


def send_sum(groups, dim, size, index, *tokens):
    parts = [p for group in groups for p in group]
    specs = [part_spec(p, dim, size, index) for p in parts]
    shape = specs[0][1]
    if len(groups) > 1:
        shape = (len(groups),) + shape
    return pl.pallas_call(
        functools.partial(send_kernel, [len(group) for group in groups]),
        grid=(1,),
        in_specs=[spec for spec, _ in specs] + [ANYWHERE] * len(tokens),
        out_specs=whole(shape),
        out_shape=jax.ShapeDtypeStruct(shape, BF16),
        compiler_params=pltpu.CompilerParams(vmem_limit_bytes=16 * MIB),
        cost_estimate=long_cost(0.2),
        name="send_sum",
    )(*[p for p, _ in parts], *tokens)


def logits_kernel(offs, gm, mixed, values, seg_row, expo, *rest):
    out, ones, masks = rest[-3:]
    step = pl.program_id(0)
    rows, length = gm.shape[:2]

    @pl.when(step == 0)
    def _():
        ones[:, 128:] = jnp.ones_like(ones[:, 128:])
        for row in range(rows):
            masks[row] = same_document(offs[0], seg_row, row, length)

    low_lane = lax.broadcasted_iota(jnp.int32, (length, 128), 1) < 64
    zero = jnp.zeros((length, 128), F32)
    sums = [None, None]
    for row in range(rows):
        ones[:, :128] = values[row]
        scaled = gm[row].astype(F32)
        product = scaled * mixed[row].astype(F32)
        high = product.astype(BF16).astype(F32)
        rest = product - high
        turned_rest = pltpu.roll(rest, 64, 1)
        left = []
        for head in range(2):
            keep = low_lane if head == 0 else jnp.logical_not(low_lane)
            left.append(
                jnp.concatenate(
                    [
                        jnp.where(keep, scaled, zero).astype(BF16),
                        (-jnp.where(keep, high, turned_rest)).astype(BF16),
                    ],
                    axis=1,
                )
            )
        both = mm(jnp.concatenate(left, 0), ones[...], 1, 1)
        for head in range(2):
            part = both[head * length : (head + 1) * length] * masks[row]
            sums[head] = part if sums[head] is None else sums[head] + part
    for head in range(2):
        grad = (expo[head].astype(F32) * sums[head]).astype(BF16).T
        blocks, _, size, _ = out.shape
        for j in range(blocks):
            out[turned(j, offs[3], blocks), head] = grad[j * size : (j + 1) * size, :]


def logits_grad(mine, offs, blocks, gm, mixed, values, seg_row, expo, *tokens):
    rows, length, width = gm.shape
    heads, _, full = expo.shape
    half = heads // 4
    pick = lambda i, offs: i + half * (offs[2] if mine else 1 - offs[2])
    shape = (blocks, heads // 2, full // blocks, length)
    return pl.pallas_call(
        logits_kernel,
        grid_spec=pltpu.PrefetchScalarGridSpec(
            num_scalar_prefetch=1,
            grid=(half,),
            in_specs=[
                pl.BlockSpec((rows, length, 128), lambda i, offs: (0, 0, pick(i, offs))),
                pl.BlockSpec((rows, length, 128), lambda i, offs: (0, 0, pick(i, offs))),
                pl.BlockSpec((rows, full, 128), lambda i, offs: (0, 0, pick(i, offs))),
                whole(seg_row.shape),
                pl.BlockSpec((2, length, full), lambda i, offs: (pick(i, offs), 0, 0)),
            ]
            + [ANYWHERE] * len(tokens),
            out_specs=pl.BlockSpec((blocks, 2, full // blocks, length), lambda i, offs: (0, i, 0, 0)),
            scratch_shapes=[pltpu.VMEM((full, 256), BF16), pltpu.VMEM((rows, length, full), F32)],
        ),
        out_shape=pltpu.HBM(shape, BF16) if mine else jax.ShapeDtypeStruct(shape, BF16),
        compiler_params=pltpu.CompilerParams(vmem_limit_bytes=32 * MIB),
        cost_estimate=long_cost(3),
        name="logits_grad",
    )(offs, *in_vmem([gm]), *in_hbm([mixed, values, seg_row]), *in_vmem([expo]), *tokens)


def square_kernel(at_ref, mixed, grad_o, h1, gv, bias, vec_two, vec_one, *rest):
    theirs, mine, out_sum, value_sum = rest[-4:]
    step = pl.program_id(0)
    out_part = mm(mixed[0], grad_o[0], 0, 0)
    value_part = mm(h1[0], gv[0], 0, 0)

    @pl.when(step == 0)
    def _():
        out_sum[...] = out_part
        value_sum[...] = value_part

    @pl.when(step > 0)
    def _():
        out_sum[...] += out_part
        value_sum[...] += value_part

    @pl.when(step == pl.num_programs(0) - 1)
    def _():
        square_store(at_ref, out_sum, value_sum, bias, vec_two, vec_one, theirs, mine)


def square_store(at_ref, out_w, value_w, bias, vec_two, vec_one, theirs, mine):
    width = out_w.shape[1]
    rows = vec_two.shape[0]
    core, near, me = at_ref[0], at_ref[1], at_ref[2]
    blocks, chunks, size, _ = mine.shape
    size -= 8
    vectors = [sum(ref[r, i : i + 1, :] for r in range(rows)) for ref, n in ((vec_two, 4), (vec_one, 3)) for i in range(n)]
    share = 2 * width // (2 * blocks)
    part = width // 4
    own_rows = [jnp.where(core == a, bias[1:2, :], bias[0:1, :]) for a in range(2)]
    pad = lambda v: jnp.concatenate([v, jnp.zeros((1, width - v.shape[1]), F32)], 1)
    none = jnp.zeros((8, width), F32)
    for j in range(blocks):
        to = turned(j, near, blocks)
        for chunk in range(chunks):
            index = 2 * j + chunk // 2
            a, start = divmod(index * share, width)
            p, at = divmod(start, 2 * part)
            own = own_rows[a][:, start : start + share]
            row = bias[2 + p : 3 + p, :]
            first, second = row[:, at : at + share], row[:, width // 2 + at : width // 2 + at + share]
            other = jnp.where(core == a, first, second)
            hidden = jnp.where(me == chunk % 2, own, other)
            begin = (j * chunks + chunk) * size
            tail = [pad(v[:, begin : begin + size]) for v in vectors] + [pad(hidden)]
            here = slice(begin, begin + size)
            with_vectors = jnp.concatenate([out_w[here, :], *tail], 0).astype(BF16)
            without = jnp.concatenate([value_w[here, :], none], 0).astype(BF16)
            mine[to, chunk] = jnp.where(core == 0, with_vectors, without)
            theirs[to, chunk] = jnp.where(core == 0, without, with_vectors)


def square_grads(at, blocks, mixed, grad_o, h1, gv, *rest):
    rows, _, width = mixed.shape
    operands = (mixed, grad_o, h1, gv, *rest[:3])
    shape = (blocks, 4, width // (4 * blocks) + 8, width)
    return pl.pallas_call(
        square_kernel,
        grid_spec=pltpu.PrefetchScalarGridSpec(
            num_scalar_prefetch=1,
            grid=(rows,),
            in_specs=[by_row(0, a.shape[1:]) for a in operands[:4]]
            + [whole(a.shape) for a in operands[4:]]
            + [ANYWHERE] * len(rest[3:]),
            out_specs=[whole(shape)] * 2,
            scratch_shapes=[pltpu.VMEM((width, width), F32)] * 2,
        ),
        out_shape=[jax.ShapeDtypeStruct(shape, BF16), pltpu.HBM(shape, BF16)],
        compiler_params=pltpu.CompilerParams(vmem_limit_bytes=40 * MIB),
        cost_estimate=long_cost(4),
        name="square_grads",
    )(at, *in_hbm(operands[:1]), *in_vmem(operands[1:2]), *in_hbm(operands[2:3]), *in_vmem(operands[3:4]), *in_hbm(operands[4:]), *rest[3:])


def partner_kernel(count, at_ref, *refs):
    keep, send = refs[-2:]
    me = at_ref[2]
    for core in range(2):
        for out, chunk in ((keep, 2 * core + me), (send, 2 * core + 1 - me)):
            sum_of = refs[0][0, chunk].astype(F32)
            for part in refs[1:count]:
                sum_of = sum_of + part[0, chunk].astype(F32)
            out[core] = sum_of.astype(out.dtype)


def partner_split(at, parts, *tokens):
    shape = (2,) + parts[0].shape[2:]
    block = (1,) + parts[0].shape[1:]
    return pl.pallas_call(
        functools.partial(partner_kernel, len(parts)),
        grid_spec=pltpu.PrefetchScalarGridSpec(
            num_scalar_prefetch=1,
            grid=(1,),
            in_specs=[whole(block)] * len(parts) + [ANYWHERE] * len(tokens),
            out_specs=[whole(shape)] * 2,
        ),
        out_shape=[jax.ShapeDtypeStruct(shape, F32), jax.ShapeDtypeStruct(shape, BF16)],
        compiler_params=pltpu.CompilerParams(vmem_limit_bytes=16 * MIB),
        cost_estimate=long_cost(0.01),
        name="partner_split",
    )(at, *in_hbm(parts[:1]), *parts[1:], *tokens)


def cover(*tokens):
    def kernel(*refs):
        refs[-1][...] = jnp.zeros_like(refs[-1])

    return pl.pallas_call(
        kernel,
        in_specs=[ANYWHERE] * len(tokens),
        out_specs=pl.BlockSpec((8, 128), lambda: (0, 0)),
        out_shape=TOKEN,
        compiler_params=pltpu.CompilerParams(vmem_limit_bytes=MIB),
        cost_estimate=long_cost(100),
        name="cover",
    )(*tokens)


def hold(a, *tokens):
    return pl.pallas_call(
        lambda *refs: None,
        in_specs=[ANYWHERE] * (1 + len(tokens)),
        out_specs=ANYWHERE,
        out_shape=pltpu.VMEM(a.shape, a.dtype),
        input_output_aliases={0: 0},
        compiler_params=pltpu.CompilerParams(vmem_limit_bytes=MIB),
        cost_estimate=long_cost(0.01),
        name="hold",
    )(*in_vmem([a]), *tokens)


def last_kernel(count, rows_first, at_ref, *refs):
    keep, send = refs[-2:]
    core = at_ref[0]
    sum_of = refs[0][...].astype(F32)
    for part in refs[1:count]:
        sum_of = sum_of + part[...].astype(F32)
    half = keep.shape[-2]
    shape = keep.shape
    low = sum_of[..., :half, :].reshape(shape)
    high = sum_of[..., half:, :].reshape(shape)
    keep[...] = jnp.where(core == 0, low, high)
    send[...] = jnp.where(core == 0, high, low).astype(BF16)


def last_split(at, parts, dim, rows, shape, *tokens):
    block = parts[0].shape[:dim] + (rows,) + parts[0].shape[dim + 1 :]
    return pl.pallas_call(
        functools.partial(last_kernel, len(parts), dim),
        grid_spec=pltpu.PrefetchScalarGridSpec(
            num_scalar_prefetch=1,
            grid=(1,),
            in_specs=[whole(block)] * len(parts) + [ANYWHERE] * len(tokens),
            out_specs=[whole(shape)] * 2,
        ),
        out_shape=[jax.ShapeDtypeStruct(shape, F32), jax.ShapeDtypeStruct(shape, BF16)],
        compiler_params=pltpu.CompilerParams(vmem_limit_bytes=16 * MIB),
        cost_estimate=long_cost(0.2),
        name="last_split",
    )(at, *in_hbm(parts[:1]), *parts[1:], *tokens)


def hidden_last_kernel(count, at_ref, *refs):
    keep, send = refs[-2:]
    core = at_ref[0]
    half = keep.shape[1]
    for which in range(2):
        sums = []
        for refs_of in (refs[:count], refs[count : 2 * count]):
            sum_of = refs_of[0][which].astype(F32)
            for p in refs_of[1:]:
                sum_of = sum_of + p[which].astype(F32)
            sums.append(sum_of)
        sum_of = jnp.concatenate(sums, 1)
        low, high = sum_of[:half], sum_of[half:]
        keep[which] = jnp.where(core == 0, low, high)
        send[which] = jnp.where(core == 0, high, low).astype(BF16)


def hidden_last(at, first, second, rows, width, *tokens):
    shape = (2, rows // 2, width)
    parts = [*first, *second]
    return pl.pallas_call(
        functools.partial(hidden_last_kernel, len(first)),
        grid_spec=pltpu.PrefetchScalarGridSpec(
            num_scalar_prefetch=1,
            grid=(1,),
            in_specs=[part_spec(p, 1, rows, 0)[0] for p in parts] + [ANYWHERE] * len(tokens),
            out_specs=[whole(shape)] * 2,
        ),
        out_shape=[jax.ShapeDtypeStruct(shape, F32), jax.ShapeDtypeStruct(shape, BF16)],
        compiler_params=pltpu.CompilerParams(vmem_limit_bytes=16 * MIB),
        cost_estimate=long_cost(0.2),
        name="hidden_last",
    )(at, *[p for p, _ in parts], *tokens)


def hidden_out_kernel(at_ref, kept, got, *rest):
    up, down = rest[-2:]
    core = at_ref[0]
    for which, out in ((0, up), (1, down)):
        mine, theirs = kept[which], got[which].astype(F32)
        out[...] = jnp.concatenate([jnp.where(core == 0, mine, theirs), jnp.where(core == 0, theirs, mine)], 1)


def logit_out_kernel(at_ref, kept, got, *rest):
    out = rest[-1]
    core = at_ref[0]
    half = kept.shape[0]
    mine, theirs = kept[...], got[...].astype(F32)
    out[:half] = jnp.where(core == 0, mine, theirs)
    out[half:] = jnp.where(core == 0, theirs, mine)


def square_out_kernel(at_ref, kept, got, *rest):
    out_w, value_w, up_bias, *vectors = rest[-10:]
    core = at_ref[0]
    size = out_w.shape[0]
    mine, theirs = kept[...], got[...].astype(F32)
    first = jnp.where(core == 0, mine, theirs)
    second = jnp.where(core == 0, theirs, mine)
    out_w[...] = first[:size]
    value_w[...] = second[:size]
    for i, v in enumerate(vectors):
        v[...] = first[size + i : size + i + 1, :size]
    up_bias[...] = first[size + 7 : size + 8, : up_bias.shape[1]]


def finish(kernel, at, kept, got, shapes, *tokens):
    return pl.pallas_call(
        kernel,
        grid_spec=pltpu.PrefetchScalarGridSpec(
            num_scalar_prefetch=1,
            grid=(1,),
            in_specs=[whole(kept.shape), whole(got.shape)] + [ANYWHERE] * len(tokens),
            out_specs=[whole(s) for s in shapes],
        ),
        out_shape=[pltpu.HBM(s, F32) for s in shapes],
        compiler_params=pltpu.CompilerParams(vmem_limit_bytes=16 * MIB),
        cost_estimate=long_cost(0.2),
        name="finish",
    )(at, kept, got, *tokens)


def input_kernel(x, grad_resid, gh_own, gh_received, small, *rest):
    grad, token = rest[-2:]
    token[...] = jnp.zeros_like(token)
    unit, scale = unit_rows(x[0].astype(F32))
    total = gh_own[0] + gh_received[0].astype(F32)
    grad[0] = grad_resid[0] + norm_back(total, unit, scale, small[0:1, :])


def input_rows(inputs, grad_resid, gh_own, gh_received, small, *tokens):
    rows, length, width = inputs.shape
    return pl.pallas_call(
        input_kernel,
        grid=(rows,),
        in_specs=[by_row(0, (length, width))] * 4 + [whole(small.shape)] + [ANYWHERE] * len(tokens),
        out_specs=[by_row(0, (length, width)), whole((8, 128))],
        out_shape=[pltpu.HBM((rows, length, width), F32), TOKEN],
        compiler_params=pltpu.CompilerParams(vmem_limit_bytes=24 * MIB),
        cost_estimate=long_cost(0.5),
        name="input_rows",
    )(*in_hbm([inputs, grad_resid, gh_own]), gh_received, *in_hbm([small]), *tokens)


def swap(a, axis, size, bit):
    return lax.ppermute(a, axis, [(i, i ^ bit) for i in range(size)])


class Scatter:
    def __init__(self, groups, dim, size):
        self.groups = [[p if isinstance(p, tuple) else (p, None) for p in parts] for parts in groups]
        array, lead = self.groups[0][0]
        self.dim, self.size, self.step = dim, size, 1
        self.rows = array.shape[dim + (lead is not None)]

    def send(self, *tokens):
        self.rows //= 2
        out = send_sum(self.groups, self.dim, self.rows, 1, *tokens)
        self.add(swap(out, "dp", self.size, 1 << self.step))
        self.step += 1
        return out

    def add(self, received):
        self.latest = received
        for i, parts in enumerate(self.groups):
            parts.append((received, i if len(self.groups) > 1 else None))

    def split(self):
        return [Part([parts], self) for parts in self.groups]

    def arrays(self):
        return [p for p, _ in self.groups[0]]


class Part(Scatter):
    def __init__(self, groups, whole):
        self.groups = groups
        self.dim, self.size, self.step, self.rows = whole.dim, whole.size, whole.step, whole.rows


def paired_shards(
    dp,
    mp,
    inputs,
    segment_ids,
    ln1_gain,
    ln1_bias,
    value_weight,
    value_bias,
    random_logits,
    out_weight,
    out_bias,
    ln2_gain,
    ln2_bias,
    up_weight,
    up_bias,
    down_weight,
    down_bias,
    out_cotangent,
):
    rows, length, width = inputs.shape
    heads = random_logits.shape[0]
    full = segment_ids.shape[1]
    positions = rows * length
    hidden = up_weight.shape[1]
    tile = hidden // 2
    me = lax.axis_index("mp")
    place = lax.axis_index("dp")
    bits = dp.bit_length() - 1
    bit = [lax.rem(lax.div(place, 1 << b), 2) for b in range(bits)]
    core = bit[0]
    near = lax.shift_right_logical(place, 1)
    blocks = dp // 2
    at = jnp.stack([core, near, me]).astype(jnp.int32)
    offs = jnp.stack([me * length, (1 - me) * length, core, near]).astype(jnp.int32)
    quarter = jnp.stack([2 * core, 2 * core + 1, bit[1]]).astype(jnp.int32)
    by_core = lambda first, second: jnp.where(core == 0, first, second)
    small, up_row = prep(
        [ln1_gain, ln1_bias, ln2_gain, ln2_bias, value_bias, out_bias, down_bias], up_bias
    )

    received = [swap(inputs[r : r + 1], "mp", mp, 1) for r in range(rows)]
    expo = jnp.exp(random_logits.astype(F32)).astype(BF16)
    seg_row = segment_ids[:, None, :]
    g = out_cotangent.reshape(positions, width)

    chain = None
    packed = []
    for r in range(rows):
        chain = mix_rows(
            r,
            1,
            offs,
            blocks,
            inputs,
            received[r],
            out_cotangent,
            seg_row,
            expo,
            (value_weight, out_weight, small),
            chain,
            *packed[-1:],
        )
        if 1 <= r <= 2:
            packed.append(pack(r - 1, quarter, up_weight, down_weight, up_row, chain[-1]))
    h1, values, recip, mixed, resid, h2, h2t, gt, _ = chain
    h2 = h2.reshape(positions, width)
    h2t = h2t.reshape(width, positions)
    gt = gt.reshape(width, positions)

    def fetch(by_x):
        by_y = swap(by_x, "dp", dp, 2)
        return by_x, by_y

    def share(by_x, by_y):
        return by_x, by_y, swap(by_x, "dp", dp, 1), swap(by_y, "dp", dp, 1)

    by_x = [swap(message, "mp", mp, 1) for message in packed]
    fixed = (h2, g, h2t, gt)
    tiles = [(1 - core).reshape(1).astype(jnp.int32), core.reshape(1).astype(jnp.int32)]
    *sums, own_theirs, bias, token = own_hidden(tiles[0], fixed, up_weight, up_row, down_weight, None)
    fetched = [fetch(hold(by_x[0], token))]
    *sums, own_mine, bias, token = own_hidden(
        tiles[1], fixed, up_weight, up_row, down_weight, (*sums, bias), fetched[0][0]
    )
    fetched.append(fetch(hold(by_x[1], token)))
    own_received = swap(own_theirs, "dp", dp, 1)
    own = Scatter([[(own_mine, i), (own_received, i)] for i in range(2)], 1, dp)
    near_y = jnp.stack([bit[1], core]).astype(jnp.int32)
    *sums, mine, theirs, bias, token = other_hidden(
        0, near_y, fixed, share(fetched[0][0], hold(fetched[0][1], token)), (*sums, bias)
    )
    others = [Scatter([[mine, swap(theirs, "dp", dp, 1)]], 1, dp)]
    sent = own.send(token)
    out, dh, mine, theirs, bias, token = other_hidden(
        1, near_y, fixed, share(fetched[1][0], hold(fetched[1][1], sent)), (*sums, bias), sent
    )
    others.append(Scatter([[mine, swap(theirs, "dp", dp, 1)]], 1, dp))
    token = others[0].send(token)

    shape = (rows, length, width)
    layer_out, grad_resid, grad_o, gm, vec_two = resid_rows(
        [out.reshape(shape), dh.reshape(shape), resid, out_cotangent, recip], (out_weight, small), token
    )
    token = others[1].send(vec_two)
    def to_partner(other, token):
        sent = send_sum(other.groups, 1, other.rows, 0, token)
        return sent, swap(sent, "mp", mp, 1)

    gv, gh_own, gh_sent, vec_one = back_rows(offs, gm, inputs, received, seg_row, expo, value_weight, token)
    token, arrived = to_partner(others[0], gh_sent)
    own = own.split()
    own[0].add(arrived)
    square_theirs, square_mine = square_grads(
        at,
        blocks,
        mixed,
        grad_o,
        h1,
        gv,
        bias,
        vec_two,
        vec_one,
        token,
    )

    square = Scatter([[square_mine, swap(square_theirs, "dp", dp, 1)]], 0, dp)
    token = cover(square_mine, others[1].latest)
    token, arrived = to_partner(others[1], token)
    own[1].add(arrived)
    token = own[0].send(token)
    token = square.send(token)
    gh_sent = hold(gh_sent, token)
    gh_received = swap(gh_sent, "mp", mp, 1)
    grads = (offs, blocks, gm, mixed, values, seg_row, expo)
    logits_theirs = logits_grad(False, *grads, gh_sent)
    token = own[0].send(logits_theirs)
    logits_mine = logits_grad(True, *grads, token)
    logit = Scatter([[logits_mine, swap(logits_theirs, "dp", dp, 1)]], 0, dp)
    token = logit.send(logits_mine, own[0].latest)
    token = square.send(token)
    token = own[1].send(token)
    token = square.send(token)
    token = logit.send(token)
    token = own[1].send(token)
    grad_inputs, token = input_rows(inputs, grad_resid, gh_own, gh_received, small, token)
    square_kept, token = partner_split(at, square.arrays(), token)
    square_received = swap(token, "mp", mp, 1)
    token = logit.send(token)
    kept, token = hidden_last(at, own[0].groups[0], own[1].groups[0], own[0].rows, tile, token)
    hidden_received = swap(token, "dp", dp, 1)
    chunk = square_mine.shape[2]
    square_parts = [p.reshape(2 * chunk, width) for p in (square_kept, square_received)]
    square_kept, token = last_split(at, square_parts, 0, 2 * chunk, (chunk, width), token)
    square_received = swap(token, "dp", dp, 1)
    up_part, down_part = finish(
        hidden_out_kernel, at, kept, hidden_received, [(width // dp, hidden)] * 2, token
    )
    part_size = width // (dp * mp)
    out_part, value_part, up_bias_part, *vector = finish(
        square_out_kernel,
        at,
        square_kept,
        square_received,
        [(part_size, width), (part_size, width), (1, hidden // dp)] + [(1, part_size)] * 7,
        up_part,
    )
    logit_kept, token = last_split(at, logit.arrays(), 0, 1, (heads // 2, full // dp, length), out_part)
    logit_received = swap(token, "dp", dp, 1)
    (logit_part,) = finish(
        logit_out_kernel, at, logit_kept, logit_received, [(heads, full // dp, length)]
    )
    bo_part, g2_part, b2_part, bd_part, g1_part, b1_part, bv_part = (v.reshape(-1) for v in vector)
    return (
        layer_out,
        grad_inputs,
        g1_part,
        b1_part,
        value_part,
        bv_part,
        logit_part.transpose(0, 2, 1),
        out_part,
        bo_part,
        g2_part,
        b2_part,
        up_part,
        up_bias_part,
        down_part.T,
        bd_part,
    )


def smooth(t):
    return jax.nn.gelu(t, approximate=True)


def contract_rows(left, right):
    return lax.dot_general(
        left, right, (((0,), (0,)), ((), ())), preferred_element_type=jnp.float32
    )


def contract_cols(left, right):
    return lax.dot_general(
        left, right, (((1,), (1,)), ((), ())), preferred_element_type=jnp.float32
    )


def normalize(x, gain, shift):
    centred = x - jnp.mean(x, -1, keepdims=True)
    scale = lax.rsqrt(jnp.mean(centred * centred, -1, keepdims=True) + 1e-05)
    unit = centred * scale
    return (unit * gain + shift, unit, scale)


def normalize_back(grad, unit, scale, gain):
    scaled = grad * gain
    inner = scale * (
        scaled
        - jnp.mean(scaled, -1, keepdims=True)
        - unit * jnp.mean(scaled * unit, -1, keepdims=True)
    )
    return (inner, jnp.sum(grad * unit, 0), jnp.sum(grad, 0))


def shards(
    inputs,
    segment_ids,
    ln1_gain,
    ln1_bias,
    value_weight,
    value_bias,
    random_logits,
    out_weight,
    out_bias,
    ln2_gain,
    ln2_bias,
    up_weight,
    up_bias,
    down_weight,
    down_bias,
    out_cotangent,
):
    seqs, local_len, width = inputs.shape
    heads = random_logits.shape[0]
    full_len = segment_ids.shape[1]
    head_dim = width // heads
    rows = seqs * local_len
    gain_one = ln1_gain.astype(jnp.float32)
    gain_two = ln2_gain.astype(jnp.float32)
    start_x = inputs.astype(jnp.float32).reshape(rows, width)
    normed_one, unit_one, scale_one = normalize(start_x, gain_one, ln1_bias.astype(jnp.float32))
    h1_low = normed_one.astype(jnp.bfloat16)
    values = (
        jnp.dot(h1_low, value_weight, preferred_element_type=jnp.float32)
        + value_bias.astype(jnp.float32)
    ).astype(jnp.bfloat16)
    gathered = lax.all_gather(values.reshape(seqs, local_len, width), "mp", axis=1, tiled=True)
    every_head = gathered.reshape(seqs, full_len, heads, head_dim)
    offset = lax.axis_index("mp") * local_len
    own_segs = lax.dynamic_slice_in_dim(segment_ids, offset, local_len, 1)
    same = own_segs[:, :, None] == segment_ids[:, None, :]
    scores = jnp.where(same[:, None], random_logits.astype(jnp.float32)[None], -1e30)
    peak = jnp.max(scores, -1, keepdims=True)
    expo = jnp.exp(scores - peak)
    total = jnp.sum(expo, -1, keepdims=True)
    probs = expo / total
    probs_low = probs.astype(jnp.bfloat16)
    mixed = jnp.einsum("shqk,skhd->sqhd", probs_low, every_head, preferred_element_type=jnp.float32)
    mixed_low = mixed.reshape(rows, width).astype(jnp.bfloat16)
    resid = (
        start_x
        + jnp.dot(mixed_low, out_weight, preferred_element_type=jnp.float32)
        + out_bias.astype(jnp.float32)
    )
    normed_two, unit_two, scale_two = normalize(resid, gain_two, ln2_bias.astype(jnp.float32))
    h2_low = normed_two.astype(jnp.bfloat16)
    grad_low = out_cotangent.reshape(rows, width)
    h2_full = lax.all_gather(
        h2_low.reshape(seqs, local_len, width), "mp", axis=1, tiled=True
    ).reshape(seqs * full_len, width)
    pre = jnp.dot(h2_full, up_weight, preferred_element_type=jnp.float32) + up_bias.astype(
        jnp.float32
    )
    act, gelu_pull = jax.vjp(smooth, pre)
    act_low = act.astype(jnp.bfloat16)
    partial_out = jnp.dot(act_low, down_weight, preferred_element_type=jnp.float32).reshape(
        seqs, full_len, width
    )
    ffn_out = lax.psum_scatter(
        partial_out.astype(jnp.bfloat16), "mp", scatter_dimension=1, tiled=True
    ).astype(jnp.float32).reshape(rows, width) + down_bias.astype(jnp.float32)
    final = resid + ffn_out
    grad_full = lax.all_gather(out_cotangent, "mp", axis=1, tiled=True).reshape(
        seqs * full_len, width
    )
    grad_down = contract_rows(act_low, grad_full)
    grad_act = contract_cols(grad_full, down_weight)
    grad_pre = gelu_pull(grad_act)[0].astype(jnp.bfloat16)
    grad_up_b = jnp.sum(grad_pre.astype(jnp.float32), 0)
    grad_up = contract_rows(h2_full, grad_pre)
    h2_terms = contract_cols(grad_pre, up_weight).reshape(seqs, full_len, width)
    grad_h2 = (
        lax.psum_scatter(h2_terms.astype(jnp.bfloat16), "mp", scatter_dimension=1, tiled=True)
        .astype(jnp.float32)
        .reshape(rows, width)
    )
    grad_final = grad_low.astype(jnp.float32)
    grad_down_b = jnp.sum(grad_final, 0)
    inner_two, gain_two_grad, shift_two_grad = normalize_back(
        grad_h2, unit_two, scale_two, gain_two
    )
    grad_resid = grad_final + inner_two
    grad_o_low = grad_resid.astype(jnp.bfloat16)
    grad_out_b = jnp.sum(grad_o_low.astype(jnp.float32), 0)
    grad_out_w = contract_rows(mixed_low, grad_o_low)
    grad_mixed = (
        contract_cols(grad_o_low, out_weight)
        .astype(jnp.bfloat16)
        .reshape(seqs, local_len, heads, head_dim)
    )
    grad_probs = jnp.einsum(
        "sqhd,skhd->shqk", grad_mixed, every_head, preferred_element_type=jnp.float32
    )
    grad_scores = probs * (grad_probs - jnp.sum(probs * grad_probs, -1, keepdims=True))
    grad_logits = jnp.sum(grad_scores, 0)
    value_terms = jnp.einsum(
        "shqk,sqhd->skhd", probs_low, grad_mixed, preferred_element_type=jnp.float32
    ).reshape(seqs, full_len, width)
    grad_values = (
        lax.psum_scatter(value_terms.astype(jnp.bfloat16), "mp", scatter_dimension=1, tiled=True)
        .astype(jnp.float32)
        .reshape(rows, width)
        .astype(jnp.bfloat16)
    )
    grad_value_b = jnp.sum(grad_values.astype(jnp.float32), 0)
    grad_value_w = contract_rows(h1_low, grad_values)
    inner_one, gain_one_grad, shift_one_grad = normalize_back(
        contract_cols(grad_values, value_weight), unit_one, scale_one, gain_one
    )
    grad_x = (grad_resid + inner_one).reshape(seqs, local_len, width)
    vectors = jnp.stack(
        [
            gain_one_grad,
            shift_one_grad,
            grad_value_b,
            grad_out_b,
            gain_two_grad,
            shift_two_grad,
            grad_down_b,
        ]
    )
    value_w_part, out_w_part, vector_part = (
        lax.psum_scatter(grad_value_w, ("dp", "mp"), scatter_dimension=0, tiled=True),
        lax.psum_scatter(grad_out_w, ("dp", "mp"), scatter_dimension=0, tiled=True),
        lax.psum_scatter(vectors, ("dp", "mp"), scatter_dimension=1, tiled=True),
    )
    up_part, up_b_part, down_part, logit_part = (
        lax.psum_scatter(
            grad_up.astype(jnp.bfloat16), "dp", scatter_dimension=0, tiled=True
        ).astype(jnp.float32),
        lax.psum_scatter(
            grad_up_b[None].astype(jnp.bfloat16), "dp", scatter_dimension=1, tiled=True
        ).astype(jnp.float32),
        lax.psum_scatter(
            grad_down.astype(jnp.bfloat16), "dp", scatter_dimension=1, tiled=True
        ).astype(jnp.float32),
        lax.psum_scatter(
            grad_logits.astype(jnp.bfloat16), "dp", scatter_dimension=2, tiled=True
        ).astype(jnp.float32),
    )
    return (
        final.astype(jnp.bfloat16).reshape(seqs, local_len, width),
        grad_x,
        vector_part[0],
        vector_part[1],
        value_w_part,
        vector_part[2],
        logit_part,
        out_w_part,
        vector_part[3],
        vector_part[4],
        vector_part[5],
        up_part,
        up_b_part,
        down_part,
        vector_part[6],
    )


def solution(mesh):
    in_specs = (
        P("dp", "mp", None),
        P("dp", None),
        P(),
        P(),
        P(),
        P(),
        P(None, "mp", None),
        P(),
        P(),
        P(),
        P(),
        P(None, "mp"),
        P("mp"),
        P("mp", None),
        P(),
        P("dp", "mp", None),
    )
    out_specs = (
        P("dp", "mp", None),
        P("dp", "mp", None),
        P(("dp", "mp")),
        P(("dp", "mp")),
        P(("dp", "mp"), None),
        P(("dp", "mp")),
        P(None, "mp", "dp"),
        P(("dp", "mp"), None),
        P(("dp", "mp")),
        P(("dp", "mp")),
        P(("dp", "mp")),
        P("dp", "mp"),
        P("mp", "dp"),
        P("mp", "dp"),
        P(("dp", "mp")),
    )
    dp, mp = mesh.shape["dp"], mesh.shape["mp"]
    body = functools.partial(paired_shards, dp, mp) if mp == 2 else shards
    return jax.shard_map(body, mesh=mesh, in_specs=in_specs, out_specs=out_specs, check_vma=False)
```
